32 devices in a mesh: gx: 16 (over z, y, core), gy: 2 (over x).
Axes of the slice: x: 2, y: 2, z: 4, core: 2. Of those that a mesh axis runs over, the one named last changes fastest.
Arguments:
- latents: int32 [768, 64, 32], P('gy', 'gx'), may hold values from 0 to 31
- actions: int32 [768, 64], P('gy', 'gx'), may hold values from 0 to 17
- segment_ids: int32 [768, 64], replicated, may hold values from 0 to 3, never falling along the last dimension, each value on 1 to 32 neighbouring positions
- cotangent: bfloat16 [768, 64, 512], P('gy', 'gx'), may hold values from -6 to 6
- stem_weight: bfloat16 [1024, 512], replicated, may hold values from -1 to 1
- action_table: bfloat16 [18, 512], replicated, may hold values from -1 to 1
- first_gain: float32 [512], replicated, may hold values from 0.5 to 1.5
- first_bias: float32 [512], replicated, may hold values from -1 to 1
- query_weight: bfloat16 [512, 512], P(None, 'gy'), may hold values from -0.25 to 0.25
- key_weight: bfloat16 [512, 512], P(None, 'gy'), may hold values from -0.25 to 0.25
- value_weight: bfloat16 [512, 512], P(None, 'gy'), may hold values from -0.25 to 0.25
- out_weight: bfloat16 [512, 512], P('gy'), may hold values from -1 to 1
- second_gain: float32 [512], replicated, may hold values from 0.5 to 1.5
- second_bias: float32 [512], replicated, may hold values from -1 to 1
- up_weight: bfloat16 [512, 2048], P(None, 'gy'), may hold values from -0.25 to 0.25
- up_bias: float32 [2048], P('gy'), may hold values from -1 to 1
- down_weight: bfloat16 [2048, 512], P('gy'), may hold values from -0.125 to 0.125
- down_bias: float32 [512], replicated, may hold values from -1 to 1
Outputs:
- output: bfloat16 [768, 64, 512], P('gy', 'gx')
- token_grad: bfloat16 [768, 64, 512], P('gy', 'gx')
- stem_grad: float32 [1024, 512], replicated
- action_grad: float32 [18, 512], replicated
- first_gain_grad: float32 [512], replicated
- first_bias_grad: float32 [512], replicated
- query_grad: float32 [512, 512], P(None, 'gy')
- key_grad: float32 [512, 512], P(None, 'gy')
- value_grad: float32 [512, 512], P(None, 'gy')
- out_grad: float32 [512, 512], P('gy')
- second_gain_grad: float32 [512], replicated
- second_bias_grad: float32 [512], replicated
- up_grad: float32 [512, 2048], P(None, 'gy')
- up_bias_grad: float32 [2048], P('gy')
- down_grad: float32 [2048, 512], P('gy')
- down_bias_grad: float32 [512], replicated
The draws below stay inside these ranges and needn't reach their ends.
Inputs may be any that keep to these rules, and one draw needn't show every extreme that they name: `segment_ids`: along each sequence of 64 frames the segment id never falls; each segment holds 1 to 32 frames.
All inputs are finite; a program needn't handle non-finite values.
Results may differ from the reference program's by a relative error of at most 0.012.
Values may be sent and summed in bfloat16 or wider, within the bound.
A program may use at most 192 MiB of HBM per device.

```python
import math
import jax
import jax.numpy as jnp
import numpy as np
from jax import lax

D = 512
HEADS = 8
HD = 64
FF = 2048
LEN = 64
GROUPS = 32
CLASSES = 32
ACTIONS = 18
SEQS = 768


def place_ends(entries, own_key, low, top_value):
    longest = entries.shape.index(max(entries.shape))
    spots = []
    for shift in (0, 1):
        where = [jax.random.randint(jax.random.fold_in(own_key, axis), (), 0, length) for axis, length in enumerate(entries.shape)]
        where[longest] = (where[longest] + shift) % entries.shape[longest]
        spots.append(tuple(where))
    return entries.at[spots[0]].set(low).at[spots[1]].set(top_value)


def level_of(stream_key, dims, cuts, smallest, top_value):
    factor_of = 1.0
    for position, blocks in cuts:
        heights = jax.random.uniform(jax.random.fold_in(jax.random.fold_in(stream_key, 6), position), (blocks,), jnp.float32, smallest / len(cuts), top_value / len(cuts))
        factor_of = factor_of * jnp.repeat(jnp.exp(heights), dims[position] // blocks).reshape((-1,) + (1,) * (len(dims) - 1 - position))
    return factor_of


def profile(count, total, limit, skew):
    portions = [(1 << 20) // math.isqrt(standing ** skew) + 1 for standing in range(2, count + 1)]
    spare, counts = total - limit - (count - 1), [1] * (count - 1)
    while spare > 0:
        movable = [i for i in range(count - 1) if counts[i] < limit]
        mass, left = sum([portions[i] for i in movable]), spare
        for i in movable:
            more = min(limit - counts[i], max(1, left * portions[i] // mass), spare)
            counts[i] = counts[i] + more
            spare = spare - more
    return np.array([limit] + counts)


def uneven_parts(key, count, total, bound, skew):
    if count == 2:
        one = jax.random.randint(key, (), max(1, total - bound), min(bound, total - 1) + 1)
        return jnp.stack([one, total - one])
    tallies = jnp.asarray(profile(count, total, bound, skew), jnp.int32)
    couples = (count - 1) // 2
    giver, receiver = tallies[1:1 + 2 * couples:2], tallies[2:2 + 2 * couples:2]
    room = jnp.minimum(giver - 1, bound - receiver)
    moved = jax.random.randint(jax.random.fold_in(key, 1), (couples,), 0, 1 << 20) % (room + 1)
    tallies = tallies.at[1:1 + 2 * couples:2].set(giver - moved).at[2:2 + 2 * couples:2].set(receiver + moved)
    return tallies[jax.random.permutation(jax.random.fold_in(key, 2), count)]


def bell_draw(own_key, extent, scale, most, cuts=(), held_as=jnp.bfloat16):
    loudness = level_of(own_key, extent, cuts, -0.22, 0.18) if cuts else 1.0
    values = jax.random.normal(own_key, extent, jnp.float32) * scale * loudness
    return jnp.minimum(jnp.maximum(values, -most), most).astype(held_as)


def setup_inputs(seed: int = 0) -> dict:
    keys = jax.random.split(jax.random.key(seed), 19)
    return {
        "latents": place_ends(jax.random.randint(keys[0], (SEQS, LEN, GROUPS), 0, CLASSES), jax.random.fold_in(keys[0], 1), 0, CLASSES - 1).astype(jnp.int32),
        "actions": place_ends(jax.random.randint(keys[1], (SEQS, LEN), 0, ACTIONS), jax.random.fold_in(keys[1], 1), 0, ACTIONS - 1).astype(jnp.int32),
        "segment_ids": jax.vmap(lambda own: jnp.searchsorted(jnp.cumsum(uneven_parts(own, 4, LEN, 32, 0)), jnp.arange(LEN), side="right"))(jax.random.split(keys[2], SEQS)).reshape((SEQS, LEN)).astype(jnp.int32),
        "cotangent": bell_draw(keys[3], (SEQS, LEN, D), 1.0, 6.0, ((0, 2), (1, 16))),
        "stem_weight": bell_draw(keys[4], (GROUPS * CLASSES, D), (GROUPS + 1) ** -0.5, 1.0),
        "action_table": bell_draw(keys[5], (ACTIONS, D), (GROUPS + 1) ** -0.5, 1.0),
        "first_gain": jnp.clip(1.0 + 0.1 * jax.random.normal(keys[6], (D,), jnp.float32), 0.5, 1.5),
        "first_bias": bell_draw(keys[7], (D,), 0.2, 1.0, (), jnp.float32),
        "query_weight": bell_draw(keys[8], (D, HEADS * HD), D ** -0.5, 0.25, ((1, 2),)),
        "key_weight": bell_draw(keys[9], (D, HEADS * HD), D ** -0.5, 0.25, ((1, 2),)),
        "value_weight": bell_draw(keys[10], (D, HEADS * HD), D ** -0.5, 0.25, ((1, 2),)),
        "out_weight": bell_draw(keys[11], (HEADS * HD, D), (HEADS * HD // 16) ** -0.5, 1.0, ((0, 2),)),
        "second_gain": jnp.clip(1.0 + 0.1 * jax.random.normal(keys[12], (D,), jnp.float32), 0.5, 1.5),
        "second_bias": bell_draw(keys[13], (D,), 0.2, 1.0, (), jnp.float32),
        "up_weight": bell_draw(keys[14], (D, FF), D ** -0.5, 0.25, ((1, 2),)),
        "up_bias": bell_draw(keys[15], (FF,), 0.2, 1.0, ((0, 2),), jnp.float32),
        "down_weight": bell_draw(keys[16], (FF, D), FF ** -0.5, 0.125, ((0, 2),)),
        "down_bias": bell_draw(keys[17], (D,), 0.2, 1.0, (), jnp.float32),
    }


@jax.custom_vjp
def low(v):
    return lax.optimization_barrier(v.astype(jnp.bfloat16)).astype(jnp.float32)

@jax.custom_vjp
def low_back(v):
    return v

def low_keep(v):
    return (low(v), None)

def low_pass(kept, grad):
    return (grad,)

def back_keep(v):
    return (v, None)

def back_low(kept, grad):
    return (low(grad),)
low.defvjp(low_keep, low_pass)
low_back.defvjp(back_keep, back_low)
HIGH = lax.Precision.HIGHEST
EPSILON = 1e-05

def norm_rows(values, gain, bias):
    average = lax.optimization_barrier(jnp.mean(values, axis=-1, keepdims=True))
    centred = values - average
    spread = lax.optimization_barrier(jnp.mean(centred * centred, axis=-1, keepdims=True))
    return centred * lax.rsqrt(spread + EPSILON) * gain + bias

def matmul(left, right):
    return jnp.dot(left, right, precision=HIGH)

def forward(params, shift, latent_hot, action_hot, segments):
    stem_weight, action_table, first_gain, first_bias, query_weight, key_weight, value_weight, out_weight, second_gain, second_bias, up_weight, up_bias, down_weight, down_bias = params
    number = segments.shape[0]
    length = segments.shape[1]
    stem = matmul(latent_hot, stem_weight) + matmul(action_hot, action_table)
    tokens = low(low_back(stem + shift))
    normed_one = low(norm_rows(tokens, first_gain, first_bias))
    layout = (number, length, HEADS, HD)
    query = low(low_back(matmul(normed_one, query_weight))).reshape(layout)
    key_rows = low(low_back(matmul(normed_one, key_weight))).reshape(layout)
    value_rows = low(low_back(matmul(normed_one, value_weight))).reshape(layout)
    scores = low_back(0.125 * jnp.einsum('gqhd,gkhd->ghqk', query, key_rows, precision=HIGH))
    place = jnp.arange(length)
    allowed = (segments[:, None, :, None] == segments[:, None, None, :]) & (place[:, None] >= place[None, :])
    probs = jax.nn.softmax(jnp.where(allowed, scores, -1e+30), axis=-1)
    probs_low = low(low_back(probs))
    mixed = jnp.einsum('ghqk,gkhd->gqhd', probs_low, value_rows, precision=HIGH)
    mixed = low(low_back(mixed.reshape(number * length, HEADS * HD)))
    branch = low_back(matmul(mixed, out_weight))
    resid = tokens + branch
    normed_two = low(norm_rows(resid, second_gain, second_bias))
    pre_act = low_back(matmul(normed_two, up_weight) + up_bias)
    hidden = low(jax.nn.gelu(pre_act))
    return resid + matmul(hidden, down_weight) + down_bias

def reference(latents, actions, segment_ids, cotangent, stem_weight, action_table, first_gain, first_bias, query_weight, key_weight, value_weight, out_weight, second_gain, second_bias, up_weight, up_bias, down_weight, down_bias):
    params = tuple((item.astype(jnp.float32) for item in (stem_weight, action_table, first_gain, first_bias, query_weight, key_weight, value_weight, out_weight, second_gain, second_bias, up_weight, up_bias, down_weight, down_bias)))
    number = latents.shape[0]
    length = latents.shape[1]
    group = math.gcd(number, max(1, 4096 // length))
    turns = number // group
    frames = group * length
    inputs = (latents.reshape(turns, group, length, GROUPS), actions.reshape(turns, group, length), segment_ids.reshape(turns, group, length), cotangent.reshape(turns, group, length, D))

    def one_group(total, pieces):
        latent_block, action_block, segment_block, cot_block = pieces
        latent_hot = (latent_block[..., None] == jnp.arange(CLASSES)).reshape(frames, GROUPS * CLASSES)
        latent_hot = latent_hot.astype(jnp.float32)
        action_hot = (action_block.reshape(frames, 1) == jnp.arange(ACTIONS)[None, :]).astype(jnp.float32)
        shift = jnp.zeros((frames, D), jnp.float32)

        def run(weights, offset):
            return forward(weights, offset, latent_hot, action_hot, segment_block)
        result, pull = jax.vjp(run, params, shift)
        grads, dshift = pull(cot_block.reshape(frames, D).astype(jnp.float32))
        total = jax.tree.map(lambda left, right: left + right, total, grads)
        return (total, (result.astype(jnp.bfloat16).reshape(group, length, D), dshift.astype(jnp.bfloat16).reshape(group, length, D)))
    start = jax.tree.map(jnp.zeros_like, params)
    total, (output, token_grad) = lax.scan(one_group, start, inputs)
    output = output.reshape(number, length, D)
    token_grad = token_grad.reshape(number, length, D)
    return (output, token_grad, total[0], total[1], total[2], total[3], total[4], total[5], total[6], total[7], total[8], total[9], total[10], total[11], total[12], total[13])
```

```python
import functools

import jax
import jax.numpy as jnp
from jax import lax
from jax.experimental import pallas as pl
from jax.experimental.pallas import tpu as pltpu
from jax.sharding import PartitionSpec as P

HD = 64
PACK = 256
EPSILON = 1e-05
FLOAT = jnp.float32
BFLOAT = jnp.bfloat16
TILE = 512
FFB = 512
HOT_PAD = 128
GELU_C = 0.7978845608028654
GELU_A = 0.044715


def dot(left, right):
    return lax.dot_general(left, right, (((1,), (0,)), ((), ())), preferred_element_type=FLOAT)


def dot_t(left, right):
    return lax.dot_general(left, right, (((1,), (1,)), ((), ())), preferred_element_type=FLOAT)


def t_dot(left, right):
    return lax.dot_general(left, right, (((0,), (0,)), ((), ())), preferred_element_type=FLOAT)


def iota(shape, dim):
    return lax.broadcasted_iota(jnp.int32, shape, dim)


def norm_stats(values):
    average = jnp.mean(values, axis=-1, keepdims=True)
    centred = values - average
    spread = jnp.mean(centred * centred, axis=-1, keepdims=True)
    scale = lax.rsqrt(spread + EPSILON)
    return centred * scale, scale


def norm_back(grad, xhat, scale, gain):
    scaled = grad * gain
    mean_e = jnp.mean(scaled, axis=-1, keepdims=True)
    mean_x = jnp.mean(scaled * xhat, axis=-1, keepdims=True)
    return (scaled - mean_e - xhat * mean_x) * scale


def col_sum(values):
    return jnp.sum(values, axis=0, keepdims=True)


def head_reduce(values, op, fill):
    parts = []
    for half in range(PACK // 128):
        piece = values[:, half * 128 : (half + 1) * 128]
        low = iota(piece.shape, 1) < HD
        first = op(jnp.where(low, piece, fill), axis=-1, keepdims=True)
        second = op(jnp.where(low, fill, piece), axis=-1, keepdims=True)
        parts.append((low, first, second))
    return parts


def head_spread(parts):
    return jnp.concatenate([jnp.where(low, a, b) for low, a, b in parts], axis=1)


def block_diag(rows):
    mask = (iota((PACK, PACK), 0) // HD) == (iota((PACK, PACK), 1) // HD)
    return jnp.where(mask, jnp.concatenate([rows] * (PACK // HD), axis=0), jnp.zeros((), rows.dtype))


def diag_rows(full):
    lane_head = iota((HD, PACK), 1) // HD
    result = full[:HD]
    for head in range(1, PACK // HD):
        result = jnp.where(lane_head == head, full[head * HD : (head + 1) * HD], result)
    return result


def unrolled_loop(count, body):
    if count == 1:
        body(0)
    else:
        pl.loop(0, count)(body)


def compute_kernel(
    local_len,
    lat_ref,
    mask_ref,
    cot_ref,
    stem_ref,
    wqkv_ref,
    wout_ref,
    wup_ref,
    wdown_ref,
    vec_ref,
    upb_ref,
    out_ref,
    tg_ref,
    gstem_ref,
    gqkv_ref,
    gout_ref,
    gup_ref,
    gdown_ref,
    gvec_ref,
    gupb_ref,
    tok_s,
    n1_s,
    qkv_s,
    prob_s,
    mix_s,
    dbr_s,
    acc_s,
    dn_s,
    n2_s,
    cotp_s,
):
    rows, width = tok_s.shape
    length = cot_ref.shape[0] * local_len
    packs = width // PACK
    group_seqs = 16 // local_len
    group_rows = group_seqs * length
    tile = max(TILE, group_rows)
    tiles = rows // tile
    ff = wup_ref.shape[1]
    hot_width = stem_ref.shape[0]
    classes = (hot_width - HOT_PAD) // 32

    def perm(shape_rows):
        dest = iota((shape_rows, shape_rows), 0)
        src = iota((shape_rows, shape_rows), 1)
        want = ((dest % length) // local_len) * 16 + (dest // length) * local_len + dest % local_len
        return jnp.where(want == src, 1.0, 0.0).astype(BFLOAT)

    def perm_back(shape_rows):
        dest = iota((shape_rows, shape_rows), 1)
        src = iota((shape_rows, shape_rows), 0)
        want = ((dest % length) // local_len) * 16 + (dest // length) * local_len + dest % local_len
        return jnp.where(want == src, 1.0, 0.0).astype(BFLOAT)

    def make_hot(r0):
        lats = lat_ref[pl.ds(r0, tile), :]
        kk = lats.shape[1]
        parts = []
        for block in range(0, hot_width, 128):
            g = iota((kk, 128), 0)
            c = iota((kk, 128), 1) + block
            spread = jnp.where(jnp.minimum(c // classes, 32) == g, 1.0, 0.0).astype(BFLOAT)
            val = dot(lats, spread)
            lane = iota((tile, 128), 1)
            target = (lane + block) % classes if block < hot_width - HOT_PAD else lane
            parts.append(jnp.where(val == target.astype(FLOAT), 1.0, 0.0).astype(BFLOAT))
        return jnp.concatenate(parts, axis=1)

    gstem_ref[...] = jnp.zeros_like(gstem_ref)
    gqkv_ref[...] = jnp.zeros_like(gqkv_ref)
    gout_ref[...] = jnp.zeros_like(gout_ref)
    gup_ref[...] = jnp.zeros_like(gup_ref)
    gdown_ref[...] = jnp.zeros_like(gdown_ref)
    gvec_ref[...] = jnp.zeros_like(gvec_ref)
    gupb_ref[...] = jnp.zeros_like(gupb_ref)

    g1 = vec_ref[0:1, :]
    b1 = vec_ref[1:2, :]
    g2 = vec_ref[2:3, :]
    b2 = vec_ref[3:4, :]
    bd = vec_ref[4:5, :]

    @pl.loop(0, tiles)
    def phase_one(t):
        r0 = pl.multiple_of(t * tile, tile)
        here = pl.ds(r0, tile)
        tokens = dot(make_hot(r0), stem_ref[...]).astype(BFLOAT)
        tok_s[here, :] = tokens
        xhat, _ = norm_stats(tokens.astype(FLOAT))
        normed = (xhat * g1 + b1).astype(BFLOAT)
        n1_s[here, :] = normed
        for part in range(3):
            cols = slice(part * width, (part + 1) * width)
            value = dot(normed, wqkv_ref[:, cols])
            if part == 0:
                value = value.astype(BFLOAT).astype(FLOAT) * 0.125
            qkv_s[here, cols] = value.astype(BFLOAT)

        @pl.loop(0, tile // 256)
        def attend(sub):
            for seq in range(256 // length):
                s0 = pl.multiple_of(r0 + sub * 256 + seq * length, length)
                bias = mask_ref[pl.ds(s0, length), :].astype(FLOAT)
                for pack in range(packs):
                    c0 = pack * PACK
                    q = qkv_s[pl.ds(s0, length), c0 : c0 + PACK]
                    k = qkv_s[pl.ds(s0, length), width + c0 : width + c0 + PACK]
                    v = qkv_s[pl.ds(s0, length), 2 * width + c0 : 2 * width + c0 + PACK]
                    scores = dot_t(q, block_diag(k)) + bias
                    top = head_spread(head_reduce(scores, jnp.max, -3e38))
                    e = jnp.exp(scores - top)
                    sums = head_reduce(e, jnp.sum, 0.0)
                    inv = head_spread([(low, 1.0 / a, 1.0 / b) for low, a, b in sums])
                    probs = (e * inv).astype(BFLOAT)
                    prob_s[pl.ds(s0, length), c0 : c0 + PACK] = probs
                    mix_s[pl.ds(s0, length), c0 : c0 + PACK] = dot(probs, block_diag(v)).astype(BFLOAT)

    @pl.loop(0, tiles)
    def phase_two(t):
        r0 = pl.multiple_of(t * tile, tile)
        here = pl.ds(r0, tile)
        mixed = mix_s[here, :]
        resid = tok_s[here, :].astype(FLOAT) + dot(mixed, wout_ref[...])
        xhat, scale = norm_stats(resid)
        n2_s[...] = (xhat * g2 + b2).astype(BFLOAT)
        for g in range(tile // group_rows):
            k0 = pl.multiple_of((t * (tile // group_rows) + g) * 16, 16)
            raw = cot_ref[:, pl.ds(k0, 16), :].reshape(group_rows, width)
            cotp_s[g * group_rows : (g + 1) * group_rows, :] = dot(perm(group_rows), raw).astype(BFLOAT)
        acc_s[...] = resid + bd
        dn_s[...] = jnp.zeros_like(dn_s)

        @pl.loop(0, ff // FFB)
        def feed(f):
            f0 = pl.multiple_of(f * FFB, FFB)
            fs = pl.ds(f0, FFB)
            n2 = n2_s[...]
            cot = cotp_s[...]
            up = wup_ref[:, fs]
            down = wdown_ref[fs, :]
            pre = dot(n2, up) + upb_ref[0:1, fs]
            square = pre * pre
            tanh = jnp.tanh(GELU_C * pre * (1.0 + GELU_A * square))
            half = 0.5 * (1.0 + tanh)
            hidden = (pre * half).astype(BFLOAT)
            slope = half + (0.5 * GELU_C) * pre * (1.0 - tanh * tanh) * (1.0 + 3.0 * GELU_A * square)
            acc_s[...] += dot(hidden, down)
            gdown_ref[fs, :] += t_dot(hidden, cot)
            d_pre_f = (dot_t(cot, down) * slope).astype(BFLOAT)
            gupb_ref[0:1, fs] += col_sum(d_pre_f.astype(FLOAT))
            gup_ref[:, fs] += t_dot(n2, d_pre_f)
            dn_s[...] += dot_t(d_pre_f, up)

        cot_f = cotp_s[...].astype(FLOAT)
        gvec_ref[4:5, :] += col_sum(cot_f)
        out = acc_s[...].astype(BFLOAT)
        for g in range(tile // group_rows):
            k0 = pl.multiple_of((t * (tile // group_rows) + g) * 16, 16)
            back = dot(perm_back(group_rows), out[g * group_rows : (g + 1) * group_rows, :])
            out_ref[:, pl.ds(k0, 16), :] = back.astype(BFLOAT).reshape(length // local_len, 16, width)
        resid = tok_s[here, :].astype(FLOAT) + dot(mix_s[here, :], wout_ref[...])
        xhat, scale = norm_stats(resid)
        dn = dn_s[...]
        gvec_ref[2:3, :] += col_sum(dn * xhat)
        gvec_ref[3:4, :] += col_sum(dn)
        d_branch = (cot_f + norm_back(dn, xhat, scale, g2)).astype(BFLOAT)
        dbr_s[here, :] = d_branch
        gout_ref[...] += t_dot(mix_s[here, :], d_branch)
        mix_s[here, :] = dot_t(d_branch, wout_ref[...]).astype(BFLOAT)

    @pl.loop(0, tiles)
    def phase_three(t):
        r0 = pl.multiple_of(t * tile, tile)
        here = pl.ds(r0, tile)

        @pl.loop(0, tile // 256)
        def attend(sub):
            for seq in range(256 // length):
                s0 = pl.multiple_of(r0 + sub * 256 + seq * length, length)
                rs = pl.ds(s0, length)
                for pack in range(packs):
                    c0 = pack * PACK
                    q = qkv_s[rs, c0 : c0 + PACK]
                    k = qkv_s[rs, width + c0 : width + c0 + PACK]
                    v = qkv_s[rs, 2 * width + c0 : 2 * width + c0 + PACK]
                    grad = mix_s[rs, c0 : c0 + PACK]
                    low = prob_s[rs, c0 : c0 + PACK]
                    probs = low.astype(FLOAT)
                    d_probs = dot_t(grad, block_diag(v)).astype(BFLOAT).astype(FLOAT)
                    centre = head_spread(head_reduce(probs * d_probs, jnp.sum, 0.0))
                    d_scores = (probs * (d_probs - centre)).astype(BFLOAT)
                    d_query = 0.125 * dot(d_scores, block_diag(k))
                    d_key = diag_rows(t_dot(d_scores, q))
                    d_value = diag_rows(t_dot(low, grad))
                    qkv_s[rs, c0 : c0 + PACK] = d_query.astype(BFLOAT)
                    qkv_s[rs, width + c0 : width + c0 + PACK] = d_key.astype(BFLOAT)
                    qkv_s[rs, 2 * width + c0 : 2 * width + c0 + PACK] = d_value.astype(BFLOAT)

        normed = n1_s[here, :]
        dn = jnp.zeros((tile, width), FLOAT)
        for part in range(3):
            cols = slice(part * width, (part + 1) * width)
            piece = qkv_s[here, cols]
            gqkv_ref[:, cols] += t_dot(normed, piece)
            dn += dot_t(piece, wqkv_ref[:, cols])
        xhat, scale = norm_stats(tok_s[here, :].astype(FLOAT))
        gvec_ref[0:1, :] += col_sum(dn * xhat)
        gvec_ref[1:2, :] += col_sum(dn)
        token_grad = (dbr_s[here, :].astype(FLOAT) + norm_back(dn, xhat, scale, g1)).astype(BFLOAT)
        gstem_ref[...] += t_dot(make_hot(r0), token_grad)
        for g in range(tile // group_rows):
            k0 = pl.multiple_of((t * (tile // group_rows) + g) * 16, 16)
            back = dot(perm_back(group_rows), token_grad[g * group_rows : (g + 1) * group_rows, :])
            tg_ref[:, pl.ds(k0, 16), :] = back.astype(BFLOAT).reshape(length // local_len, 16, width)


def run_compute(local_len, lat, mask, cot, stem, wqkv, wout, wup, wdown, vec, upb):
    rows, width = lat.shape[0], stem.shape[1]
    ff = wup.shape[1]
    group_rows = 16 // local_len * (cot.shape[0] * local_len)
    tile = max(TILE, group_rows)
    shape = jax.ShapeDtypeStruct
    vm = pl.BlockSpec(memory_space=pltpu.VMEM)
    return pl.pallas_call(
        functools.partial(compute_kernel, local_len),
        out_shape=(
            shape(cot.shape, BFLOAT),
            shape(cot.shape, BFLOAT),
            shape(stem.shape, FLOAT),
            shape(wqkv.shape, FLOAT),
            shape(wout.shape, FLOAT),
            shape(wup.shape, FLOAT),
            shape(wdown.shape, FLOAT),
            shape(vec.shape, FLOAT),
            shape(upb.shape, FLOAT),
        ),
        in_specs=[vm] * 10,
        out_specs=[vm] * 9,
        scratch_shapes=[
            pltpu.VMEM((rows, width), BFLOAT),
            pltpu.VMEM((rows, width), BFLOAT),
            pltpu.VMEM((rows, 3 * width), BFLOAT),
            pltpu.VMEM((rows, width), BFLOAT),
            pltpu.VMEM((rows, width), BFLOAT),
            pltpu.VMEM((rows, width), BFLOAT),
            pltpu.VMEM((tile, width), FLOAT),
            pltpu.VMEM((tile, width), FLOAT),
            pltpu.VMEM((tile, width), BFLOAT),
            pltpu.VMEM((tile, width), BFLOAT),
        ],
        compiler_params=pltpu.CompilerParams(vmem_limit_bytes=60 * 1024 * 1024),
    )(lat, mask, cot, stem, wqkv, wout, wup, wdown, vec, upb)


def per_device(
    latents,
    actions,
    segment_ids,
    cotangent,
    stem_weight,
    action_table,
    first_gain,
    first_bias,
    query_weight,
    key_weight,
    value_weight,
    out_weight,
    second_gain,
    second_bias,
    up_weight,
    up_bias,
    down_weight,
    down_bias,
):
    half_seqs, local_len, groups = latents.shape
    width = stem_weight.shape[1]
    places = lax.axis_size("gx")
    length = places * local_len
    seqs = half_seqs // places
    rows = seqs * length
    actions_n = action_table.shape[0]

    lat = jnp.concatenate([latents, actions[..., None]], axis=-1).astype(BFLOAT)
    lat = lat.reshape(places, seqs, local_len, groups + 1)
    lat = lax.all_to_all(lat, "gx", split_axis=0, concat_axis=0, tiled=True)
    lat = lat.transpose(1, 0, 2, 3).reshape(rows, groups + 1)
    lat = jnp.pad(lat, ((0, 0), (0, 128 - groups - 1)))
    cot = cotangent.reshape(places, seqs * local_len, width)
    cot = lax.all_to_all(cot, "gx", split_axis=0, concat_axis=0, tiled=True)
    first_seq = (lax.axis_index("gy") * places + lax.axis_index("gx")) * seqs
    seg = lax.dynamic_slice_in_dim(segment_ids, first_seq, seqs, 0)
    place = jnp.arange(length)
    allowed = (seg[:, :, None] == seg[:, None, :]) & (place[:, None] >= place[None, :])[None]
    mask = jnp.where(allowed, 0.0, -1e30).astype(BFLOAT).reshape(rows, length)
    mask = jnp.tile(mask, (1, PACK // length))
    stem = jnp.concatenate(
        [stem_weight, jnp.pad(action_table, ((0, HOT_PAD - actions_n), (0, 0)))], axis=0
    )
    gather = functools.partial(lax.all_gather, axis_name="gy", tiled=True)
    wqkv = jnp.concatenate(
        [gather(item, axis=1) for item in (query_weight, key_weight, value_weight)], axis=1
    )
    wout = gather(out_weight, axis=0)
    wup = gather(up_weight, axis=1)
    wdown = gather(down_weight, axis=0)
    upb = jnp.broadcast_to(gather(up_bias, axis=0)[None], (8, wup.shape[1]))
    vec = jnp.stack([first_gain, first_bias, second_gain, second_bias, down_bias] + [down_bias] * 3)
    out, tg, gstem, gqkv, gout, gup, gdown, gvec, gupb = run_compute(
        local_len, lat, mask, cot, stem, wqkv, wout, wup, wdown, vec, upb
    )
    out = lax.all_to_all(out, "gx", split_axis=0, concat_axis=0, tiled=True)
    tg = lax.all_to_all(tg, "gx", split_axis=0, concat_axis=0, tiled=True)
    out = out.reshape(half_seqs, local_len, width)
    tg = tg.reshape(half_seqs, local_len, width)
    both = ("gx", "gy")
    gstem, gvec = lax.psum((gstem, gvec), both)

    def shard(value, dim):
        return lax.psum(lax.psum_scatter(value, "gy", scatter_dimension=dim, tiled=True), "gx")

    gq = shard(gqkv[:, :width], 1)
    gk = shard(gqkv[:, width : 2 * width], 1)
    gv = shard(gqkv[:, 2 * width :], 1)
    return (
        out,
        tg,
        gstem[: groups * 32],
        gstem[groups * 32 : groups * 32 + actions_n],
        gvec[0],
        gvec[1],
        gq,
        gk,
        gv,
        shard(gout, 0),
        gvec[2],
        gvec[3],
        shard(gup, 1),
        shard(gupb[0], 0),
        shard(gdown, 0),
        gvec[4],
    )


def solution(mesh):
    return jax.shard_map(
        per_device,
        mesh=mesh,
        in_specs=(
            P("gy", "gx", None),
            P("gy", "gx"),
            P(),
            P("gy", "gx", None),
            P(),
            P(),
            P(),
            P(),
            P(None, "gy"),
            P(None, "gy"),
            P(None, "gy"),
            P("gy", None),
            P(),
            P(),
            P(None, "gy"),
            P("gy"),
            P("gy", None),
            P(),
        ),
        out_specs=(
            P("gy", "gx", None),
            P("gy", "gx", None),
            P(),
            P(),
            P(),
            P(),
            P(None, "gy"),
            P(None, "gy"),
            P(None, "gy"),
            P("gy", None),
            P(),
            P(),
            P(None, "gy"),
            P("gy"),
            P("gy", None),
            P(),
        ),
        check_vma=False,
    )
```

```python
import functools

import jax
import jax.numpy as jnp
from jax import lax
from jax.experimental import pallas as pl
from jax.experimental.pallas import tpu as pltpu
from jax.sharding import PartitionSpec as P

HD = 64
PACK = 256
EPSILON = 1e-05
FLOAT = jnp.float32
BFLOAT = jnp.bfloat16
TILE = 512
MAX_ROWS = 2048
VMEM_LIMIT = 60 * 1024 * 1024
UNIT = 4
FFB = 512
HOT_PAD = 128
GELU_C = 0.7978845608028654
GELU_A = 0.044715


def dot(left, right):
    return lax.dot_general(left, right, (((1,), (0,)), ((), ())), preferred_element_type=FLOAT)


def dot_t(left, right):
    return lax.dot_general(left, right, (((1,), (1,)), ((), ())), preferred_element_type=FLOAT)


def t_dot(left, right):
    return lax.dot_general(left, right, (((0,), (0,)), ((), ())), preferred_element_type=FLOAT)


def iota(shape, dim):
    return lax.broadcasted_iota(jnp.int32, shape, dim)


def norm_stats(values):
    average = jnp.mean(values, axis=-1, keepdims=True)
    centred = values - average
    spread = jnp.mean(centred * centred, axis=-1, keepdims=True)
    scale = lax.rsqrt(spread + EPSILON)
    return centred * scale, scale


def norm_back(grad, xhat, scale, gain):
    scaled = grad * gain
    mean_e = jnp.mean(scaled, axis=-1, keepdims=True)
    mean_x = jnp.mean(scaled * xhat, axis=-1, keepdims=True)
    return (scaled - mean_e - xhat * mean_x) * scale


def col_sum(values):
    return jnp.sum(values, axis=0, keepdims=True)


def head_reduce(values, op, fill):
    parts = []
    for half in range(PACK // 128):
        piece = values[:, half * 128 : (half + 1) * 128]
        low = iota(piece.shape, 1) < HD
        first = op(jnp.where(low, piece, fill), axis=-1, keepdims=True)
        second = op(jnp.where(low, fill, piece), axis=-1, keepdims=True)
        parts.append((low, first, second))
    return parts


def head_spread(parts):
    return jnp.concatenate([jnp.where(low, a, b) for low, a, b in parts], axis=1)


def block_diag(rows):
    mask = (iota((PACK, PACK), 0) // HD) == (iota((PACK, PACK), 1) // HD)
    return jnp.where(mask, jnp.concatenate([rows] * (PACK // HD), axis=0), jnp.zeros((), rows.dtype))


def diag_rows(full):
    lane_head = iota((HD, PACK), 1) // HD
    result = full[:HD]
    for head in range(1, PACK // HD):
        result = jnp.where(lane_head == head, full[head * HD : (head + 1) * HD], result)
    return result


def unrolled_loop(count, body):
    if count == 1:
        body(0)
    else:
        pl.loop(0, count)(body)


def row_maps(local_len, length, count, back):
    dest = iota((count, count), 1 if back else 0)
    src = iota((count, count), 0 if back else 1)
    want = ((dest % length) // local_len) * 16 + (dest // length) * local_len + dest % local_len
    return jnp.where(want == src, 1.0, 0.0).astype(BFLOAT)


def block_compute(local_len, refs, hooks):
    lat_ref, mask_ref, cot_ref, stem_ref, wqkv_ref, wout_ref, wup_ref, wdown_ref, vec_ref, upb_ref = refs["in"]
    out_ref, tg_ref = refs["stage"]
    gstem_ref, gqkv_ref, gout_ref, gup_ref, gdown_ref, gvec_ref = refs["grads"]
    tok_s, qkv_s, prob_s, mix_s, dbr_s, acc_s, dn_s, n2_s, cotp_s = refs["work"]
    rows, width = tok_s.shape
    places = cot_ref.shape[0]
    length = places * local_len
    packs = width // PACK
    group_rows = 16 // local_len * length
    tile = acc_s.shape[0]
    tiles = rows // tile
    groups = tile // group_rows
    ff = wup_ref.shape[1]
    hot_width = stem_ref.shape[0]
    classes = (hot_width - HOT_PAD) // 32

    def to_frames(ref, t, values):
        for g in range(groups):
            k0 = pl.multiple_of((t * groups + g) * 16, 16)
            back = dot(
                row_maps(local_len, length, group_rows, True),
                values[g * group_rows : (g + 1) * group_rows, :],
            )
            ref[:, pl.ds(k0, 16), :] = back.astype(BFLOAT).reshape(places, 16, width)

    def from_frames(ref, t):
        parts = []
        for g in range(groups):
            k0 = pl.multiple_of((t * groups + g) * 16, 16)
            raw = ref[:, pl.ds(k0, 16), :].reshape(group_rows, ref.shape[2])
            parts.append(dot(row_maps(local_len, length, group_rows, False), raw).astype(BFLOAT))
        return jnp.concatenate(parts, axis=0) if groups > 1 else parts[0]

    def make_hot(t):
        lats = from_frames(lat_ref, t)
        kk = lats.shape[1]
        parts = []
        for block in range(0, hot_width, 128):
            g = iota((kk, 128), 0)
            c = iota((kk, 128), 1) + block
            spread = jnp.where(jnp.minimum(c // classes, 32) == g, 1.0, 0.0).astype(BFLOAT)
            val = dot(lats, spread)
            lane = iota((tile, 128), 1)
            target = (lane + block) % classes if block < hot_width - HOT_PAD else lane
            parts.append(jnp.where(val == target.astype(FLOAT), 1.0, 0.0).astype(BFLOAT))
        return jnp.concatenate(parts, axis=1)

    def gvec_add(row, values):
        gvec_ref[row : row + 1, :] += values

    gstem_ref[...] = jnp.zeros_like(gstem_ref)
    gqkv_ref[...] = jnp.zeros_like(gqkv_ref)
    gout_ref[...] = jnp.zeros_like(gout_ref)
    gup_ref[...] = jnp.zeros_like(gup_ref)
    gdown_ref[...] = jnp.zeros_like(gdown_ref)
    gvec_ref[...] = jnp.zeros_like(gvec_ref)

    g1 = vec_ref[0:1, :]
    b1 = vec_ref[1:2, :]
    g2 = vec_ref[2:3, :]
    b2 = vec_ref[3:4, :]
    bd = vec_ref[4:5, :]

    hooks["start"]()

    @pl.loop(0, tiles)
    def phase_one(t):
        r0 = pl.multiple_of(t * tile, tile)
        here = pl.ds(r0, tile)
        hooks["lat_ready"](t)
        tokens = dot(make_hot(t), stem_ref[...]).astype(BFLOAT)
        tok_s[here, :] = tokens
        xhat, _ = norm_stats(tokens.astype(FLOAT))
        normed = (xhat * g1 + b1).astype(BFLOAT)
        hooks["qkv_ready"](t)
        for part in range(3):
            cols = slice(part * width, (part + 1) * width)
            value = dot(normed, wqkv_ref[:, cols])
            if part == 0:
                value = value.astype(BFLOAT).astype(FLOAT) * 0.125
            qkv_s[here, cols] = value.astype(BFLOAT)

        @pl.loop(0, tile // 256)
        def attend(sub):
            for seq0 in range(0, 256 // length, UNIT):
                units = []
                for seq in range(seq0, seq0 + UNIT):
                    s0 = pl.multiple_of(r0 + sub * 256 + seq * length, length)
                    units += [(pl.ds(s0, length), pack * PACK) for pack in range(packs)]
                qs = [block_diag(qkv_s[rs, c0 : c0 + PACK]) for rs, c0 in units]
                ks = [qkv_s[rs, width + c0 : width + c0 + PACK] for rs, c0 in units]
                scores = [dot_t(k, q) + mask_ref[rs, :].astype(FLOAT) for q, k, (rs, _) in zip(qs, ks, units)]
                es = [jnp.exp(x - jnp.max(x, axis=0, keepdims=True)) for x in scores]
                ps = [(e * (1.0 / jnp.sum(e, axis=0, keepdims=True))).astype(BFLOAT) for e in es]
                vs = [qkv_s[rs, 2 * width + c0 : 2 * width + c0 + PACK] for rs, c0 in units]
                ms = [diag_rows(t_dot(p, v)).astype(BFLOAT) for p, v in zip(ps, vs)]
                for p, m, (rs, c0) in zip(ps, ms, units):
                    prob_s[rs, c0 : c0 + PACK] = p
                    mix_s[rs, c0 : c0 + PACK] = m

    hooks["forward_done"]()

    @pl.loop(0, tiles)
    def phase_two(t):
        r0 = pl.multiple_of(t * tile, tile)
        here = pl.ds(r0, tile)
        resid = tok_s[here, :].astype(FLOAT) + dot(mix_s[here, :], wout_ref[...])
        xhat, scale = norm_stats(resid)
        n2_s[...] = (xhat * g2 + b2).astype(BFLOAT)
        hooks["cot_ready"](t)
        cotp_s[...] = from_frames(cot_ref, t)
        acc_s[...] = resid + bd
        dn_s[...] = jnp.zeros_like(dn_s)

        @pl.loop(0, ff // FFB)
        def feed(f):
            f0 = pl.multiple_of(f * FFB, FFB)
            fs = pl.ds(f0, FFB)
            n2 = n2_s[...]
            cot = cotp_s[...]
            up = wup_ref[:, fs]
            down = wdown_ref[fs, :]
            pre = dot(n2, up) + upb_ref[0:1, fs]
            square = pre * pre
            tanh = jnp.tanh(GELU_C * pre * (1.0 + GELU_A * square))
            half = 0.5 * (1.0 + tanh)
            hidden = (pre * half).astype(BFLOAT)
            slope = half + (0.5 * GELU_C) * pre * (1.0 - tanh * tanh) * (1.0 + 3.0 * GELU_A * square)
            acc_s[...] += dot(hidden, down)
            gdown_ref[fs, :] += t_dot(hidden, cot)
            d_pre = (dot_t(cot, down) * slope).astype(BFLOAT)
            sums = col_sum(d_pre.astype(FLOAT))
            for part in range(FFB // width):
                row = pl.multiple_of((f * (FFB // width) + part) * 16, 16)
                gvec_ref[pl.ds(row, 1), :] += sums[:, part * width : (part + 1) * width]
            gup_ref[:, fs] += t_dot(n2, d_pre)
            dn_s[...] += dot_t(d_pre, up)

        cot_f = cotp_s[...].astype(FLOAT)
        gvec_add(5, col_sum(cot_f))
        to_frames(out_ref, t, acc_s[...].astype(BFLOAT))
        hooks["out_ready"](t)
        resid = tok_s[here, :].astype(FLOAT) + dot(mix_s[here, :], wout_ref[...])
        xhat, scale = norm_stats(resid)
        dn = dn_s[...]
        gvec_add(3, col_sum(dn * xhat))
        gvec_add(4, col_sum(dn))
        d_branch = (cot_f + norm_back(dn, xhat, scale, g2)).astype(BFLOAT)
        dbr_s[here, :] = d_branch
        gout_ref[...] += t_dot(mix_s[here, :], d_branch)
        mix_s[here, :] = dot_t(d_branch, wout_ref[...]).astype(BFLOAT)

    hooks["feed_done"]()

    @pl.loop(0, tiles)
    def phase_three(t):
        r0 = pl.multiple_of(t * tile, tile)
        here = pl.ds(r0, tile)

        @pl.loop(0, tile // 256)
        def attend(sub):
            for seq0 in range(0, 256 // length, UNIT):
                units = []
                for seq in range(seq0, seq0 + UNIT):
                    s0 = pl.multiple_of(r0 + sub * 256 + seq * length, length)
                    units += [(pl.ds(s0, length), pack * PACK) for pack in range(packs)]
                gs = [block_diag(mix_s[rs, c0 : c0 + PACK]) for rs, c0 in units]
                vs = [qkv_s[rs, 2 * width + c0 : 2 * width + c0 + PACK] for rs, c0 in units]
                dps = [dot_t(v, g).astype(BFLOAT).astype(FLOAT) for v, g in zip(vs, gs)]
                lows = [prob_s[rs, c0 : c0 + PACK] for rs, c0 in units]
                ws = [low.astype(FLOAT) * dp for low, dp in zip(lows, dps)]
                dss = [
                    (w - low.astype(FLOAT) * jnp.sum(w, axis=0, keepdims=True)).astype(BFLOAT)
                    for w, low in zip(ws, lows)
                ]
                dvs = [dot(low, g).astype(BFLOAT) for low, g in zip(lows, gs)]
                ks = [qkv_s[rs, width + c0 : width + c0 + PACK] for rs, c0 in units]
                qs = [block_diag(qkv_s[rs, c0 : c0 + PACK]) for rs, c0 in units]
                dks = [dot(ds, q).astype(BFLOAT) for ds, q in zip(dss, qs)]
                dqs = [(0.125 * diag_rows(t_dot(ds, k))).astype(BFLOAT) for ds, k in zip(dss, ks)]
                for dq, dk, dv, (rs, c0) in zip(dqs, dks, dvs, units):
                    qkv_s[rs, c0 : c0 + PACK] = dq
                    qkv_s[rs, width + c0 : width + c0 + PACK] = dk
                    qkv_s[rs, 2 * width + c0 : 2 * width + c0 + PACK] = dv

        xhat, scale = norm_stats(tok_s[here, :].astype(FLOAT))
        normed = (xhat * g1 + b1).astype(BFLOAT)
        for part in range(3):
            cols = slice(part * width, (part + 1) * width)
            gqkv_ref[:, cols] += t_dot(normed, qkv_s[here, cols])
        dn = dot_t(qkv_s[here, :], wqkv_ref[...])
        gvec_add(1, col_sum(dn * xhat))
        gvec_add(2, col_sum(dn))
        token_grad = (dbr_s[here, :].astype(FLOAT) + norm_back(dn, xhat, scale, g1)).astype(BFLOAT)
        hooks["tg_room"](t)
        to_frames(tg_ref, t, token_grad)
        hooks["tg_ready"](t)
        gstem_ref[...] += t_dot(make_hot(t), token_grad)
        hooks["tile_done"](t)


def no_tile_hook(t):
    return None


def no_hook():
    return None


NO_HOOKS = {
    "lat_ready": no_tile_hook,
    "qkv_ready": no_tile_hook,
    "cot_ready": no_tile_hook,
    "out_ready": no_tile_hook,
    "tg_room": no_tile_hook,
    "tg_ready": no_tile_hook,
    "tile_done": no_tile_hook,
    "start": no_hook,
    "forward_done": no_hook,
    "feed_done": no_hook,
}


def work_shapes(rows, width, tile):
    return [
        pltpu.VMEM((rows, width), BFLOAT),
        pltpu.VMEM((rows, 3 * width), BFLOAT),
        pltpu.VMEM((rows, width), BFLOAT),
        pltpu.VMEM((rows, width), BFLOAT),
        pltpu.VMEM((rows, width), BFLOAT),
        pltpu.VMEM((tile, width), FLOAT),
        pltpu.VMEM((tile, width), FLOAT),
        pltpu.VMEM((tile, width), BFLOAT),
        pltpu.VMEM((tile, width), BFLOAT),
    ]


def local_kernel(local_len, *refs):
    block_compute(
        local_len,
        {"in": refs[:10], "stage": refs[10:12], "grads": refs[12:18], "work": refs[18:]},
        NO_HOOKS,
    )


def run_local(local_len, lat, mask, cot, stem, wqkv, wout, wup, wdown, vec, upb):
    places, per, width = cot.shape
    group_rows = 16 // local_len * (places * local_len)
    shape = jax.ShapeDtypeStruct
    vm = pl.BlockSpec(memory_space=pltpu.VMEM)
    return pl.pallas_call(
        functools.partial(local_kernel, local_len),
        out_shape=(
            shape(cot.shape, BFLOAT),
            shape(cot.shape, BFLOAT),
            shape(stem.shape, FLOAT),
            shape(wqkv.shape, FLOAT),
            shape(wout.shape, FLOAT),
            shape(wup.shape, FLOAT),
            shape(wdown.shape, FLOAT),
            shape((wup.shape[1] // width * 16, width), FLOAT),
        ),
        in_specs=[vm] * 10,
        out_specs=[vm] * 8,
        scratch_shapes=work_shapes(places * per, width, max(TILE, group_rows)),
        compiler_params=pltpu.CompilerParams(vmem_limit_bytes=60 * 1024 * 1024),
    )(lat, mask, cot, stem, wqkv, wout, wup, wdown, vec, upb)


def wait_for(ref, sem):
    pltpu.make_async_copy(ref, ref, sem).wait()


class Reducer:
    def __init__(self, where, pieces, bufs, final, sems):
        self.i, self.j, self.peer = where
        self.pieces = pieces
        self.send, self.r1, self.r2, self.r3, self.r4, self.r5, self.own, self.fin = bufs
        self.final = final
        self.ssem, self.rsem = sems
        self.half = self.own.shape[0]
        self.core = lax.rem(self.i, 2)

    def copy(self, n, src, dst, device):
        return pltpu.make_async_remote_copy(
            src_ref=src,
            dst_ref=dst,
            send_sem=self.ssem.at[n],
            recv_sem=self.rsem.at[n],
            device_id=device,
            device_id_type=pl.DeviceIdType.MESH,
        )

    def near(self, bit):
        step = 1 << bit
        return (self.i + step - 2 * step * lax.rem(self.i // step, 2), self.j)

    def bit(self, n):
        return lax.rem(self.i // (1 << n), 2)

    def start_core(self):
        for h in range(2):
            for at, take in self.pieces(h, 1 - self.core):
                self.send[h, at[0], at[1]] = take().astype(BFLOAT)
        self.copy(0, self.send, self.r1, self.near(0)).start()

    def core_to_x(self):
        self.copy(0, self.send, self.r1, self.near(0)).wait()
        for at, take in self.pieces(1 - self.j, self.core):
            arrived = self.r1[1 - self.j, at[0], at[1]].astype(FLOAT)
            self.send[0, at[0], at[1]] = (take() + arrived).astype(BFLOAT)
        self.copy(1, self.send.at[0], self.r2, (self.i, 1 - self.j)).start()
        for at, take in self.pieces(self.j, self.core):
            self.own[at[0], at[1]] = take() + self.r1[self.j, at[0], at[1]].astype(FLOAT)

    def region(self, level):
        start, count = 0, self.half
        for n in range(1, level + 1):
            count //= 2
            start = start + self.bit(n) * count
        return start, count

    def halving(self, level):
        start, count = self.region(level - 1)
        half = count // 2
        theirs = pl.multiple_of(start + (1 - self.bit(level)) * half, 16)
        mine = pl.multiple_of(start + self.bit(level) * half, 16)
        base = self.half - 2 * half
        src = self.send.at[1, base : base + half, :]
        return half, theirs, mine, base, self.copy(1 + level, src, (self.r3, self.r4, self.r5)[level - 1], self.near(level))

    def start_level(self, level):
        half, theirs, mine, base, copy = self.halving(level)
        self.send[1, base : base + half, :] = self.own[pl.ds(theirs, half), :].astype(BFLOAT)
        copy.start()

    def finish_level(self, level):
        half, theirs, mine, base, copy = self.halving(level)
        copy.wait()
        rows = pl.ds(mine, half)
        self.own[rows, :] += (self.r3, self.r4, self.r5)[level - 1][...].astype(FLOAT)

    def x_to_level(self):
        self.copy(1, self.send.at[0], self.r2, (self.i, 1 - self.j)).wait()
        self.own[...] += self.r2[...].astype(FLOAT)
        self.start_level(1)

    def next_level(self, level):
        self.finish_level(level)
        self.start_level(level + 1)

    def place(self, level):
        start, count = self.region(level)
        return self.final.at[self.core, pl.ds(pl.multiple_of(start, 16), count), :]

    def gather_copy(self, level):
        src = self.place(level)
        return self.copy(4 + level, src, src, self.near(level))

    def last_level(self):
        self.finish_level(3)
        start, count = self.region(3)
        self.fin[...] = self.own[pl.ds(pl.multiple_of(start, 16), count), :].astype(BFLOAT)
        keep = pltpu.make_async_copy(self.fin, self.place(3), self.ssem.at[8])
        keep.start()
        keep.wait()
        self.gather_copy(3).start()

    def gather(self, level):
        self.gather_copy(level).wait()
        self.gather_copy(level - 1).start()

    def core_gather(self):
        return self.copy(9, self.final.at[self.core], self.final.at[self.core], self.near(0))


def wide_kernel(local_len, *refs):
    (
        lat_hbm, mask_ref, cot_hbm, stem_ref, wq_hbm, wk_hbm, wv_hbm, wo_hbm, wup_hbm, wdown_hbm, vec_ref, upb_hbm,
        out_hbm, tg_hbm, feed_hbm, rest_hbm, shared_hbm,
        lat_s, frame_s, wqkv_s, wout_s, wup_s, wdown_s, upb_s,
        gstem_s, gqkv_s, gout_s, gup_s, gdown_s, gvec_s,
    ) = refs[:30]
    work = refs[30:37]
    feed_bufs = refs[37:45]
    rest_bufs = refs[45:51] + (gdown_s.at[0 : refs[45].shape[1], :],) + refs[51:52]
    tile = work[5].shape[0]
    own_s = feed_bufs[6]
    work = work[:5] + (own_s.at[0:tile, :], own_s.at[tile : 2 * tile, :]) + work[5:]
    (
        lat_send, lat_recv, cot_send, cot_recv, own_sem, out_send, out_recv, tg_send, tg_recv,
        w_local, wx_send, wx_recv, wc_send, wc_recv, fs_send, fs_recv, rs_send, rs_recv, sh_send, sh_recv,
    ) = refs[52:]
    i, j = lax.axis_index("gx"), lax.axis_index("gy")
    places = lax.axis_size("gx")
    core = lax.rem(i, 2)
    sibling = (i + 1 - 2 * core, j)
    across = (i, 1 - j)
    tiles = work[0].shape[0] // tile
    width = work[0].shape[1]
    per = tile // places
    mesh_id = pl.DeviceIdType.MESH

    def remote(src, dst, send, recv, device):
        return pltpu.make_async_remote_copy(
            src_ref=src, dst_ref=dst, send_sem=send, recv_sem=recv, device_id=device, device_id_type=mesh_id
        )

    barrier = pltpu.get_barrier_semaphore()

    @pl.loop(1, places)
    def greet(k):
        pl.semaphore_signal(barrier, inc=1, device_id=(lax.rem(i + k, places), j), device_id_type=mesh_id)

    pl.semaphore_signal(barrier, inc=1, device_id=across, device_id_type=mesh_id)
    pl.semaphore_wait(barrier, places)

    def chunk(t):
        return pl.ds(pl.multiple_of(t * per, per), per)

    def scatter(src, dst, t, send, recv):
        @pl.loop(1, places)
        def each(k):
            d = lax.rem(i + k, places)
            remote(src.at[d, chunk(t), :], dst.at[i, chunk(t), :], send, recv, (d, j)).start()

    def keep(src, dst, t, sem):
        return pltpu.make_async_copy(src.at[i, chunk(t), :], dst.at[i, chunk(t), :], sem)

    def most(ref, t):
        return ref.at[0 : places - 1, chunk(t), :]

    half = wq_hbm.shape[1]
    cols = [pl.multiple_of(part * width + j * half, half) for part in range(3)]
    far_cols = [pl.multiple_of(part * width + (1 - j) * half, half) for part in range(3)]

    def weight_views(owner, whole):
        def rows_of(count):
            return pl.ds(0, count) if whole else pl.ds(pl.multiple_of(core * (count // 2), 16), count // 2)

        views = []
        for part, src in enumerate((wq_hbm, wk_hbm, wv_hbm)):
            r = rows_of(width)
            at = pl.ds(pl.multiple_of(part * width + owner * half, half), half)
            views.append((src.at[r, :], wqkv_s.at[r, at]))
        count = wo_hbm.shape[0]
        r = rows_of(count)
        base = 0 if whole else core * (count // 2)
        size = count if whole else count // 2
        views.append((wo_hbm.at[r, :], wout_s.at[pl.ds(pl.multiple_of(owner * count + base, 16), size), :]))
        r = rows_of(width)
        count = wup_hbm.shape[1]
        views.append((wup_hbm.at[r, :], wup_s.at[r, pl.ds(pl.multiple_of(owner * count, 128), count)]))
        count = wdown_hbm.shape[0]
        r = rows_of(count)
        base = 0 if whole else core * (count // 2)
        size = count if whole else count // 2
        views.append((wdown_hbm.at[r, :], wdown_s.at[pl.ds(pl.multiple_of(owner * count + base, 16), size), :]))
        return views

    here_views = weight_views(j, True)
    x_copies = [
        remote(src, dst, wx_send.at[n], wx_recv.at[n], across) for n, (src, dst) in enumerate(weight_views(j, False))
    ]
    c_copies = [
        remote(dst, dst, wc_send.at[n], wc_recv.at[n], sibling)
        for n, (_, dst) in enumerate(weight_views(1 - j, False))
    ]
    own_copies = [pltpu.make_async_copy(src, dst, w_local.at[n]) for n, (src, dst) in enumerate(here_views)]
    ff_half = upb_hbm.shape[1]
    upb_at = pl.ds(pl.multiple_of(j * ff_half, 128), ff_half)
    upb_x = remote(upb_hbm, upb_s.at[:, upb_at], wx_send.at[6], wx_recv.at[6], across)
    upb_own = pltpu.make_async_copy(upb_hbm, upb_s.at[:, upb_at], w_local.at[6])

    for n in range(3):
        x_copies[n].start()

    @pl.loop(0, tiles)
    def send_lat(t):
        keep(lat_hbm, lat_s, t, own_sem.at[t]).start()
        scatter(lat_hbm, lat_s, t, lat_send, lat_recv.at[t])

    for n in range(3):
        own_copies[n].start()

    @pl.loop(0, tiles)
    def send_cot(t):
        keep(cot_hbm, frame_s, t, own_sem.at[tiles + t]).start()
        scatter(cot_hbm, frame_s, t, cot_send, cot_recv.at[t])

    upb_x.start()
    upb_own.start()
    for n in range(3, 6):
        x_copies[n].start()
        own_copies[n].start()

    def pass_on(first, last):
        for n in range(first, last):
            x_copies[n].wait()
            c_copies[n].start()

    def settle(first, last):
        for n in range(first, last):
            c_copies[n].wait()
            own_copies[n].wait()

    hooks = dict(NO_HOOKS)

    def lat_ready(t):
        keep(lat_hbm, lat_s, t, own_sem.at[t]).wait()
        wait_for(most(lat_s, t), lat_recv.at[t])

    def qkv_ready(t):
        @pl.when(t == 0)
        def _():
            pass_on(0, 3)
            settle(0, 3)

    def forward_done():
        pass_on(3, 6)
        upb_x.wait()
        upb_own.wait()
        settle(3, 6)

    def cot_ready(t):
        keep(cot_hbm, frame_s, t, own_sem.at[tiles + t]).wait()
        wait_for(most(frame_s, t), cot_recv.at[t])

    def out_ready(t):
        keep(frame_s, out_hbm, t, own_sem.at[2 * tiles + t]).start()
        scatter(frame_s, out_hbm, t, out_send.at[t], out_recv)

    def tg_room(t):
        keep(frame_s, out_hbm, t, own_sem.at[2 * tiles + t]).wait()
        wait_for(most(frame_s, t), out_send.at[t])

    def tg_ready(t):
        keep(frame_s, tg_hbm, t, own_sem.at[3 * tiles + t]).start()
        scatter(frame_s, tg_hbm, t, tg_send.at[t], tg_recv)

    def grab(ref, r0, nrows, c0, ncols):
        return lambda: ref[pl.ds(r0, nrows), pl.ds(c0, ncols)]

    def mult(value, by):
        return pl.multiple_of(value, by)

    up_half = gup_s.shape[1] // 2
    up_rows = width // 2
    down_rows = gdown_s.shape[0] // 4
    out_rows = gout_s.shape[0] // 4
    stem_rows = gstem_s.shape[0] // 4

    def feed_pieces(h, c):
        found, base = [], 0
        for block in range(up_half // width):
            found.append(
                (
                    (slice(base, base + up_rows), slice(None)),
                    grab(gup_s, mult(c * up_rows, 16), up_rows, mult(h * up_half + block * width, 128), width),
                )
            )
            base += up_rows
        found.append(
            (
                (slice(base, base + down_rows), slice(None)),
                grab(gdown_s, mult((h * 2 + c) * down_rows, 16), down_rows, 0, width),
            )
        )
        base += down_rows
        found.append(
            (
                (slice(base, base + out_rows), slice(None)),
                grab(gout_s, mult((h * 2 + c) * out_rows, 16), out_rows, 0, width),
            )
        )
        return found

    def rest_pieces(h, c):
        found, base = [], 0
        qrows = width // 2
        for part in range(2):
            found.append(
                (
                    (slice(0, qrows), slice(part * half, (part + 1) * half)),
                    grab(gqkv_s, mult(c * qrows, 16), qrows, mult(part * width + h * half, 128), half),
                )
            )
        base = qrows
        for part in range(2):
            found.append(
                (
                    (slice(base, base + qrows // 2), slice(part * half, (part + 1) * half)),
                    grab(gqkv_s, mult(c * qrows + part * (qrows // 2), 16), qrows // 2, mult(2 * width + h * half, 128), half),
                )
            )
        base += qrows // 2
        found.append(
            (
                (slice(base, base + stem_rows), slice(None)),
                grab(gstem_s, mult((h * 2 + c) * stem_rows, 16), stem_rows, 0, width),
            )
        )
        base += stem_rows
        found.append(
            ((slice(base, base + 16), slice(None)), grab(gvec_s, mult((h * 2 + c) * 16, 16), 16, 0, width))
        )
        base += 16
        end = rest_bufs[6].shape[0]
        found.append(
            ((slice(base, end), slice(None)), lambda base=base: jnp.zeros((end - base, width), FLOAT))
        )
        return found

    where = (i, j, places)
    feed = Reducer(where, feed_pieces, feed_bufs, feed_hbm, (fs_send, fs_recv))
    rest = Reducer(where, rest_pieces, rest_bufs, rest_hbm, (rs_send, rs_recv))

    def feed_done():
        feed.start_core()

    def tile_done(t):
        @pl.when(t == 0)
        def _():
            feed.core_to_x()

    hooks.update(
        lat_ready=lat_ready,
        qkv_ready=qkv_ready,
        forward_done=forward_done,
        cot_ready=cot_ready,
        out_ready=out_ready,
        tg_room=tg_room,
        tg_ready=tg_ready,
        feed_done=feed_done,
        tile_done=tile_done,
    )
    block_compute(
        local_len,
        {
            "in": (lat_s, mask_ref, frame_s, stem_ref, wqkv_s, wout_s, wup_s, wdown_s, vec_ref, upb_s),
            "stage": (frame_s, frame_s),
            "grads": (gstem_s, gqkv_s, gout_s, gup_s, gdown_s, gvec_s),
            "work": work,
        },
        hooks,
    )
    rest.start_core()
    rest.core_to_x()
    feed.x_to_level()
    feed.next_level(1)
    rest.x_to_level()
    feed.next_level(2)
    rest.next_level(1)
    feed.last_level()
    rest.next_level(2)
    feed.gather(3)
    rest.last_level()
    feed.gather(2)
    rest.gather(3)
    feed.gather_copy(1).wait()
    feed.core_gather().start()
    rest.gather(2)
    rest.gather_copy(1).wait()
    rest.core_gather().start()
    first = shared_hbm.shape[2]
    tail_at = rest.half - first
    tail = rest_hbm.at[core, tail_at : tail_at + first, :]
    mine = shared_hbm.at[j, core]
    to_x = remote(tail, mine, sh_send.at[0], sh_recv.at[0], across)
    to_x.start()
    stay = pltpu.make_async_copy(tail, mine, sh_send.at[2])
    stay.start()
    stay.wait()
    to_x.wait()
    to_core = remote(shared_hbm.at[:, core], shared_hbm.at[:, core], sh_send.at[1], sh_recv.at[1], sibling)
    to_core.start()
    feed.core_gather().wait()
    rest.core_gather().wait()
    to_core.wait()
    wait_for(lat_hbm.at[0 : places - 1], lat_send)
    wait_for(cot_hbm.at[0 : places - 1], cot_send)
    wait_for(out_hbm.at[0 : places - 1], out_recv)
    wait_for(tg_hbm.at[0 : places - 1], tg_recv)

    @pl.loop(0, tiles)
    def drain(t):
        keep(frame_s, tg_hbm, t, own_sem.at[3 * tiles + t]).wait()
        wait_for(most(frame_s, t), tg_send.at[t])


def reduce_shapes(half, width, own):
    return [
        pltpu.VMEM((2, half, width), BFLOAT),
        pltpu.VMEM((2, half, width), BFLOAT),
        pltpu.VMEM((half, width), BFLOAT),
        pltpu.VMEM((half // 2, width), BFLOAT),
        pltpu.VMEM((half // 4, width), BFLOAT),
        pltpu.VMEM((half // 8, width), BFLOAT),
    ] + [pltpu.VMEM((half, width), FLOAT)] * own + [pltpu.VMEM((half // 8, width), BFLOAT)]


def run_wide(local_len, lat, mask, cot, stem, wq, wk, wv, wo, wup, wdown, vec, upb):
    places, per, width = cot.shape
    rows = places * per
    ff = 2 * wup.shape[1]
    shape = jax.ShapeDtypeStruct
    vm = pl.BlockSpec(memory_space=pltpu.VMEM)
    hbm = pl.BlockSpec(memory_space=pl.ANY)
    feed_half = (width // 2) * (wup.shape[1] // width) + ff // 4 + width // 4
    rest_used = width // 2 + width // 4 + stem.shape[0] // 4 + 16
    rest_half = -(-rest_used // 128) * 128
    shared = rest_half - (width // 2 + width // 4)
    tiles = rows // TILE
    dma = pltpu.SemaphoreType.DMA
    return pl.pallas_call(
        functools.partial(wide_kernel, local_len),
        out_shape=(
            shape(cot.shape, BFLOAT),
            shape(cot.shape, BFLOAT),
            shape((2, feed_half, width), BFLOAT),
            shape((2, rest_half, width), BFLOAT),
            shape((2, 2, shared, width), BFLOAT),
        ),
        in_specs=[hbm, vm, hbm, vm, hbm, hbm, hbm, hbm, hbm, hbm, vm, hbm],
        out_specs=[hbm] * 5,
        scratch_shapes=[
            pltpu.VMEM(lat.shape, BFLOAT),
            pltpu.VMEM(cot.shape, BFLOAT),
            pltpu.VMEM((width, 3 * width), BFLOAT),
            pltpu.VMEM((width, width), BFLOAT),
            pltpu.VMEM((width, ff), BFLOAT),
            pltpu.VMEM((ff, width), BFLOAT),
            pltpu.VMEM((8, ff), FLOAT),
            pltpu.VMEM(stem.shape, FLOAT),
            pltpu.VMEM((width, 3 * width), FLOAT),
            pltpu.VMEM((width, width), FLOAT),
            pltpu.VMEM((width, ff), FLOAT),
            pltpu.VMEM((ff, width), FLOAT),
            pltpu.VMEM((ff // width * 16, width), FLOAT),
        ]
        + [item for n, item in enumerate(work_shapes(rows, width, TILE)) if n not in (5, 6)]
        + reduce_shapes(feed_half, width, 1)
        + reduce_shapes(rest_half, width, 0)
        + [
            dma,
            dma((tiles,)),
            dma,
            dma((tiles,)),
            dma((4 * tiles,)),
            dma((tiles,)),
            dma,
            dma((tiles,)),
            dma,
            dma((7,)),
            dma((7,)),
            dma((7,)),
            dma((6,)),
            dma((6,)),
            dma((10,)),
            dma((10,)),
            dma((10,)),
            dma((10,)),
            dma((3,)),
            dma((3,)),
        ],
        compiler_params=pltpu.CompilerParams(
            vmem_limit_bytes=VMEM_LIMIT, collective_id=0, has_side_effects=True
        ),
    )(lat, mask, cot, stem, wq, wk, wv, wo, wup, wdown, vec, upb)


def per_device(
    latents,
    actions,
    segment_ids,
    cotangent,
    stem_weight,
    action_table,
    first_gain,
    first_bias,
    query_weight,
    key_weight,
    value_weight,
    out_weight,
    second_gain,
    second_bias,
    up_weight,
    up_bias,
    down_weight,
    down_bias,
):
    half_seqs, local_len, groups = latents.shape
    width = stem_weight.shape[1]
    places = lax.axis_size("gx")
    length = places * local_len
    seqs = half_seqs // places
    rows = seqs * length
    actions_n = action_table.shape[0]

    lat = jnp.concatenate([latents, actions[..., None]], axis=-1).astype(BFLOAT)
    lat = lat.reshape(places, seqs * local_len, groups + 1)
    lat = jnp.pad(lat, ((0, 0), (0, 0), (0, 128 - groups - 1)))
    cot = cotangent.reshape(places, seqs * local_len, width)
    first_seq = (lax.axis_index("gy") * places + lax.axis_index("gx")) * seqs
    seg = lax.dynamic_slice_in_dim(segment_ids, first_seq, seqs, 0)
    place = jnp.arange(length)
    allowed = (seg[:, :, None] == seg[:, None, :]) & (place[:, None] >= place[None, :])[None]
    mask = jnp.where(allowed.swapaxes(1, 2), 0.0, -1e30).astype(BFLOAT).reshape(rows, length)
    mask = jnp.tile(mask, (1, PACK // length))
    stem = jnp.concatenate(
        [stem_weight, jnp.pad(action_table, ((0, HOT_PAD - actions_n), (0, 0)))], axis=0
    )
    vec = jnp.stack([first_gain, first_bias, second_gain, second_bias, down_bias] + [down_bias] * 3)
    if rows % TILE == 0 and rows <= MAX_ROWS and places == 16:
        upb = jnp.broadcast_to(up_bias[None], (8, up_bias.shape[0]))
        out, tg, feed, rest, shared = run_wide(
            local_len, lat, mask, cot, stem, query_weight, key_weight, value_weight,
            out_weight, up_weight, down_weight, vec, upb,
        )
        out = out.reshape(half_seqs, local_len, width)
        tg = tg.reshape(half_seqs, local_len, width)
        feed = feed.astype(FLOAT)
        rest = rest.astype(FLOAT)
        shared = shared.astype(FLOAT)
        half = width // 2
        cols = query_weight.shape[1]
        blocks = up_weight.shape[1] // width
        gup = jnp.concatenate([feed[:, b * half : (b + 1) * half] for b in range(blocks)], axis=2)
        gup = gup.reshape(up_weight.shape)
        base = blocks * half
        quarter = down_weight.shape[0] // 2
        gdown = feed[:, base : base + quarter].reshape(down_weight.shape)
        gout = feed[:, base + quarter :].reshape(out_weight.shape)
        gq = rest[:, :half, :cols].reshape(width, cols)
        gk = rest[:, :half, cols:].reshape(width, cols)
        part = rest[:, half : half + half // 2]
        gv = jnp.concatenate([part[:, :, :cols], part[:, :, cols:]], axis=1).reshape(width, cols)
        stem_rows = stem.shape[0] // 4
        gstem = shared[:, :, :stem_rows].reshape(stem.shape)
        first = shared[0, 0, stem_rows:]
        at = half + half // 2 + stem_rows
        return (
            out,
            tg,
            gstem[: groups * 32],
            gstem[groups * 32 : groups * 32 + actions_n],
            first[1],
            first[2],
            gq,
            gk,
            gv,
            gout,
            first[3],
            first[4],
            gup,
            rest[:, at].reshape(up_bias.shape),
            gdown,
            first[5],
        )
    lat = lax.all_to_all(lat, "gx", split_axis=0, concat_axis=0, tiled=True)
    cot = lax.all_to_all(cot, "gx", split_axis=0, concat_axis=0, tiled=True)
    gather = functools.partial(lax.all_gather, axis_name="gy", tiled=True)
    wqkv = jnp.concatenate(
        [gather(item, axis=1) for item in (query_weight, key_weight, value_weight)], axis=1
    )
    wout = gather(out_weight, axis=0)
    wup = gather(up_weight, axis=1)
    wdown = gather(down_weight, axis=0)
    upb = jnp.broadcast_to(gather(up_bias, axis=0)[None], (8, wup.shape[1]))
    out, tg, gstem, gqkv, gout, gup, gdown, gvec = run_local(
        local_len, lat, mask, cot, stem, wqkv, wout, wup, wdown, vec, upb
    )
    out = lax.all_to_all(out, "gx", split_axis=0, concat_axis=0, tiled=True)
    tg = lax.all_to_all(tg, "gx", split_axis=0, concat_axis=0, tiled=True)
    out = out.reshape(half_seqs, local_len, width)
    tg = tg.reshape(half_seqs, local_len, width)
    both = ("gx", "gy")
    gstem, gvec = lax.psum((gstem, gvec), both)
    upb_grad = gvec[::16].reshape(-1)
    upb_grad = lax.dynamic_slice_in_dim(upb_grad, lax.axis_index("gy") * up_bias.shape[0], up_bias.shape[0])

    def shard(value, dim):
        return lax.psum(lax.psum_scatter(value, "gy", scatter_dimension=dim, tiled=True), "gx")

    gq = shard(gqkv[:, :width], 1)
    gk = shard(gqkv[:, width : 2 * width], 1)
    gv = shard(gqkv[:, 2 * width :], 1)
    return (
        out,
        tg,
        gstem[: groups * 32],
        gstem[groups * 32 : groups * 32 + actions_n],
        gvec[1],
        gvec[2],
        gq,
        gk,
        gv,
        shard(gout, 0),
        gvec[3],
        gvec[4],
        shard(gup, 1),
        upb_grad,
        shard(gdown, 0),
        gvec[5],
    )


def solution(mesh):
    return jax.shard_map(
        per_device,
        mesh=mesh,
        in_specs=(
            P("gy", "gx", None),
            P("gy", "gx"),
            P(),
            P("gy", "gx", None),
            P(),
            P(),
            P(),
            P(),
            P(None, "gy"),
            P(None, "gy"),
            P(None, "gy"),
            P("gy", None),
            P(),
            P(),
            P(None, "gy"),
            P("gy"),
            P("gy", None),
            P(),
        ),
        out_specs=(
            P("gy", "gx", None),
            P("gy", "gx", None),
            P(),
            P(),
            P(),
            P(),
            P(None, "gy"),
            P(None, "gy"),
            P(None, "gy"),
            P("gy", None),
            P(),
            P(),
            P(None, "gy"),
            P("gy"),
            P("gy", None),
            P(),
        ),
        check_vma=False,
    )
```

```python
import functools

import jax
import jax.numpy as jnp
from jax import lax
from jax.experimental import pallas as pl
from jax.experimental.pallas import tpu as pltpu
from jax.sharding import PartitionSpec as P

HD = 64
PACK = 256
EPSILON = 1e-05
FLOAT = jnp.float32
BFLOAT = jnp.bfloat16
TILE = 512
MAX_ROWS = 2048
VMEM_LIMIT = 60 * 1024 * 1024
UNIT = 4
SUB = 512
FFB = 512
HOT_PAD = 128
GELU_C = 0.7978845608028654
GELU_A = 0.044715


def dot(left, right):
    return lax.dot_general(left, right, (((1,), (0,)), ((), ())), preferred_element_type=FLOAT)


def dot_t(left, right):
    return lax.dot_general(left, right, (((1,), (1,)), ((), ())), preferred_element_type=FLOAT)


def t_dot(left, right):
    return lax.dot_general(left, right, (((0,), (0,)), ((), ())), preferred_element_type=FLOAT)


def iota(shape, dim):
    return lax.broadcasted_iota(jnp.int32, shape, dim)


def norm_stats(values):
    average = jnp.mean(values, axis=-1, keepdims=True)
    centred = values - average
    spread = jnp.mean(centred * centred, axis=-1, keepdims=True)
    scale = lax.rsqrt(spread + EPSILON)
    return centred * scale, scale


def norm_back(grad, xhat, scale, gain):
    scaled = grad * gain
    mean_e = jnp.mean(scaled, axis=-1, keepdims=True)
    mean_x = jnp.mean(scaled * xhat, axis=-1, keepdims=True)
    return (scaled - mean_e - xhat * mean_x) * scale


def col_sum(values):
    return jnp.sum(values, axis=0, keepdims=True)


def head_reduce(values, op, fill):
    parts = []
    for half in range(PACK // 128):
        piece = values[:, half * 128 : (half + 1) * 128]
        low = iota(piece.shape, 1) < HD
        first = op(jnp.where(low, piece, fill), axis=-1, keepdims=True)
        second = op(jnp.where(low, fill, piece), axis=-1, keepdims=True)
        parts.append((low, first, second))
    return parts


def head_spread(parts):
    return jnp.concatenate([jnp.where(low, a, b) for low, a, b in parts], axis=1)


def block_diag(rows):
    mask = (iota((PACK, PACK), 0) // HD) == (iota((PACK, PACK), 1) // HD)
    return jnp.where(mask, jnp.concatenate([rows] * (PACK // HD), axis=0), jnp.zeros((), rows.dtype))


def diag_rows(full):
    lane_head = iota((HD, PACK), 1) // HD
    result = full[:HD]
    for head in range(1, PACK // HD):
        result = jnp.where(lane_head == head, full[head * HD : (head + 1) * HD], result)
    return result


def unrolled_loop(count, body):
    if count == 1:
        body(0)
    else:
        pl.loop(0, count)(body)


def row_maps(local_len, length, count, back):
    dest = iota((count, count), 1 if back else 0)
    src = iota((count, count), 0 if back else 1)
    want = ((dest % length) // local_len) * 16 + (dest // length) * local_len + dest % local_len
    return jnp.where(want == src, 1.0, 0.0).astype(BFLOAT)


def block_compute(local_len, refs, hooks):
    lat_ref, seg_ref, cot_ref, stem_ref, wqkv_ref, wout_ref, wup_ref, wdown_ref, upb_ref = refs["in"]
    out_ref, tg_ref = refs["stage"]
    gstem_ref, gqkv_ref, gout_ref, gup_ref, gdown_ref, gvec_ref = refs["grads"]
    tok_s, qkv_s, prob_s, mix_s, dbr_s, acc_s, dn_s, n2_s, cotp_s = refs["work"]
    rows, width = tok_s.shape
    places = cot_ref.shape[0]
    length = places * local_len
    packs = width // PACK
    group_rows = 16 // local_len * length
    tile = acc_s.shape[0]
    tiles = rows // tile
    groups = tile // group_rows
    ff = wup_ref.shape[1]
    hot_width = stem_ref.shape[0]
    classes = (hot_width - HOT_PAD) // 32

    def to_frames(ref, t, values):
        for g in range(groups):
            k0 = pl.multiple_of((t * groups + g) * 16, 16)
            back = dot(
                row_maps(local_len, length, group_rows, True),
                values[g * group_rows : (g + 1) * group_rows, :],
            )
            ref[:, pl.ds(k0, 16), :] = back.astype(BFLOAT).reshape(places, 16, width)

    def from_frames(ref, t):
        parts = []
        for g in range(groups):
            k0 = pl.multiple_of((t * groups + g) * 16, 16)
            raw = ref[:, pl.ds(k0, 16), :].reshape(group_rows, ref.shape[2])
            parts.append(dot(row_maps(local_len, length, group_rows, False), raw).astype(BFLOAT))
        return jnp.concatenate(parts, axis=0) if groups > 1 else parts[0]

    pairs = refs["pairs"]
    lat_rows = tile // places // pairs
    slot = lat_ref.shape[2] // pairs

    def make_hot(t):
        k0 = pl.multiple_of(t * lat_rows, lat_rows)
        raw = lat_ref[:, pl.ds(k0, lat_rows), :].reshape(places * lat_rows, lat_ref.shape[2])
        dest = iota((tile, places * lat_rows), 0)
        src = iota((tile, places * lat_rows), 1)
        frame = dest % local_len
        want = ((dest % length) // local_len) * lat_rows
        want += (dest // length) * (local_len // pairs) + frame // pairs
        lats = dot(jnp.where(want == src, 1.0, 0.0).astype(BFLOAT), raw)
        if pairs > 1:
            turn = iota(lats.shape, 0) % pairs
            lats = jnp.where(iota(lats.shape, 1) // slot == turn, lats, 0.0)
        lats = lats.astype(BFLOAT)
        parts = []
        for block in range(0, hot_width, 128):
            g = iota((lats.shape[1], 128), 0) % slot
            c = iota((lats.shape[1], 128), 1) + block
            spread = jnp.where(jnp.minimum(c // classes, 32) == g, 1.0, 0.0).astype(BFLOAT)
            val = dot(lats, spread)
            lane = iota((tile, 128), 1)
            target = (lane + block) % classes if block < hot_width - HOT_PAD else lane
            parts.append(jnp.where(val == target.astype(FLOAT), 1.0, 0.0).astype(BFLOAT))
        return jnp.concatenate(parts, axis=1)

    def gvec_add(row, values):
        gvec_ref[row : row + 1, :] += values

    gstem_ref[...] = jnp.zeros_like(gstem_ref)
    gqkv_ref[...] = jnp.zeros_like(gqkv_ref)
    gout_ref[...] = jnp.zeros_like(gout_ref)
    gup_ref[...] = jnp.zeros_like(gup_ref)
    gdown_ref[...] = jnp.zeros_like(gdown_ref)
    gvec_ref[...] = jnp.zeros_like(gvec_ref)

    g1, b1, g2, b2, bd = [ref[...] for ref in refs["vec"]]

    def seg_bias(seq):
        row = seg_ref[pl.ds(seq, 1), :]
        lane = iota((length, PACK), 1) % length
        key = iota((length, PACK), 0)
        first = jnp.broadcast_to(row[:, :128], (length, 128))
        pick = iota((length, 128), 0) == iota((length, 128), 1)
        column = jnp.sum(jnp.where(pick, first, 0.0), axis=1, keepdims=True)
        return jnp.where((column == row) & (key <= lane), 0.0, -1e30)

    hooks["start"]()

    @pl.loop(0, tiles)
    def phase_zero(t):
        hooks["lat_ready"](t)
        r0 = pl.multiple_of(t * tile, tile)
        tok_s[pl.ds(r0, tile), :] = dot(make_hot(t), stem_ref[...]).astype(BFLOAT)
        hooks["stem_done"](t)

    @pl.loop(0, packs)
    def phase_one(turn):
        pack = lax.rem(turn + refs["own"], packs)

        @pl.loop(0, tiles)
        def each(t):
            r0 = pl.multiple_of(t * tile, tile)
            here = pl.ds(r0, tile)
            xhat, _ = norm_stats(tok_s[here, :].astype(FLOAT))
            normed = (xhat * g1 + b1).astype(BFLOAT)
            col0 = pl.multiple_of(pack * PACK, PACK)
            cols = [pl.ds(pl.multiple_of(part * width + pack * PACK, PACK), PACK) for part in range(3)]
            for part in range(3):
                value = dot(normed, wqkv_ref[:, cols[part]])
                if part == 0:
                    value = value.astype(BFLOAT).astype(FLOAT) * 0.125
                qkv_s[here, cols[part]] = value.astype(BFLOAT)

            @pl.loop(0, tile // SUB)
            def attend(sub):
                units, bias = [], []
                for seq in range(SUB // length):
                    s0 = pl.multiple_of(r0 + sub * SUB + seq * length, length)
                    units.append(pl.ds(s0, length))
                    bias.append(seg_bias(t * (tile // length) + sub * (SUB // length) + seq))
                qs = [block_diag(qkv_s[rs, cols[0]]) for rs in units]
                ks = [qkv_s[rs, cols[1]] for rs in units]
                scores = [dot_t(k, q) + b for q, k, b in zip(qs, ks, bias)]
                es = [jnp.exp(x - jnp.max(x, axis=0, keepdims=True)) for x in scores]
                ps = [(e * (1.0 / jnp.sum(e, axis=0, keepdims=True))).astype(BFLOAT) for e in es]
                vs = [qkv_s[rs, cols[2]] for rs in units]
                ms = [diag_rows(t_dot(p, v)).astype(BFLOAT) for p, v in zip(ps, vs)]
                for p, m, rs in zip(ps, ms, units):
                    prob_s[rs, pl.ds(col0, PACK)] = p
                    mix_s[rs, pl.ds(col0, PACK)] = m

            hooks["attend_done"](turn, t)

    hooks["forward_done"]()

    @pl.loop(0, tiles)
    def phase_two(t):
        r0 = pl.multiple_of(t * tile, tile)
        here = pl.ds(r0, tile)
        resid = tok_s[here, :].astype(FLOAT) + dot(mix_s[here, :], wout_ref[...])
        xhat, scale = norm_stats(resid)
        n2_s[...] = (xhat * g2 + b2).astype(BFLOAT)
        hooks["cot_ready"](t)
        cotp_s[...] = from_frames(cot_ref, t)
        acc_s[...] = resid + bd
        dn_s[...] = jnp.zeros_like(dn_s)

        @pl.loop(0, ff // FFB)
        def feed(turn):
            hooks["feed_block"](t, turn)
            blocks = ff // FFB
            f = lax.rem(turn + refs["own"] * (blocks // 2), blocks)
            f0 = pl.multiple_of(f * FFB, FFB)
            fs = pl.ds(f0, FFB)
            n2 = n2_s[...]
            cot = cotp_s[...]
            up = wup_ref[:, fs]
            down = wdown_ref[fs, :]
            pre = dot(n2, up) + upb_ref[0:1, fs]
            square = pre * pre
            tanh = jnp.tanh(GELU_C * pre * (1.0 + GELU_A * square))
            half = 0.5 * (1.0 + tanh)
            hidden = (pre * half).astype(BFLOAT)
            slope = half + (0.5 * GELU_C) * pre * (1.0 - tanh * tanh) * (1.0 + 3.0 * GELU_A * square)
            acc_s[...] += dot(hidden, down)
            gdown_ref[fs, :] += t_dot(hidden, cot)
            d_pre = (dot_t(cot, down) * slope).astype(BFLOAT)
            sums = col_sum(d_pre.astype(FLOAT))
            for part in range(FFB // width):
                row = pl.multiple_of((f * (FFB // width) + part) * 16, 16)
                gvec_ref[pl.ds(row, 1), :] += sums[:, part * width : (part + 1) * width]
            gup_ref[:, fs] += t_dot(n2, d_pre)
            dn_s[...] += dot_t(d_pre, up)

        cot_f = cotp_s[...].astype(FLOAT)
        gvec_add(5, col_sum(cot_f))
        to_frames(out_ref, t, acc_s[...].astype(BFLOAT))
        hooks["out_ready"](t)
        resid = tok_s[here, :].astype(FLOAT) + dot(mix_s[here, :], wout_ref[...])
        xhat, scale = norm_stats(resid)
        dn = dn_s[...]
        gvec_add(3, col_sum(dn * xhat))
        gvec_add(4, col_sum(dn))
        d_branch = (cot_f + norm_back(dn, xhat, scale, g2)).astype(BFLOAT)
        dbr_s[here, :] = d_branch
        gout_ref[...] += t_dot(mix_s[here, :], d_branch)
        mix_s[here, :] = dot_t(d_branch, wout_ref[...]).astype(BFLOAT)

    hooks["feed_done"]()

    @pl.loop(0, tiles)
    def phase_three(t):
        r0 = pl.multiple_of(t * tile, tile)
        here = pl.ds(r0, tile)

        @pl.loop(0, tile // 256)
        def attend(sub):
            for seq0 in range(0, 256 // length, UNIT):
                units = []
                for seq in range(seq0, seq0 + UNIT):
                    s0 = pl.multiple_of(r0 + sub * 256 + seq * length, length)
                    units += [(pl.ds(s0, length), pack * PACK) for pack in range(packs)]
                gs = [block_diag(mix_s[rs, c0 : c0 + PACK]) for rs, c0 in units]
                vs = [qkv_s[rs, 2 * width + c0 : 2 * width + c0 + PACK] for rs, c0 in units]
                dps = [dot_t(v, g).astype(BFLOAT).astype(FLOAT) for v, g in zip(vs, gs)]
                lows = [prob_s[rs, c0 : c0 + PACK] for rs, c0 in units]
                ws = [low.astype(FLOAT) * dp for low, dp in zip(lows, dps)]
                dss = [
                    (w - low.astype(FLOAT) * jnp.sum(w, axis=0, keepdims=True)).astype(BFLOAT)
                    for w, low in zip(ws, lows)
                ]
                dvs = [dot(low, g).astype(BFLOAT) for low, g in zip(lows, gs)]
                ks = [qkv_s[rs, width + c0 : width + c0 + PACK] for rs, c0 in units]
                qs = [block_diag(qkv_s[rs, c0 : c0 + PACK]) for rs, c0 in units]
                dks = [dot(ds, q).astype(BFLOAT) for ds, q in zip(dss, qs)]
                dqs = [(0.125 * diag_rows(t_dot(ds, k))).astype(BFLOAT) for ds, k in zip(dss, ks)]
                for dq, dk, dv, (rs, c0) in zip(dqs, dks, dvs, units):
                    qkv_s[rs, c0 : c0 + PACK] = dq
                    qkv_s[rs, width + c0 : width + c0 + PACK] = dk
                    qkv_s[rs, 2 * width + c0 : 2 * width + c0 + PACK] = dv

        hooks["attend_back_done"](t)
        xhat, scale = norm_stats(tok_s[here, :].astype(FLOAT))
        normed = (xhat * g1 + b1).astype(BFLOAT)
        for part in range(3):
            cols = slice(part * width, (part + 1) * width)
            gqkv_ref[:, cols] += t_dot(normed, qkv_s[here, cols])
        dn = dot_t(qkv_s[here, :], wqkv_ref[...])
        gvec_add(1, col_sum(dn * xhat))
        gvec_add(2, col_sum(dn))
        token_grad = (dbr_s[here, :].astype(FLOAT) + norm_back(dn, xhat, scale, g1)).astype(BFLOAT)
        hooks["tg_room"](t)
        to_frames(tg_ref, t, token_grad)
        hooks["tg_ready"](t)
        gstem_ref[...] += t_dot(make_hot(t), token_grad)
        hooks["tile_done"](t)


def no_tile_hook(t):
    return None


def no_pair_hook(a, b):
    return None


def no_hook():
    return None


NO_HOOKS = {
    "lat_ready": no_tile_hook,
    "stem_done": no_tile_hook,
    "attend_done": no_pair_hook,
    "feed_block": no_pair_hook,
    "attend_back_done": no_tile_hook,
    "cot_ready": no_tile_hook,
    "out_ready": no_tile_hook,
    "tg_room": no_tile_hook,
    "tg_ready": no_tile_hook,
    "tile_done": no_tile_hook,
    "start": no_hook,
    "forward_done": no_hook,
    "feed_done": no_hook,
}


def work_shapes(rows, width, tile):
    return [
        pltpu.VMEM((rows, width), BFLOAT),
        pltpu.VMEM((rows, 3 * width), BFLOAT),
        pltpu.VMEM((rows, width), BFLOAT),
        pltpu.VMEM((rows, width), BFLOAT),
        pltpu.VMEM((rows, width), BFLOAT),
        pltpu.VMEM((tile, width), FLOAT),
        pltpu.VMEM((tile, width), FLOAT),
        pltpu.VMEM((tile, width), BFLOAT),
        pltpu.VMEM((tile, width), BFLOAT),
    ]


def local_kernel(local_len, *refs):
    block_compute(
        local_len,
        {"in": refs[:9], "vec": refs[9:14], "stage": refs[14:16], "grads": refs[16:22], "work": refs[22:], "own": 0, "pairs": 1},
        NO_HOOKS,
    )


def run_local(local_len, lat, seg, cot, stem, wqkv, wout, wup, wdown, upb, *vec):
    places, per, width = cot.shape
    group_rows = 16 // local_len * (places * local_len)
    shape = jax.ShapeDtypeStruct
    vm = pl.BlockSpec(memory_space=pltpu.VMEM)
    return pl.pallas_call(
        functools.partial(local_kernel, local_len),
        out_shape=(
            shape(cot.shape, BFLOAT),
            shape(cot.shape, BFLOAT),
            shape(stem.shape, FLOAT),
            shape(wqkv.shape, FLOAT),
            shape(wout.shape, FLOAT),
            shape(wup.shape, FLOAT),
            shape(wdown.shape, FLOAT),
            shape((wup.shape[1] // width * 16, width), FLOAT),
        ),
        in_specs=[vm] * 14,
        out_specs=[vm] * 8,
        scratch_shapes=work_shapes(places * per, width, max(TILE, group_rows)),
        compiler_params=pltpu.CompilerParams(vmem_limit_bytes=60 * 1024 * 1024),
    )(lat, seg, cot, stem, wqkv, wout, wup, wdown, upb, *vec)


def wait_for(ref, sem):
    pltpu.make_async_copy(ref, ref, sem).wait()


Y_FIRST = (False, False, True, False)
DOWN, UP, STEM, QUERY = range(4)
EARLY = ((0, DOWN, 1), (1, UP, 1), (2, DOWN, 2))
ORDER = (
    (STEM, 1),
    (QUERY, 1),
    (DOWN, 3),
    (UP, 2),
    (STEM, 2),
    (QUERY, 2),
    (DOWN, 4),
    (STEM, 3),
    (UP, 3),
    (STEM, 4),
    (QUERY, 3),
    (UP, 4),
    (QUERY, 4),
    (DOWN, 5),
    (STEM, 5),
    (DOWN, 6),
    (STEM, 6),
    (UP, 5),
    (DOWN, 7),
    (QUERY, 5),
    (UP, 6),
    (STEM, 7),
    (QUERY, 6),
    (UP, 7),
    (STEM, 8),
    (QUERY, 7),
)


class Reducer:
    def __init__(self, where, pieces, bufs, final, sems, y_first):
        self.i, self.j = where
        self.pieces = pieces
        self.send, self.r1, self.r2, self.r3, self.r4, self.r5, self.fin, self.own = bufs
        self.final = final
        self.ssem, self.rsem = sems
        self.half = self.send.shape[1]
        self.core = self.bit(0)
        self.y_first = y_first
        self.across = (self.i, 1 - self.j)
        count = self.half // 2
        start = self.bit(1) * count
        self.y_rows = pl.ds(pl.multiple_of(start, 16), count)
        self.y_other = pl.ds(pl.multiple_of(count - start, 16), count)
        count = count // 2
        self.z_rows = pl.ds(pl.multiple_of(start + self.bit(2) * count, 16), count)
        self.z_other = pl.ds(pl.multiple_of(start + (1 - self.bit(2)) * count, 16), count)
        if y_first:
            self.zbuf = [self.send.at[self.j, pl.ds(pl.multiple_of(start + n * count, 16), count), :] for n in range(2)]
        else:
            self.zbuf = [self.send.at[1, (2 + n) * count : (3 + n) * count, :] for n in range(2)]

    def bit(self, n):
        return lax.rem(self.i // (1 << n), 2)

    def near(self, bit):
        step = 1 << bit
        return (self.i + step - 2 * step * self.bit(bit), self.j)

    def copy(self, n, src, dst, device):
        return pltpu.make_async_remote_copy(
            src_ref=src,
            dst_ref=dst,
            send_sem=self.ssem.at[n],
            recv_sem=self.rsem.at[n],
            device_id=device,
            device_id_type=pl.DeviceIdType.MESH,
        )

    def core_copy(self):
        return self.copy(0, self.send, self.r1, self.near(0))

    def first_copy(self):
        if self.y_first:
            return self.copy(1, self.send.at[:, self.y_other, :], self.r2, self.near(1))
        return self.copy(1, self.send.at[0], self.r2, self.across)

    def second_copy(self):
        if self.y_first:
            return self.copy(2, self.send.at[1 - self.j, self.y_rows, :], self.r3, self.across)
        return self.copy(2, self.send.at[1, 0 : self.half // 2, :], self.r3, self.near(1))

    def start_core(self):
        for h in range(2):
            for at, take in self.pieces(h, 1 - self.core):
                self.send[h, at[0], at[1]] = take().astype(BFLOAT)
        self.core_copy().start()

    def core_to_first(self):
        self.core_copy().wait()
        if self.y_first:
            for h in range(2):
                for at, take in self.pieces(h, self.core):
                    arrived = self.r1[h, at[0], at[1]].astype(FLOAT)
                    self.send[h, at[0], at[1]] = (take() + arrived).astype(BFLOAT)
            self.first_copy().start()
            return
        for at, take in self.pieces(1 - self.j, self.core):
            arrived = self.r1[1 - self.j, at[0], at[1]].astype(FLOAT)
            self.send[0, at[0], at[1]] = (take() + arrived).astype(BFLOAT)
        self.first_copy().start()
        for at, take in self.pieces(self.j, self.core):
            self.own[at[0], at[1]] = take() + self.r1[self.j, at[0], at[1]].astype(FLOAT)

    def first_to_second(self):
        self.first_copy().wait()
        if self.y_first:
            far = self.send[1 - self.j, self.y_rows, :].astype(FLOAT) + self.r2[1 - self.j].astype(FLOAT)
            self.send[1 - self.j, self.y_rows, :] = far.astype(BFLOAT)
            self.second_copy().start()
            near = self.send[self.j, self.y_rows, :].astype(FLOAT) + self.r2[self.j].astype(FLOAT)
            self.own[self.y_rows, :] = near
            return
        far = self.own[self.y_other, :] + self.r2[self.y_other, :].astype(FLOAT)
        self.send[1, 0 : self.half // 2, :] = far.astype(BFLOAT)
        self.second_copy().start()
        self.own[self.y_rows, :] += self.r2[self.y_rows, :].astype(FLOAT)

    def third_copy(self):
        return self.copy(3, self.zbuf[0], self.r4, self.near(2))

    def fourth_copy(self):
        return self.copy(4, self.zbuf[1], self.r5, self.near(3))

    def second_to_third(self):
        self.second_copy().wait()
        self.own[self.y_rows, :] += self.r3[...].astype(FLOAT)
        self.zbuf[0][...] = self.own[self.z_other, :].astype(BFLOAT)
        self.third_copy().start()

    def third_to_fourth(self):
        self.third_copy().wait()
        total = self.own[self.z_rows, :] + self.r4[...].astype(FLOAT)
        self.zbuf[1][...] = total.astype(BFLOAT)
        self.fourth_copy().start()

    def keep_copy(self):
        return pltpu.make_async_copy(self.fin, self.final.at[self.core, self.z_rows, :], self.ssem.at[8])

    def z_gather(self):
        return self.copy(5, self.fin, self.final.at[self.core, self.z_rows, :], self.near(2))

    def y_gather(self):
        place = self.final.at[self.core, self.y_rows, :]
        return self.copy(6, place, place, self.near(1))

    def core_gather(self):
        place = self.final.at[self.core]
        return self.copy(7, place, place, self.near(0))

    def fourth_done(self):
        self.fourth_copy().wait()
        self.fin[...] = (self.zbuf[1][...].astype(FLOAT) + self.r5[...].astype(FLOAT)).astype(BFLOAT)
        self.keep_copy().start()
        self.z_gather().start()

    def z_to_y(self):
        self.keep_copy().wait()
        self.z_gather().wait()
        self.y_gather().start()

    def y_done(self):
        self.y_gather().wait()

    def step(self, n):
        (
            self.start_core,
            self.core_to_first,
            self.first_to_second,
            self.second_to_third,
            self.third_to_fourth,
            self.fourth_done,
            self.z_to_y,
            self.y_done,
        )[n]()


def wide_kernel(local_len, *refs):
    (
        lat_hbm, seg_ref, cot_hbm, stem_hbm, extra_hbm,
        wq_hbm, wk_hbm, wv_hbm, wo_hbm, wup_hbm, wdown_hbm, upb_hbm,
    ) = refs[:12]
    vec = refs[12:17]
    out_hbm, tg_hbm, down_hbm, up_hbm, query_hbm, shared_hbm = refs[17:23]
    (
        lat_s, frame_s, stem_s, wqkv_s, wout_s, wup_s, wdown_s, upb_s,
        gstem_s, gqkv_s, gout_s, gup_s, gdown_s, gvec_s,
    ) = refs[23:37]
    work = refs[37:44]
    own_s = refs[44]
    group_bufs = [refs[45 + 7 * n : 52 + 7 * n] for n in range(4)]
    sizes = [bufs[0].shape[1] for bufs in group_bufs]
    owns = (
        own_s.at[0 : sizes[0], :],
        own_s.at[sizes[0] : sizes[0] + sizes[1], :],
        gdown_s.at[0 : sizes[2], :],
        gdown_s.at[sizes[2] : sizes[2] + sizes[3], :],
    )
    tile = work[5].shape[0]
    work = work[:5] + (own_s.at[0:tile, :], own_s.at[tile : 2 * tile, :]) + work[5:]
    (
        lat_send, lat_recv, cot_send, cot_recv, own_sem, out_send, out_recv, tg_send, tg_recv,
        w_local, wx_send, wx_recv, wc_send, wc_recv, sh_send, sh_recv,
    ) = refs[73:89]
    group_sems = [refs[89 + 2 * n : 91 + 2 * n] for n in range(4)]
    i, j = lax.axis_index("gx"), lax.axis_index("gy")
    places = lax.axis_size("gx")
    core = lax.rem(i, 2)
    sibling = (i + 1 - 2 * core, j)
    ybit = lax.rem(i // 2, 2)
    beside = (i + 2 - 4 * ybit, j)
    across = (i, 1 - j)
    tiles = work[0].shape[0] // tile
    width = work[0].shape[1]
    mesh_id = pl.DeviceIdType.MESH

    def remote(src, dst, send, recv, device):
        return pltpu.make_async_remote_copy(
            src_ref=src, dst_ref=dst, send_sem=send, recv_sem=recv, device_id=device, device_id_type=mesh_id
        )

    barrier = pltpu.get_barrier_semaphore()

    @pl.loop(1, places)
    def greet(k):
        pl.semaphore_signal(barrier, inc=1, device_id=(lax.rem(i + k, places), j), device_id_type=mesh_id)

    pl.semaphore_signal(barrier, inc=1, device_id=across, device_id_type=mesh_id)
    pl.semaphore_wait(barrier, places)

    def part(ref, t):
        count = ref.shape[1] // tiles
        return pl.ds(pl.multiple_of(t * count, count), count)

    def scatter(src, dst, t, send, recv):
        @pl.loop(1, places)
        def each(k):
            d = lax.rem(i + k, places)
            remote(src.at[d, part(src, t), :], dst.at[i, part(src, t), :], send, recv, (d, j)).start()

    def keep(src, dst, t, sem):
        return pltpu.make_async_copy(src.at[i, part(src, t), :], dst.at[i, part(src, t), :], sem)

    def most(ref, t):
        return ref.at[0 : places - 1, part(ref, t), :]

    half = wq_hbm.shape[1]

    ff_half = upb_hbm.shape[1]
    blocks = ff_half // FFB

    def weight_views(owner, whole):
        def rows_of(count):
            return (0, count) if whole else (pl.multiple_of(core * (count // 2), 16), count // 2)

        start, size = rows_of(width)
        r = pl.ds(start, size)
        views = []
        for n, src in enumerate((wq_hbm, wk_hbm, wv_hbm)):
            at = pl.ds(pl.multiple_of(n * width + owner * half, half), half)
            views.append((src.at[r, :], wqkv_s.at[r, at]))
        count = wo_hbm.shape[0]
        start, size = rows_of(count)
        there = pl.ds(pl.multiple_of(owner * count + start, 16), size)
        views.append((wo_hbm.at[pl.ds(start, size), :], wout_s.at[there, :]))
        start, size = rows_of(FFB)
        for block in range(blocks):
            at = pl.ds(pl.multiple_of(owner * ff_half + block * FFB, 128), FFB)
            views.append((wup_hbm.at[r, block * FFB : (block + 1) * FFB], wup_s.at[r, at]))
            here = pl.ds(pl.multiple_of(block * FFB + start, 16), size)
            there = pl.ds(pl.multiple_of(owner * ff_half + block * FFB + start, 16), size)
            views.append((wdown_hbm.at[here, :], wdown_s.at[there, :]))
        return views

    here_views = weight_views(j, True)
    x_copies = [
        remote(src, dst, wx_send.at[n], wx_recv.at[n], across)
        for n, (src, dst) in enumerate(weight_views(j, False))
    ]
    c_copies = [
        remote(dst, dst, wc_send.at[n], wc_recv.at[n], sibling)
        for n, (_, dst) in enumerate(weight_views(1 - j, False))
    ]
    own_copies = [pltpu.make_async_copy(src, dst, w_local.at[n]) for n, (src, dst) in enumerate(here_views)]
    n_weights = len(x_copies)
    upb_at = pl.ds(pl.multiple_of(j * ff_half, 128), ff_half)
    upb_x = remote(upb_hbm, upb_s.at[:, upb_at], wx_send.at[n_weights], wx_recv.at[n_weights], across)
    upb_own = pltpu.make_async_copy(upb_hbm, upb_s.at[:, upb_at], w_local.at[n_weights])

    for n in range(4):
        x_copies[n].start()

    @pl.loop(0, tiles)
    def send_lat(t):
        keep(lat_hbm, lat_s, t, own_sem.at[t]).start()
        scatter(lat_hbm, lat_s, t, lat_send, lat_recv.at[t])

    stem_rows_in = stem_hbm.shape[0]
    stem_copies = [
        pltpu.make_async_copy(stem_hbm, stem_s.at[0:stem_rows_in, :], w_local.at[n_weights + 1]),
        pltpu.make_async_copy(extra_hbm, stem_s.at[stem_rows_in:, :], w_local.at[n_weights + 2]),
    ]
    for copy in stem_copies:
        copy.start()
    for n in range(4, n_weights):
        x_copies[n].start()
    for copy in own_copies:
        copy.start()
    upb_x.start()
    upb_own.start()

    @pl.loop(0, tiles)
    def send_cot(t):
        keep(cot_hbm, frame_s, t, own_sem.at[tiles + t]).start()
        scatter(cot_hbm, frame_s, t, cot_send, cot_recv.at[t])

    def move(first, last, before, after):
        for n in range(first, last):
            before[n].wait()
            if after is not None:
                after[n].start()

    last_tile = tiles - 1
    middle = min(1, last_tile)

    hooks = dict(NO_HOOKS)

    def lat_ready(t):
        keep(lat_hbm, lat_s, t, own_sem.at[t]).wait()
        wait_for(most(lat_s, t), lat_recv.at[t])

        @pl.when(t == 0)
        def _():
            for copy in stem_copies:
                copy.wait()

    def stem_done(t):
        @pl.when(t == last_tile)
        def _():
            move(0, 4, own_copies, None)

    def attend_done(turn, t):
        @pl.when((turn == 0) & (t == middle))
        def _():
            move(0, 4, x_copies, c_copies)

        @pl.when((turn == 0) & (t == last_tile))
        def _():
            move(0, 4, c_copies, None)

        @pl.when((turn == 1) & (t == last_tile))
        def _():
            move(4, 6, x_copies, c_copies)

    def forward_done():
        upb_x.wait()
        upb_own.wait()
        move(4, n_weights, own_copies, None)

    def feed_block(t, turn):
        for block in range(blocks):

            @pl.when((t == 0) & (turn == blocks + block))
            def _():
                first = 4 + 2 * block
                if block > 0:
                    move(first, first + 2, x_copies, c_copies)
                move(first, first + 2, c_copies, None)

    def cot_ready(t):
        keep(cot_hbm, frame_s, t, own_sem.at[tiles + t]).wait()
        wait_for(most(frame_s, t), cot_recv.at[t])

    def out_ready(t):
        keep(frame_s, out_hbm, t, own_sem.at[2 * tiles + t]).start()
        scatter(frame_s, out_hbm, t, out_send.at[t], out_recv)

    def tg_room(t):
        keep(frame_s, out_hbm, t, own_sem.at[2 * tiles + t]).wait()
        wait_for(most(frame_s, t), out_send.at[t])

    def tg_ready(t):
        keep(frame_s, tg_hbm, t, own_sem.at[3 * tiles + t]).start()
        scatter(frame_s, tg_hbm, t, tg_send.at[t], tg_recv)

    def grab(ref, r0, nrows, c0, ncols):
        return lambda: ref[pl.ds(r0, nrows), pl.ds(c0, ncols)]

    def mult(value, by):
        return pl.multiple_of(value, by)

    up_half = gup_s.shape[1] // 2
    up_rows = width // 2
    down_rows = gdown_s.shape[0] // 4
    out_rows = gout_s.shape[0] // 4
    stem_rows = gstem_s.shape[0] // 4

    qrows = width // 2

    def down_pieces(h, c):
        return [((slice(None), slice(None)), grab(gdown_s, mult((h * 2 + c) * down_rows, 16), down_rows, 0, width))]

    def up_pieces(h, c):
        found, base = [], 0
        for block in range(up_half // width):
            found.append(
                (
                    (slice(base, base + up_rows), slice(None)),
                    grab(gup_s, mult(c * up_rows, 16), up_rows, mult(h * up_half + block * width, 128), width),
                )
            )
            base += up_rows
        found.append(
            (
                (slice(base, base + out_rows), slice(None)),
                grab(gout_s, mult((h * 2 + c) * out_rows, 16), out_rows, 0, width),
            )
        )
        return found

    def stem_pieces(h, c):
        found = [
            (
                (slice(0, stem_rows), slice(None)),
                grab(gstem_s, mult((h * 2 + c) * stem_rows, 16), stem_rows, 0, width),
            ),
            (
                (slice(stem_rows, stem_rows + 16), slice(None)),
                grab(gvec_s, mult((h * 2 + c) * 16, 16), 16, 0, width),
            ),
        ]
        base, end = stem_rows + 16, sizes[2]
        if end > base:
            found.append(((slice(base, end), slice(None)), lambda: jnp.zeros((end - base, width), FLOAT)))
        return found

    def query_pieces(h, c):
        found = [
            (
                (slice(0, qrows), slice(n * half, (n + 1) * half)),
                grab(gqkv_s, mult(c * qrows, 16), qrows, mult(n * width + h * half, 128), half),
            )
            for n in range(2)
        ]
        for n in range(2):
            found.append(
                (
                    (slice(qrows, qrows + qrows // 2), slice(n * half, (n + 1) * half)),
                    grab(gqkv_s, mult(c * qrows + n * (qrows // 2), 16), qrows // 2, mult(2 * width + h * half, 128), half),
                )
            )
        return found

    where = (i, j)
    down, up, stem, query = [
        Reducer(where, pieces, bufs + (own,), final, sems, y_first)
        for pieces, bufs, own, final, sems, y_first in zip(
            (down_pieces, up_pieces, stem_pieces, query_pieces),
            group_bufs,
            owns,
            (down_hbm, up_hbm, shared_hbm.at[j], query_hbm),
            group_sems,
            Y_FIRST,
        )
    ]

    def feed_done():
        down.start_core()
        up.start_core()

    def attend_back_done(t):
        for at, group, n in EARLY:

            @pl.when(t == min(at, last_tile))
            def _():
                (down, up)[group].step(n)

    hooks.update(
        lat_ready=lat_ready,
        stem_done=stem_done,
        attend_done=attend_done,
        feed_block=feed_block,
        attend_back_done=attend_back_done,
        forward_done=forward_done,
        cot_ready=cot_ready,
        out_ready=out_ready,
        tg_room=tg_room,
        tg_ready=tg_ready,
        feed_done=feed_done,
    )
    block_compute(
        local_len,
        {
            "in": (lat_s, seg_ref, frame_s, stem_s, wqkv_s, wout_s, wup_s, wdown_s, upb_s),
            "vec": vec,
            "own": j,
            "pairs": frame_s.shape[1] // lat_s.shape[1],
            "stage": (frame_s, frame_s),
            "grads": (gstem_s, gqkv_s, gout_s, gup_s, gdown_s, gvec_s),
            "work": work,
        },
        hooks,
    )
    stem.start_core()
    query.start_core()
    to_x = remote(shared_hbm.at[j, core], shared_hbm.at[j, core], sh_send.at[0], sh_recv.at[0], across)
    to_core = remote(shared_hbm.at[:, core], shared_hbm.at[:, core], sh_send.at[1], sh_recv.at[1], sibling)
    for g, n in ORDER:
        group = (down, up, stem, query)[g]
        if n == 8 and g == STEM:
            to_x.wait()
            to_core.start()
            continue
        group.step(n)
        if n == 7:
            (to_x if g == STEM else group.core_gather()).start()
    for group in (down, up, query):
        group.core_gather().wait()
    to_core.wait()
    wait_for(lat_hbm.at[0 : places - 1], lat_send)
    wait_for(cot_hbm.at[0 : places - 1], cot_send)
    wait_for(out_hbm.at[0 : places - 1], out_recv)
    wait_for(tg_hbm.at[0 : places - 1], tg_recv)

    @pl.loop(0, tiles)
    def drain(t):
        keep(frame_s, tg_hbm, t, own_sem.at[3 * tiles + t]).wait()
        wait_for(most(frame_s, t), tg_send.at[t])


def reduce_shapes(half, width, y_first):
    return [
        pltpu.VMEM((2, half, width), BFLOAT),
        pltpu.VMEM((2, half, width), BFLOAT),
        pltpu.VMEM((2, half // 2, width) if y_first else (half, width), BFLOAT),
        pltpu.VMEM((half // 2, width), BFLOAT),
        pltpu.VMEM((half // 4, width), BFLOAT),
        pltpu.VMEM((half // 4, width), BFLOAT),
        pltpu.VMEM((half // 4, width), BFLOAT),
    ]


def run_wide(local_len, lat, seg, cot, stem, extra, wq, wk, wv, wo, wup, wdown, upb, *vec):
    places, per, width = cot.shape
    rows = places * per
    ff = 2 * wup.shape[1]
    hot_width = stem.shape[0] + extra.shape[0]
    shape = jax.ShapeDtypeStruct
    vm = pl.BlockSpec(memory_space=pltpu.VMEM)
    hbm = pl.BlockSpec(memory_space=pl.ANY)
    stem_used = hot_width // 4 + 16
    sizes = (
        ff // 4,
        (width // 2) * (wup.shape[1] // width) + width // 4,
        -(-stem_used // 64) * 64,
        width // 2 + width // 4,
    )
    tiles = rows // TILE
    n_weights = 4 + 2 * (wup.shape[1] // FFB)
    dma = pltpu.SemaphoreType.DMA
    scratch = [
        pltpu.VMEM(lat.shape, BFLOAT),
        pltpu.VMEM(cot.shape, BFLOAT),
        pltpu.VMEM((hot_width, width), BFLOAT),
        pltpu.VMEM((width, 3 * width), BFLOAT),
        pltpu.VMEM((width, width), BFLOAT),
        pltpu.VMEM((width, ff), BFLOAT),
        pltpu.VMEM((ff, width), BFLOAT),
        pltpu.VMEM((1, ff), FLOAT),
        pltpu.VMEM((hot_width, width), FLOAT),
        pltpu.VMEM((width, 3 * width), FLOAT),
        pltpu.VMEM((width, width), FLOAT),
        pltpu.VMEM((width, ff), FLOAT),
        pltpu.VMEM((ff, width), FLOAT),
        pltpu.VMEM((ff // width * 16, width), FLOAT),
    ]
    scratch += [item for n, item in enumerate(work_shapes(rows, width, TILE)) if n not in (5, 6)]
    scratch += [pltpu.VMEM((sizes[0] + sizes[1], width), FLOAT)]
    for size, y_first in zip(sizes, Y_FIRST):
        scratch += reduce_shapes(size, width, y_first)
    scratch += [
        dma,
        dma((tiles,)),
        dma,
        dma((tiles,)),
        dma((4 * tiles,)),
        dma((tiles,)),
        dma,
        dma((tiles,)),
        dma,
        dma((n_weights + 3,)),
        dma((n_weights + 1,)),
        dma((n_weights + 1,)),
        dma((n_weights,)),
        dma((n_weights,)),
        dma((2,)),
        dma((2,)),
    ]
    scratch += [dma((9,))] * 8
    return pl.pallas_call(
        functools.partial(wide_kernel, local_len),
        out_shape=(shape(cot.shape, BFLOAT), shape(cot.shape, BFLOAT))
        + tuple(shape((2, sizes[n], width), BFLOAT) for n in (0, 1, 3))
        + (shape((2, 2, sizes[2], width), BFLOAT),),
        in_specs=[hbm, vm] + [hbm] * 10 + [vm] * 5,
        out_specs=[hbm] * 6,
        scratch_shapes=scratch,
        compiler_params=pltpu.CompilerParams(
            vmem_limit_bytes=VMEM_LIMIT, collective_id=0, has_side_effects=True
        ),
    )(lat, seg, cot, stem, extra, wq, wk, wv, wo, wup, wdown, upb, *vec)


def per_device(
    latents,
    actions,
    segment_ids,
    cotangent,
    stem_weight,
    action_table,
    first_gain,
    first_bias,
    query_weight,
    key_weight,
    value_weight,
    out_weight,
    second_gain,
    second_bias,
    up_weight,
    up_bias,
    down_weight,
    down_bias,
):
    half_seqs, local_len, groups = latents.shape
    width = stem_weight.shape[1]
    places = lax.axis_size("gx")
    length = places * local_len
    seqs = half_seqs // places
    rows = seqs * length
    actions_n = action_table.shape[0]

    lat = jnp.concatenate([latents, actions[..., None]], axis=-1).astype(BFLOAT)
    lat = lat.reshape(places, seqs, local_len, groups + 1)
    cot = cotangent.reshape(places, seqs * local_len, width)
    first_seq = (lax.axis_index("gy") * places + lax.axis_index("gx")) * seqs
    seg = lax.dynamic_slice_in_dim(segment_ids, first_seq, seqs, 0)
    seg = jnp.tile(seg.astype(FLOAT), (1, PACK // length))
    extra = jnp.pad(action_table, ((0, HOT_PAD - actions_n), (0, 0)))
    vec = [item[None] for item in (first_gain, first_bias, second_gain, second_bias, down_bias)]
    if rows % TILE == 0 and rows <= MAX_ROWS and places == 16:
        lat = jnp.pad(lat, ((0, 0), (0, 0), (0, 0), (0, 64 - groups - 1)))
        lat = lat.reshape(places, seqs * local_len // 2, 128)
        out, tg, gdown, up, query, shared = run_wide(
            local_len, lat, seg, cot, stem_weight, extra, query_weight, key_weight, value_weight,
            out_weight, up_weight, down_weight, up_bias[None], *vec,
        )
        out = out.reshape(half_seqs, local_len, width)
        tg = tg.reshape(half_seqs, local_len, width)
        half = width // 2
        cols = query_weight.shape[1]
        blocks = up_weight.shape[1] // width
        gdown = gdown.astype(FLOAT).reshape(down_weight.shape)
        gup = jnp.concatenate([up[:, b * half : (b + 1) * half] for b in range(blocks)], axis=2)
        gup = gup.astype(FLOAT).reshape(up_weight.shape)
        gout = up[:, blocks * half :].astype(FLOAT).reshape(out_weight.shape)
        query = query.astype(FLOAT)
        gq = query[:, :half, :cols].reshape(width, cols)
        gk = query[:, :half, cols:].reshape(width, cols)
        part = query[:, half:]
        gv = jnp.concatenate([part[:, :, :cols], part[:, :, cols:]], axis=1).reshape(width, cols)
        stem_rows = (stem_weight.shape[0] + HOT_PAD) // 4
        gstem = shared[:, :, :stem_rows].astype(FLOAT).reshape(4 * stem_rows, width)
        first = shared[0, 0, stem_rows : stem_rows + 16].astype(FLOAT)
        upb_grad = lax.dynamic_index_in_dim(shared[:, :, stem_rows], lax.axis_index("gy"), 0, False)
        upb_grad = upb_grad.astype(FLOAT).reshape(up_bias.shape)
        return (
            out,
            tg,
            gstem[: groups * 32],
            gstem[groups * 32 : groups * 32 + actions_n],
            first[1],
            first[2],
            gq,
            gk,
            gv,
            gout,
            first[3],
            first[4],
            gup,
            upb_grad,
            gdown,
            first[5],
        )
    lat = lat.reshape(places, seqs * local_len, groups + 1)
    lat = jnp.pad(lat, ((0, 0), (0, 0), (0, 128 - groups - 1)))
    lat = lax.all_to_all(lat, "gx", split_axis=0, concat_axis=0, tiled=True)
    cot = lax.all_to_all(cot, "gx", split_axis=0, concat_axis=0, tiled=True)
    gather = functools.partial(lax.all_gather, axis_name="gy", tiled=True)
    wqkv = jnp.concatenate(
        [gather(item, axis=1) for item in (query_weight, key_weight, value_weight)], axis=1
    )
    wout = gather(out_weight, axis=0)
    wup = gather(up_weight, axis=1)
    wdown = gather(down_weight, axis=0)
    upb = gather(up_bias, axis=0)[None]
    stem = jnp.concatenate([stem_weight, extra], axis=0)
    out, tg, gstem, gqkv, gout, gup, gdown, gvec = run_local(
        local_len, lat, seg, cot, stem, wqkv, wout, wup, wdown, upb, *vec
    )
    out = lax.all_to_all(out, "gx", split_axis=0, concat_axis=0, tiled=True)
    tg = lax.all_to_all(tg, "gx", split_axis=0, concat_axis=0, tiled=True)
    out = out.reshape(half_seqs, local_len, width)
    tg = tg.reshape(half_seqs, local_len, width)
    both = ("gx", "gy")
    gstem, gvec = lax.psum((gstem, gvec), both)
    upb_grad = gvec[::16].reshape(-1)
    upb_grad = lax.dynamic_slice_in_dim(upb_grad, lax.axis_index("gy") * up_bias.shape[0], up_bias.shape[0])

    def shard(value, dim):
        return lax.psum(lax.psum_scatter(value, "gy", scatter_dimension=dim, tiled=True), "gx")

    gq = shard(gqkv[:, :width], 1)
    gk = shard(gqkv[:, width : 2 * width], 1)
    gv = shard(gqkv[:, 2 * width :], 1)
    return (
        out,
        tg,
        gstem[: groups * 32],
        gstem[groups * 32 : groups * 32 + actions_n],
        gvec[1],
        gvec[2],
        gq,
        gk,
        gv,
        shard(gout, 0),
        gvec[3],
        gvec[4],
        shard(gup, 1),
        upb_grad,
        shard(gdown, 0),
        gvec[5],
    )


def solution(mesh):
    return jax.shard_map(
        per_device,
        mesh=mesh,
        in_specs=(
            P("gy", "gx", None),
            P("gy", "gx"),
            P(),
            P("gy", "gx", None),
            P(),
            P(),
            P(),
            P(),
            P(None, "gy"),
            P(None, "gy"),
            P(None, "gy"),
            P("gy", None),
            P(),
            P(),
            P(None, "gy"),
            P("gy"),
            P("gy", None),
            P(),
        ),
        out_specs=(
            P("gy", "gx", None),
            P("gy", "gx", None),
            P(),
            P(),
            P(),
            P(),
            P(None, "gy"),
            P(None, "gy"),
            P(None, "gy"),
            P("gy", None),
            P(),
            P(),
            P(None, "gy"),
            P("gy"),
            P("gy", None),
            P(),
        ),
        check_vma=False,
    )
```

```python
import functools

import jax
import jax.numpy as jnp
from jax import lax
from jax.experimental import pallas as pl
from jax.experimental.pallas import tpu as pltpu
from jax.sharding import PartitionSpec as P

HD = 64
PACK = 256
EPSILON = 1e-05
FLOAT = jnp.float32
BFLOAT = jnp.bfloat16
TILE = 512
MAX_ROWS = 2048
VMEM_LIMIT = 62 * 1024 * 1024
UNIT = 4
SUB = 512
FFB = 512
HOT_PAD = 128
GELU_C = 0.7978845608028654
GELU_A = 0.044715


def dot(left, right):
    return lax.dot_general(left, right, (((1,), (0,)), ((), ())), preferred_element_type=FLOAT)


def dot_t(left, right):
    return lax.dot_general(left, right, (((1,), (1,)), ((), ())), preferred_element_type=FLOAT)


def t_dot(left, right):
    return lax.dot_general(left, right, (((0,), (0,)), ((), ())), preferred_element_type=FLOAT)


def iota(shape, dim):
    return lax.broadcasted_iota(jnp.int32, shape, dim)


def norm_stats(values):
    average = jnp.mean(values, axis=-1, keepdims=True)
    centred = values - average
    spread = jnp.mean(centred * centred, axis=-1, keepdims=True)
    scale = lax.rsqrt(spread + EPSILON)
    return centred * scale, scale


def norm_back(grad, xhat, scale, gain):
    scaled = grad * gain
    mean_e = jnp.mean(scaled, axis=-1, keepdims=True)
    mean_x = jnp.mean(scaled * xhat, axis=-1, keepdims=True)
    return (scaled - mean_e - xhat * mean_x) * scale


def col_sum(values):
    return jnp.sum(values, axis=0, keepdims=True)


def head_reduce(values, op, fill):
    parts = []
    for half in range(PACK // 128):
        piece = values[:, half * 128 : (half + 1) * 128]
        low = iota(piece.shape, 1) < HD
        first = op(jnp.where(low, piece, fill), axis=-1, keepdims=True)
        second = op(jnp.where(low, fill, piece), axis=-1, keepdims=True)
        parts.append((low, first, second))
    return parts


def head_spread(parts):
    return jnp.concatenate([jnp.where(low, a, b) for low, a, b in parts], axis=1)


def block_diag(rows):
    mask = (iota((PACK, PACK), 0) // HD) == (iota((PACK, PACK), 1) // HD)
    return jnp.where(mask, jnp.concatenate([rows] * (PACK // HD), axis=0), jnp.zeros((), rows.dtype))


def diag_rows(full):
    lane_head = iota((HD, PACK), 1) // HD
    result = full[:HD]
    for head in range(1, PACK // HD):
        result = jnp.where(lane_head == head, full[head * HD : (head + 1) * HD], result)
    return result


def unrolled_loop(count, body):
    if count == 1:
        body(0)
    else:
        pl.loop(0, count)(body)


def row_maps(local_len, length, count, back):
    dest = iota((count, count), 1 if back else 0)
    src = iota((count, count), 0 if back else 1)
    want = ((dest % length) // local_len) * 16 + (dest // length) * local_len + dest % local_len
    return jnp.where(want == src, 1.0, 0.0).astype(BFLOAT)


def block_compute(local_len, refs, hooks):
    lat_ref, seg_ref, cot_ref, stem_ref, wqkv_ref, wout_ref, wup_ref, wdown_ref, upb_ref = refs["in"]
    out_ref, tg_ref = refs["stage"]
    gstem_ref, gqkv_ref, gout_ref, gup_ref, gdown_ref, gvec_ref = refs["grads"]
    tok_s, qkv_s, prob_s, mix_s, dbr_s, acc_s, dn_s, n2_s, cotp_s = refs["work"]
    rows, width = tok_s.shape
    places = cot_ref.shape[0]
    length = places * local_len
    packs = width // PACK
    group_rows = 16 // local_len * length
    tile = acc_s.shape[0]
    tiles = rows // tile
    groups = tile // group_rows
    ff = wup_ref.shape[1]
    hot_width = stem_ref.shape[0]
    classes = (hot_width - HOT_PAD) // 32

    def to_frames(ref, t, values):
        for g in range(groups):
            k0 = pl.multiple_of((t * groups + g) * 16, 16)
            back = dot(
                row_maps(local_len, length, group_rows, True),
                values[g * group_rows : (g + 1) * group_rows, :],
            )
            ref[:, pl.ds(k0, 16), :] = back.astype(BFLOAT).reshape(places, 16, width)

    def from_frames(ref, t):
        parts = []
        for g in range(groups):
            k0 = pl.multiple_of((t * groups + g) * 16, 16)
            raw = ref[:, pl.ds(k0, 16), :].reshape(group_rows, ref.shape[2])
            parts.append(dot(row_maps(local_len, length, group_rows, False), raw).astype(BFLOAT))
        return jnp.concatenate(parts, axis=0) if groups > 1 else parts[0]

    pairs = refs["pairs"]
    lat_rows = tile // places // pairs
    slot = lat_ref.shape[2] // pairs

    def make_hot(t):
        k0 = pl.multiple_of(t * lat_rows, lat_rows)
        raw = lat_ref[:, pl.ds(k0, lat_rows), :].reshape(places * lat_rows, lat_ref.shape[2])
        dest = iota((tile, places * lat_rows), 0)
        src = iota((tile, places * lat_rows), 1)
        frame = dest % local_len
        want = ((dest % length) // local_len) * lat_rows
        want += (dest // length) * (local_len // pairs) + frame // pairs
        lats = dot(jnp.where(want == src, 1.0, 0.0).astype(BFLOAT), raw)
        if pairs > 1:
            turn = iota(lats.shape, 0) % pairs
            lats = jnp.where(iota(lats.shape, 1) // slot == turn, lats, 0.0)
        lats = lats.astype(BFLOAT)
        parts = []
        for block in range(0, hot_width, 128):
            g = iota((lats.shape[1], 128), 0) % slot
            c = iota((lats.shape[1], 128), 1) + block
            spread = jnp.where(jnp.minimum(c // classes, 32) == g, 1.0, 0.0).astype(BFLOAT)
            val = dot(lats, spread)
            lane = iota((tile, 128), 1)
            target = (lane + block) % classes if block < hot_width - HOT_PAD else lane
            parts.append(jnp.where(val == target.astype(FLOAT), 1.0, 0.0).astype(BFLOAT))
        return jnp.concatenate(parts, axis=1)

    def gvec_add(row, values):
        gvec_ref[row : row + 1, :] += values

    gstem_ref[...] = jnp.zeros_like(gstem_ref)
    gqkv_ref[...] = jnp.zeros_like(gqkv_ref)
    gout_ref[...] = jnp.zeros_like(gout_ref)
    gup_ref[...] = jnp.zeros_like(gup_ref)
    gdown_ref[...] = jnp.zeros_like(gdown_ref)
    gvec_ref[...] = jnp.zeros_like(gvec_ref)

    g1, b1, g2, b2, bd = [ref[...] for ref in refs["vec"]]

    def seg_bias(seq):
        row = seg_ref[pl.ds(seq, 1), :]
        lane = iota((length, PACK), 1) % length
        key = iota((length, PACK), 0)
        first = jnp.broadcast_to(row[:, :128], (length, 128))
        pick = iota((length, 128), 0) == iota((length, 128), 1)
        column = jnp.sum(jnp.where(pick, first, 0.0), axis=1, keepdims=True)
        return jnp.where((column == row) & (key <= lane), 0.0, -1e30)

    hooks["start"]()

    @pl.loop(0, tiles)
    def phase_zero(t):
        hooks["lat_ready"](t)
        r0 = pl.multiple_of(t * tile, tile)
        tok_s[pl.ds(r0, tile), :] = dot(make_hot(t), stem_ref[...]).astype(BFLOAT)
        hooks["stem_done"](t)

    @pl.loop(0, packs)
    def phase_one(turn):
        pack = lax.rem(turn + refs["own"], packs)

        @pl.loop(0, tiles)
        def each(t):
            r0 = pl.multiple_of(t * tile, tile)
            here = pl.ds(r0, tile)
            xhat, _ = norm_stats(tok_s[here, :].astype(FLOAT))
            normed = (xhat * g1 + b1).astype(BFLOAT)
            col0 = pl.multiple_of(pack * PACK, PACK)
            cols = [pl.ds(pl.multiple_of(part * width + pack * PACK, PACK), PACK) for part in range(3)]
            for part in range(3):
                value = dot(normed, wqkv_ref[:, cols[part]])
                if part == 0:
                    value = value.astype(BFLOAT).astype(FLOAT) * 0.125
                qkv_s[here, cols[part]] = value.astype(BFLOAT)

            @pl.loop(0, tile // SUB)
            def attend(sub):
                units, bias = [], []
                for seq in range(SUB // length):
                    s0 = pl.multiple_of(r0 + sub * SUB + seq * length, length)
                    units.append(pl.ds(s0, length))
                    bias.append(seg_bias(t * (tile // length) + sub * (SUB // length) + seq))
                qs = [block_diag(qkv_s[rs, cols[0]]) for rs in units]
                ks = [qkv_s[rs, cols[1]] for rs in units]
                scores = [dot_t(k, q) + b for q, k, b in zip(qs, ks, bias)]
                es = [jnp.exp(x - jnp.max(x, axis=0, keepdims=True)) for x in scores]
                ps = [(e * (1.0 / jnp.sum(e, axis=0, keepdims=True))).astype(BFLOAT) for e in es]
                vs = [qkv_s[rs, cols[2]] for rs in units]
                ms = [diag_rows(t_dot(p, v)).astype(BFLOAT) for p, v in zip(ps, vs)]
                for p, m, rs in zip(ps, ms, units):
                    prob_s[rs, pl.ds(col0, PACK)] = p
                    mix_s[rs, pl.ds(col0, PACK)] = m

            hooks["attend_done"](turn, t)

    hooks["forward_done"]()

    def phase_two(t, leading):
        r0 = pl.multiple_of(t * tile, tile)
        here = pl.ds(r0, tile)
        resid = tok_s[here, :].astype(FLOAT) + dot(mix_s[here, :], wout_ref[...])
        xhat, scale = norm_stats(resid)
        n2_s[...] = (xhat * g2 + b2).astype(BFLOAT)
        hooks["cot_ready"](t)
        cotp_s[...] = from_frames(cot_ref, t)
        acc_s[...] = resid + bd
        dn_s[...] = jnp.zeros_like(dn_s)

        def feed(turn):
            if leading:
                hooks["feed_block"](turn)
            blocks = ff // FFB
            f = lax.rem(turn + refs["own"] * (blocks // 2), blocks)
            f0 = pl.multiple_of(f * FFB, FFB)
            fs = pl.ds(f0, FFB)
            n2 = n2_s[...]
            cot = cotp_s[...]
            up = wup_ref[:, fs]
            down = wdown_ref[fs, :]
            pre = dot(n2, up) + upb_ref[0:1, fs]
            square = pre * pre
            tanh = jnp.tanh(GELU_C * pre * (1.0 + GELU_A * square))
            half = 0.5 * (1.0 + tanh)
            hidden = (pre * half).astype(BFLOAT)
            slope = half + (0.5 * GELU_C) * pre * (1.0 - tanh * tanh) * (1.0 + 3.0 * GELU_A * square)
            acc_s[...] += dot(hidden, down)
            gdown_ref[fs, :] += t_dot(hidden, cot)
            d_pre = (dot_t(cot, down) * slope).astype(BFLOAT)
            sums = col_sum(d_pre.astype(FLOAT))
            for part in range(FFB // width):
                row = pl.multiple_of((f * (FFB // width) + part) * 16, 16)
                gvec_ref[pl.ds(row, 1), :] += sums[:, part * width : (part + 1) * width]
            gup_ref[:, fs] += t_dot(n2, d_pre)
            dn_s[...] += dot_t(d_pre, up)

        for turn in range(ff // FFB):
            feed(turn)

        cot_f = cotp_s[...].astype(FLOAT)
        gvec_add(5, col_sum(cot_f))
        to_frames(out_ref, t, acc_s[...].astype(BFLOAT))
        hooks["out_ready"](t)
        resid = tok_s[here, :].astype(FLOAT) + dot(mix_s[here, :], wout_ref[...])
        xhat, scale = norm_stats(resid)
        dn = dn_s[...]
        gvec_add(3, col_sum(dn * xhat))
        gvec_add(4, col_sum(dn))
        d_branch = (cot_f + norm_back(dn, xhat, scale, g2)).astype(BFLOAT)
        dbr_s[here, :] = d_branch
        gout_ref[...] += t_dot(mix_s[here, :], d_branch)
        mix_s[here, :] = dot_t(d_branch, wout_ref[...]).astype(BFLOAT)

    phase_two(0, True)
    pl.loop(1, tiles)(functools.partial(phase_two, leading=False))
    hooks["feed_done"]()

    @pl.loop(0, tiles)
    def phase_three(t):
        r0 = pl.multiple_of(t * tile, tile)
        here = pl.ds(r0, tile)

        @pl.loop(0, tile // 256)
        def attend(sub):
            for seq0 in range(0, 256 // length, UNIT):
                units = []
                for seq in range(seq0, seq0 + UNIT):
                    s0 = pl.multiple_of(r0 + sub * 256 + seq * length, length)
                    units += [(pl.ds(s0, length), pack * PACK) for pack in range(packs)]
                gs = [block_diag(mix_s[rs, c0 : c0 + PACK]) for rs, c0 in units]
                vs = [qkv_s[rs, 2 * width + c0 : 2 * width + c0 + PACK] for rs, c0 in units]
                dps = [dot_t(v, g).astype(BFLOAT).astype(FLOAT) for v, g in zip(vs, gs)]
                lows = [prob_s[rs, c0 : c0 + PACK] for rs, c0 in units]
                ws = [low.astype(FLOAT) * dp for low, dp in zip(lows, dps)]
                dss = [
                    (w - low.astype(FLOAT) * jnp.sum(w, axis=0, keepdims=True)).astype(BFLOAT)
                    for w, low in zip(ws, lows)
                ]
                dvs = [dot(low, g).astype(BFLOAT) for low, g in zip(lows, gs)]
                ks = [qkv_s[rs, width + c0 : width + c0 + PACK] for rs, c0 in units]
                qs = [block_diag(qkv_s[rs, c0 : c0 + PACK]) for rs, c0 in units]
                dks = [dot(ds, q).astype(BFLOAT) for ds, q in zip(dss, qs)]
                dqs = [(0.125 * diag_rows(t_dot(ds, k))).astype(BFLOAT) for ds, k in zip(dss, ks)]
                for dq, dk, dv, (rs, c0) in zip(dqs, dks, dvs, units):
                    qkv_s[rs, c0 : c0 + PACK] = dq
                    qkv_s[rs, width + c0 : width + c0 + PACK] = dk
                    qkv_s[rs, 2 * width + c0 : 2 * width + c0 + PACK] = dv

        hooks["attend_back_done"](t)
        xhat, scale = norm_stats(tok_s[here, :].astype(FLOAT))
        normed = (xhat * g1 + b1).astype(BFLOAT)
        for part in range(3):
            cols = slice(part * width, (part + 1) * width)
            gqkv_ref[:, cols] += t_dot(normed, qkv_s[here, cols])
        dn = dot_t(qkv_s[here, :], wqkv_ref[...])
        gvec_add(1, col_sum(dn * xhat))
        gvec_add(2, col_sum(dn))
        token_grad = (dbr_s[here, :].astype(FLOAT) + norm_back(dn, xhat, scale, g1)).astype(BFLOAT)
        hooks["tg_room"](t)
        to_frames(tg_ref, t, token_grad)
        hooks["tg_ready"](t)
        gstem_ref[...] += t_dot(make_hot(t), token_grad)
        hooks["tile_done"](t)


def no_tile_hook(t):
    return None


def no_pair_hook(a, b):
    return None


def no_hook():
    return None


NO_HOOKS = {
    "lat_ready": no_tile_hook,
    "stem_done": no_tile_hook,
    "attend_done": no_pair_hook,
    "feed_block": no_tile_hook,
    "attend_back_done": no_tile_hook,
    "cot_ready": no_tile_hook,
    "out_ready": no_tile_hook,
    "tg_room": no_tile_hook,
    "tg_ready": no_tile_hook,
    "tile_done": no_tile_hook,
    "start": no_hook,
    "forward_done": no_hook,
    "feed_done": no_hook,
}


def work_shapes(rows, width, tile):
    return [
        pltpu.VMEM((rows, width), BFLOAT),
        pltpu.VMEM((rows, 3 * width), BFLOAT),
        pltpu.VMEM((rows, width), BFLOAT),
        pltpu.VMEM((rows, width), BFLOAT),
        pltpu.VMEM((rows, width), BFLOAT),
        pltpu.VMEM((tile, width), FLOAT),
        pltpu.VMEM((tile, width), FLOAT),
        pltpu.VMEM((tile, width), BFLOAT),
        pltpu.VMEM((tile, width), BFLOAT),
    ]


def local_kernel(local_len, *refs):
    block_compute(
        local_len,
        {"in": refs[:9], "vec": refs[9:14], "stage": refs[14:16], "grads": refs[16:22], "work": refs[22:], "own": 0, "pairs": 1},
        NO_HOOKS,
    )


def run_local(local_len, lat, seg, cot, stem, wqkv, wout, wup, wdown, upb, *vec):
    places, per, width = cot.shape
    group_rows = 16 // local_len * (places * local_len)
    shape = jax.ShapeDtypeStruct
    vm = pl.BlockSpec(memory_space=pltpu.VMEM)
    return pl.pallas_call(
        functools.partial(local_kernel, local_len),
        out_shape=(
            shape(cot.shape, BFLOAT),
            shape(cot.shape, BFLOAT),
            shape(stem.shape, FLOAT),
            shape(wqkv.shape, FLOAT),
            shape(wout.shape, FLOAT),
            shape(wup.shape, FLOAT),
            shape(wdown.shape, FLOAT),
            shape((wup.shape[1] // width * 16, width), FLOAT),
        ),
        in_specs=[vm] * 14,
        out_specs=[vm] * 8,
        scratch_shapes=work_shapes(places * per, width, max(TILE, group_rows)),
        compiler_params=pltpu.CompilerParams(vmem_limit_bytes=60 * 1024 * 1024),
    )(lat, seg, cot, stem, wqkv, wout, wup, wdown, upb, *vec)


def wait_for(ref, sem):
    pltpu.make_async_copy(ref, ref, sem).wait()


DOWN, UP, STEM, QUERY = range(4)
EARLY = ((0, DOWN, 1), (1, UP, 1), (2, DOWN, 2))
ORDER = (
    (STEM, 1),
    (QUERY, 1),
    (UP, 2),
    (DOWN, 3),
    (STEM, 2),
    (UP, 3),
    (QUERY, 2),
    (STEM, 3),
    (DOWN, 4),
    (QUERY, 3),
    (UP, 4),
    (STEM, 4),
    (DOWN, 5),
    (QUERY, 4),
    (UP, 5),
    (STEM, 5),
    (QUERY, 5),
)
TURNS = tuple((dx, dy, dz) for dx in range(2) for dy in range(2) for dz in range(2))


class Reducer:
    def __init__(self, where, pieces, bufs, final, sems, everywhere):
        self.i, self.j = where
        self.pieces = pieces
        self.send, self.r1, self.r2, self.r3, self.r5, self.fin = bufs
        self.final = final
        self.ssem, self.rsem = sems
        self.core = self.bit(0)
        self.part = self.send.shape[1] // 4
        self.everywhere = everywhere
        self.mine = self.rows(0, 0)

    def bit(self, n):
        return lax.rem(self.i // (1 << n), 2)

    def near(self, bit):
        step = 1 << bit
        return (self.i + step - 2 * step * self.bit(bit), self.j)

    def rows(self, dy, dz):
        y = self.bit(1) + dy - 2 * dy * self.bit(1)
        z = self.bit(2) + dz - 2 * dz * self.bit(2)
        return pl.ds(pl.multiple_of((y * 2 + z) * self.part, 16), self.part)

    def plane(self, dx):
        return 1 - self.j if dx else self.j

    def member(self, dx, dy, dz):
        place = self.i + dy * (2 - 4 * self.bit(1)) + dz * (4 - 8 * self.bit(2))
        return (place, self.plane(dx))

    def copy(self, n, src, dst, device):
        return pltpu.make_async_remote_copy(
            src_ref=src,
            dst_ref=dst,
            send_sem=self.ssem.at[n],
            recv_sem=self.rsem.at[n],
            device_id=device,
            device_id_type=pl.DeviceIdType.MESH,
        )

    def core_copy(self):
        return self.copy(0, self.send, self.r1, self.near(0))

    def start_core(self):
        for h in range(2):
            for at, take in self.pieces(h, 1 - self.core):
                self.send[h, at[0], at[1]] = take().astype(BFLOAT)
        self.core_copy().start()

    def x_copy(self):
        return self.copy(1, self.send.at[0], self.r2, (self.i, 1 - self.j))

    def core_to_x(self):
        self.core_copy().wait()
        for n, h in enumerate((1 - self.j, self.j)):
            for at, take in self.pieces(h, self.core):
                arrived = self.r1[h, at[0], at[1]].astype(FLOAT)
                self.send[n, at[0], at[1]] = (take() + arrived).astype(BFLOAT)
            if n == 0:
                self.x_copy().start()

    def x_to_direct(self):
        self.x_copy().wait()
        self.send[1] = (self.send[1].astype(FLOAT) + self.r2[...].astype(FLOAT)).astype(BFLOAT)
        for n, (dx, dy, dz) in enumerate(TURNS[3:0:-1]):
            self.copy(6, self.send.at[1, self.rows(dy, dz), :], self.r3.at[n], self.member(dx, dy, dz)).start()

    def z_copy(self):
        return self.copy(2, self.send.at[1, self.mine, :], self.r5, self.near(3))

    def direct_to_z(self):
        wait_for(self.r3, self.ssem.at[6])
        wait_for(self.r3, self.rsem.at[6])
        total = self.send[1, self.mine, :].astype(FLOAT)
        for n in range(3):
            total += self.r3[n].astype(FLOAT)
        self.send[1, self.mine, :] = total.astype(BFLOAT)
        self.z_copy().start()

    def keep_copy(self):
        return pltpu.make_async_copy(self.fin, self.final.at[self.core, self.mine, :], self.ssem.at[7])

    def z_to_gather(self):
        self.z_copy().wait()
        total = self.send[1, self.mine, :].astype(FLOAT) + self.r5[...].astype(FLOAT)
        self.fin[...] = total.astype(BFLOAT)
        self.keep_copy().start()
        dst = self.final.at[self.core, self.mine, :]
        for dx, dy, dz in TURNS[:0:-1]:
            if dx == 0 or self.everywhere is not None:
                self.copy(3 + dx, self.fin, dst, self.member(dx, dy, dz)).start()

    def core_gather(self):
        if self.everywhere is not None:
            place = self.everywhere.at[:, self.core]
        else:
            place = self.final.at[self.core]
        return self.copy(5, place, place, self.near(0))

    def gather_to_core(self):
        self.keep_copy().wait()
        three = self.final.at[self.core, 0 : 3 * self.part, :]
        wait_for(three, self.ssem.at[3])
        wait_for(three, self.rsem.at[3])
        if self.everywhere is not None:
            four = self.everywhere.at[1 - self.j, self.core]
            wait_for(four, self.ssem.at[4])
            wait_for(four, self.rsem.at[4])
        self.core_gather().start()

    def step(self, n):
        (
            self.start_core,
            self.core_to_x,
            self.x_to_direct,
            self.direct_to_z,
            self.z_to_gather,
            self.gather_to_core,
        )[n]()


def wide_kernel(local_len, *refs):
    (
        lat_hbm, seg_ref, cot_hbm, stem_hbm, extra_hbm,
        wq_hbm, wk_hbm, wv_hbm, wo_hbm, wup_hbm, wdown_hbm, upb_hbm,
    ) = refs[:12]
    vec = refs[12:17]
    out_hbm, tg_hbm, down_hbm, up_hbm, query_hbm, shared_hbm = refs[17:23]
    (
        lat_s, frame_s, stem_s, wqkv_s, wout_s, wup_s, wdown_s, upb_s,
        gstem_s, gqkv_s, gout_s, gup_s, gdown_s, gvec_s,
    ) = refs[23:37]
    work = refs[37:44]
    own_s = refs[44]
    group_bufs = [refs[45 + 6 * n : 51 + 6 * n] for n in range(4)]
    sizes = [bufs[0].shape[1] for bufs in group_bufs]
    tile = work[5].shape[0]
    work = work[:5] + (own_s.at[0:tile, :], own_s.at[tile : 2 * tile, :]) + work[5:]
    (
        lat_send, lat_recv, cot_send, cot_recv, own_sem, out_send, out_recv, tg_send, tg_recv,
        w_local, wx_send, wx_recv, wy_send, wy_recv, wc_send, wc_recv,
    ) = refs[69:85]
    group_sems = [refs[85 + 2 * n : 87 + 2 * n] for n in range(4)]
    i, j = lax.axis_index("gx"), lax.axis_index("gy")
    places = lax.axis_size("gx")
    core = lax.rem(i, 2)
    sibling = (i + 1 - 2 * core, j)
    ybit = lax.rem(i // 2, 2)
    beside = (i + 2 - 4 * ybit, j)
    across = (i, 1 - j)
    tiles = work[0].shape[0] // tile
    width = work[0].shape[1]
    mesh_id = pl.DeviceIdType.MESH

    def remote(src, dst, send, recv, device):
        return pltpu.make_async_remote_copy(
            src_ref=src, dst_ref=dst, send_sem=send, recv_sem=recv, device_id=device, device_id_type=mesh_id
        )

    barrier = pltpu.get_barrier_semaphore()

    @pl.loop(1, places)
    def greet(k):
        pl.semaphore_signal(barrier, inc=1, device_id=(lax.rem(i + k, places), j), device_id_type=mesh_id)

    for dy in range(2):
        for dz in range(2):
            place = i + dy * (2 - 4 * ybit) + dz * (4 - 8 * lax.rem(i // 4, 2))
            pl.semaphore_signal(barrier, inc=1, device_id=(place, 1 - j), device_id_type=mesh_id)
    pl.semaphore_wait(barrier, places + 3)

    def part(ref, t):
        count = ref.shape[1] // tiles
        return pl.ds(pl.multiple_of(t * count, count), count)

    def scatter(src, dst, t, send, recv):
        @pl.loop(1, places)
        def each(k):
            d = lax.rem(i + k, places)
            remote(src.at[d, part(src, t), :], dst.at[i, part(src, t), :], send, recv, (d, j)).start()

    def keep(src, dst, t, sem):
        return pltpu.make_async_copy(src.at[i, part(src, t), :], dst.at[i, part(src, t), :], sem)

    def most(ref, t):
        return ref.at[0 : places - 1, part(ref, t), :]

    half = wq_hbm.shape[1]

    ff_half = upb_hbm.shape[1]
    blocks = ff_half // FFB

    def weight_views(owner, share):
        def rows_of(count):
            if share == "all":
                return 0, count
            if share == "half":
                return pl.multiple_of(core * (count // 2), 16), count // 2
            return pl.multiple_of((core * 2 + ybit) * (count // 4), 16), count // 4

        start, size = rows_of(width)
        r = pl.ds(start, size)
        views = []
        for n, src in enumerate((wq_hbm, wk_hbm, wv_hbm)):
            at = pl.ds(pl.multiple_of(n * width + owner * half, half), half)
            views.append((src.at[r, :], wqkv_s.at[r, at]))
        count = wo_hbm.shape[0]
        start, size = rows_of(count)
        there = pl.ds(pl.multiple_of(owner * count + start, 16), size)
        views.append((wo_hbm.at[pl.ds(start, size), :], wout_s.at[there, :]))
        start, size = rows_of(FFB)
        for block in range(blocks):
            at = pl.ds(pl.multiple_of(owner * ff_half + block * FFB, 128), FFB)
            views.append((wup_hbm.at[r, block * FFB : (block + 1) * FFB], wup_s.at[r, at]))
            here = pl.ds(pl.multiple_of(block * FFB + start, 16), size)
            there = pl.ds(pl.multiple_of(owner * ff_half + block * FFB + start, 16), size)
            views.append((wdown_hbm.at[here, :], wdown_s.at[there, :]))
        return views

    here_views = weight_views(j, "all")
    x_copies = [
        remote(src, dst, wx_send.at[n], wx_recv.at[n], across)
        for n, (src, dst) in enumerate(weight_views(j, "quarter")[:4] + weight_views(j, "half")[4:])
    ]
    y_copies = [
        remote(dst, dst, wy_send.at[n], wy_recv.at[n], beside)
        for n, (_, dst) in enumerate(weight_views(1 - j, "quarter")[:4])
    ]
    c_copies = [
        remote(dst, dst, wc_send.at[n], wc_recv.at[n], sibling)
        for n, (_, dst) in enumerate(weight_views(1 - j, "half"))
    ]
    own_copies = [pltpu.make_async_copy(src, dst, w_local.at[n]) for n, (src, dst) in enumerate(here_views)]
    n_weights = len(x_copies)
    upb_at = pl.ds(pl.multiple_of(j * ff_half, 128), ff_half)
    upb_x = remote(upb_hbm, upb_s.at[:, upb_at], wx_send.at[n_weights], wx_recv.at[n_weights], across)
    upb_own = pltpu.make_async_copy(upb_hbm, upb_s.at[:, upb_at], w_local.at[n_weights])

    for n in range(4):
        x_copies[n].start()

    @pl.loop(0, tiles)
    def send_lat(t):
        keep(lat_hbm, lat_s, t, own_sem.at[t]).start()
        scatter(lat_hbm, lat_s, t, lat_send, lat_recv.at[t])

    stem_rows_in = stem_hbm.shape[0]
    stem_copies = [
        pltpu.make_async_copy(stem_hbm, stem_s.at[0:stem_rows_in, :], w_local.at[n_weights + 1]),
        pltpu.make_async_copy(extra_hbm, stem_s.at[stem_rows_in:, :], w_local.at[n_weights + 2]),
    ]
    for copy in stem_copies:
        copy.start()
    for n in range(4, n_weights):
        x_copies[n].start()
    for copy in own_copies:
        copy.start()
    upb_x.start()
    upb_own.start()

    def send_cot(t):
        keep(cot_hbm, frame_s, t, own_sem.at[tiles + t]).start()
        scatter(cot_hbm, frame_s, t, cot_send, cot_recv.at[t])

    def move(first, last, before, after):
        for n in range(first, last):
            before[n].wait()
            if after is not None:
                after[n].start()

    for t in range(tiles):
        send_cot(t)

    last_tile = tiles - 1
    middle = min(1, last_tile)

    hooks = dict(NO_HOOKS)

    def lat_ready(t):
        keep(lat_hbm, lat_s, t, own_sem.at[t]).wait()
        wait_for(most(lat_s, t), lat_recv.at[t])

        @pl.when(t == 0)
        def _():
            for copy in stem_copies:
                copy.wait()

    def stem_done(t):
        @pl.when(t == last_tile)
        def _():
            move(0, 4, x_copies, y_copies)
            move(0, 4, own_copies, None)

    def attend_done(turn, t):
        @pl.when((turn == 0) & (t == last_tile))
        def _():
            move(0, 4, y_copies, c_copies)
            move(0, 4, c_copies, None)

        @pl.when((turn == 1) & (t == middle))
        def _():
            move(4, 6, x_copies, c_copies)

    def forward_done():
        upb_x.wait()
        upb_own.wait()
        move(4, n_weights, own_copies, None)

    def feed_block(turn):
        first = 4 + 2 * (turn - blocks)
        if turn > blocks:
            move(first, first + 2, x_copies, c_copies)
        if turn >= blocks:
            move(first, first + 2, c_copies, None)

    def cot_ready(t):
        keep(cot_hbm, frame_s, t, own_sem.at[tiles + t]).wait()
        wait_for(most(frame_s, t), cot_recv.at[t])

    def out_ready(t):
        keep(frame_s, out_hbm, t, own_sem.at[2 * tiles + t]).start()
        scatter(frame_s, out_hbm, t, out_send.at[t], out_recv)

    def tg_room(t):
        keep(frame_s, out_hbm, t, own_sem.at[2 * tiles + t]).wait()
        wait_for(most(frame_s, t), out_send.at[t])

    def send_tg(t):
        keep(frame_s, tg_hbm, t, own_sem.at[3 * tiles + t]).start()
        scatter(frame_s, tg_hbm, t, tg_send.at[t], tg_recv)

    def tg_ready(t):
        send_tg(t)

    def grab(ref, r0, nrows, c0, ncols):
        return lambda: ref[pl.ds(r0, nrows), pl.ds(c0, ncols)]

    def mult(value, by):
        return pl.multiple_of(value, by)

    up_half = gup_s.shape[1] // 2
    up_rows = width // 2
    down_rows = gdown_s.shape[0] // 4
    out_rows = gout_s.shape[0] // 4
    stem_rows = gstem_s.shape[0] // 4

    qrows = width // 2

    def down_pieces(h, c):
        return [((slice(None), slice(None)), grab(gdown_s, mult((h * 2 + c) * down_rows, 16), down_rows, 0, width))]

    def up_pieces(h, c):
        found, base = [], 0
        for block in range(up_half // width):
            found.append(
                (
                    (slice(base, base + up_rows), slice(None)),
                    grab(gup_s, mult(c * up_rows, 16), up_rows, mult(h * up_half + block * width, 128), width),
                )
            )
            base += up_rows
        found.append(
            (
                (slice(base, base + out_rows), slice(None)),
                grab(gout_s, mult((h * 2 + c) * out_rows, 16), out_rows, 0, width),
            )
        )
        return found

    def stem_pieces(h, c):
        found = [
            (
                (slice(0, stem_rows), slice(None)),
                grab(gstem_s, mult((h * 2 + c) * stem_rows, 16), stem_rows, 0, width),
            ),
            (
                (slice(stem_rows, stem_rows + 16), slice(None)),
                grab(gvec_s, mult((h * 2 + c) * 16, 16), 16, 0, width),
            ),
        ]
        base, end = stem_rows + 16, sizes[2]
        if end > base:
            found.append(((slice(base, end), slice(None)), lambda: jnp.zeros((end - base, width), FLOAT)))
        return found

    def query_pieces(h, c):
        found = [
            (
                (slice(0, qrows), slice(n * half, (n + 1) * half)),
                grab(gqkv_s, mult(c * qrows, 16), qrows, mult(n * width + h * half, 128), half),
            )
            for n in range(2)
        ]
        for n in range(2):
            found.append(
                (
                    (slice(qrows, qrows + qrows // 2), slice(n * half, (n + 1) * half)),
                    grab(gqkv_s, mult(c * qrows + n * (qrows // 2), 16), qrows // 2, mult(2 * width + h * half, 128), half),
                )
            )
        return found

    where = (i, j)
    down, up, stem, query = [
        Reducer(where, pieces, bufs, final, sems, everywhere)
        for pieces, bufs, final, sems, everywhere in zip(
            (down_pieces, up_pieces, stem_pieces, query_pieces),
            group_bufs,
            (down_hbm, up_hbm, shared_hbm.at[j], query_hbm),
            group_sems,
            (None, None, shared_hbm, None),
        )
    ]

    def feed_done():
        down.start_core()
        up.start_core()

    def attend_back_done(t):
        for at, group, n in EARLY:

            @pl.when(t == min(at, last_tile))
            def _():
                (down, up)[group].step(n)

    hooks.update(
        lat_ready=lat_ready,
        stem_done=stem_done,
        attend_done=attend_done,
        feed_block=feed_block,
        attend_back_done=attend_back_done,
        forward_done=forward_done,
        cot_ready=cot_ready,
        out_ready=out_ready,
        tg_room=tg_room,
        tg_ready=tg_ready,
        feed_done=feed_done,
    )
    block_compute(
        local_len,
        {
            "in": (lat_s, seg_ref, frame_s, stem_s, wqkv_s, wout_s, wup_s, wdown_s, upb_s),
            "vec": vec,
            "own": j,
            "pairs": frame_s.shape[1] // lat_s.shape[1],
            "stage": (frame_s, frame_s),
            "grads": (gstem_s, gqkv_s, gout_s, gup_s, gdown_s, gvec_s),
            "work": work,
        },
        hooks,
    )
    stem.start_core()
    query.start_core()
    groups = (down, up, stem, query)
    for g, n in ORDER:
        groups[g].step(n)
    for group in groups:
        group.core_gather().wait()
    wait_for(lat_hbm.at[0 : places - 1], lat_send)
    wait_for(cot_hbm.at[0 : places - 1], cot_send)
    wait_for(out_hbm.at[0 : places - 1], out_recv)
    wait_for(tg_hbm.at[0 : places - 1], tg_recv)

    @pl.loop(0, tiles)
    def drain(t):
        keep(frame_s, tg_hbm, t, own_sem.at[3 * tiles + t]).wait()
        wait_for(most(frame_s, t), tg_send.at[t])


def reduce_shapes(half, width):
    return [
        pltpu.VMEM((2, half, width), BFLOAT),
        pltpu.VMEM((2, half, width), BFLOAT),
        pltpu.VMEM((half, width), BFLOAT),
        pltpu.VMEM((3, half // 4, width), BFLOAT),
        pltpu.VMEM((half // 4, width), BFLOAT),
        pltpu.VMEM((half // 4, width), BFLOAT),
    ]


def run_wide(local_len, lat, seg, cot, stem, extra, wq, wk, wv, wo, wup, wdown, upb, *vec):
    places, per, width = cot.shape
    rows = places * per
    ff = 2 * wup.shape[1]
    hot_width = stem.shape[0] + extra.shape[0]
    shape = jax.ShapeDtypeStruct
    vm = pl.BlockSpec(memory_space=pltpu.VMEM)
    hbm = pl.BlockSpec(memory_space=pl.ANY)
    stem_used = hot_width // 4 + 16
    sizes = (
        ff // 4,
        (width // 2) * (wup.shape[1] // width) + width // 4,
        -(-stem_used // 64) * 64,
        width // 2 + width // 4,
    )
    tiles = rows // TILE
    n_weights = 4 + 2 * (wup.shape[1] // FFB)
    dma = pltpu.SemaphoreType.DMA
    scratch = [
        pltpu.VMEM(lat.shape, BFLOAT),
        pltpu.VMEM(cot.shape, BFLOAT),
        pltpu.VMEM((hot_width, width), BFLOAT),
        pltpu.VMEM((width, 3 * width), BFLOAT),
        pltpu.VMEM((width, width), BFLOAT),
        pltpu.VMEM((width, ff), BFLOAT),
        pltpu.VMEM((ff, width), BFLOAT),
        pltpu.VMEM((1, ff), FLOAT),
        pltpu.VMEM((hot_width, width), FLOAT),
        pltpu.VMEM((width, 3 * width), FLOAT),
        pltpu.VMEM((width, width), FLOAT),
        pltpu.VMEM((width, ff), FLOAT),
        pltpu.VMEM((ff, width), FLOAT),
        pltpu.VMEM((ff // width * 16, width), FLOAT),
    ]
    scratch += [item for n, item in enumerate(work_shapes(rows, width, TILE)) if n not in (5, 6)]
    scratch += [pltpu.VMEM((2 * TILE, width), FLOAT)]
    for size in sizes:
        scratch += reduce_shapes(size, width)
    scratch += [
        dma,
        dma((tiles,)),
        dma,
        dma((tiles,)),
        dma((4 * tiles,)),
        dma((tiles,)),
        dma,
        dma((tiles,)),
        dma,
        dma((n_weights + 3,)),
        dma((n_weights + 1,)),
        dma((n_weights + 1,)),
        dma((n_weights,)),
        dma((n_weights,)),
        dma((n_weights,)),
        dma((n_weights,)),
    ]
    scratch += [dma((8,))] * 8
    return pl.pallas_call(
        functools.partial(wide_kernel, local_len),
        out_shape=(shape(cot.shape, BFLOAT), shape(cot.shape, BFLOAT))
        + tuple(shape((2, sizes[n], width), BFLOAT) for n in (0, 1, 3))
        + (shape((2, 2, sizes[2], width), BFLOAT),),
        in_specs=[hbm, vm] + [hbm] * 10 + [vm] * 5,
        out_specs=[hbm] * 6,
        scratch_shapes=scratch,
        compiler_params=pltpu.CompilerParams(
            vmem_limit_bytes=VMEM_LIMIT, collective_id=0, has_side_effects=True
        ),
    )(lat, seg, cot, stem, extra, wq, wk, wv, wo, wup, wdown, upb, *vec)


def per_device(
    latents,
    actions,
    segment_ids,
    cotangent,
    stem_weight,
    action_table,
    first_gain,
    first_bias,
    query_weight,
    key_weight,
    value_weight,
    out_weight,
    second_gain,
    second_bias,
    up_weight,
    up_bias,
    down_weight,
    down_bias,
):
    half_seqs, local_len, groups = latents.shape
    width = stem_weight.shape[1]
    places = lax.axis_size("gx")
    length = places * local_len
    seqs = half_seqs // places
    rows = seqs * length
    actions_n = action_table.shape[0]

    lat = jnp.concatenate([latents, actions[..., None]], axis=-1).astype(BFLOAT)
    lat = lat.reshape(places, seqs, local_len, groups + 1)
    cot = cotangent.reshape(places, seqs * local_len, width)
    first_seq = (lax.axis_index("gy") * places + lax.axis_index("gx")) * seqs
    seg = lax.dynamic_slice_in_dim(segment_ids, first_seq, seqs, 0)
    seg = jnp.tile(seg.astype(FLOAT), (1, PACK // length))
    extra = jnp.pad(action_table, ((0, HOT_PAD - actions_n), (0, 0)))
    vec = [item[None] for item in (first_gain, first_bias, second_gain, second_bias, down_bias)]
    if rows % TILE == 0 and rows <= MAX_ROWS and places == 16:
        lat = jnp.pad(lat, ((0, 0), (0, 0), (0, 0), (0, 64 - groups - 1)))
        lat = lat.reshape(places, seqs * local_len // 2, 128)
        out, tg, gdown, up, query, shared = run_wide(
            local_len, lat, seg, cot, stem_weight, extra, query_weight, key_weight, value_weight,
            out_weight, up_weight, down_weight, up_bias[None], *vec,
        )
        out = out.reshape(half_seqs, local_len, width)
        tg = tg.reshape(half_seqs, local_len, width)
        half = width // 2
        cols = query_weight.shape[1]
        blocks = up_weight.shape[1] // width
        gdown = gdown.astype(FLOAT).reshape(down_weight.shape)
        gup = jnp.concatenate([up[:, b * half : (b + 1) * half] for b in range(blocks)], axis=2)
        gup = gup.astype(FLOAT).reshape(up_weight.shape)
        gout = up[:, blocks * half :].astype(FLOAT).reshape(out_weight.shape)
        query = query.astype(FLOAT)
        gq = query[:, :half, :cols].reshape(width, cols)
        gk = query[:, :half, cols:].reshape(width, cols)
        part = query[:, half:]
        gv = jnp.concatenate([part[:, :, :cols], part[:, :, cols:]], axis=1).reshape(width, cols)
        stem_rows = (stem_weight.shape[0] + HOT_PAD) // 4
        gstem = shared[:, :, :stem_rows].astype(FLOAT).reshape(4 * stem_rows, width)
        first = shared[0, 0, stem_rows : stem_rows + 16].astype(FLOAT)
        upb_grad = lax.dynamic_index_in_dim(shared[:, :, stem_rows], lax.axis_index("gy"), 0, False)
        upb_grad = upb_grad.astype(FLOAT).reshape(up_bias.shape)
        return (
            out,
            tg,
            gstem[: groups * 32],
            gstem[groups * 32 : groups * 32 + actions_n],
            first[1],
            first[2],
            gq,
            gk,
            gv,
            gout,
            first[3],
            first[4],
            gup,
            upb_grad,
            gdown,
            first[5],
        )
    lat = lat.reshape(places, seqs * local_len, groups + 1)
    lat = jnp.pad(lat, ((0, 0), (0, 0), (0, 128 - groups - 1)))
    lat = lax.all_to_all(lat, "gx", split_axis=0, concat_axis=0, tiled=True)
    cot = lax.all_to_all(cot, "gx", split_axis=0, concat_axis=0, tiled=True)
    gather = functools.partial(lax.all_gather, axis_name="gy", tiled=True)
    wqkv = jnp.concatenate(
        [gather(item, axis=1) for item in (query_weight, key_weight, value_weight)], axis=1
    )
    wout = gather(out_weight, axis=0)
    wup = gather(up_weight, axis=1)
    wdown = gather(down_weight, axis=0)
    upb = gather(up_bias, axis=0)[None]
    stem = jnp.concatenate([stem_weight, extra], axis=0)
    out, tg, gstem, gqkv, gout, gup, gdown, gvec = run_local(
        local_len, lat, seg, cot, stem, wqkv, wout, wup, wdown, upb, *vec
    )
    out = lax.all_to_all(out, "gx", split_axis=0, concat_axis=0, tiled=True)
    tg = lax.all_to_all(tg, "gx", split_axis=0, concat_axis=0, tiled=True)
    out = out.reshape(half_seqs, local_len, width)
    tg = tg.reshape(half_seqs, local_len, width)
    both = ("gx", "gy")
    gstem, gvec = lax.psum((gstem, gvec), both)
    upb_grad = gvec[::16].reshape(-1)
    upb_grad = lax.dynamic_slice_in_dim(upb_grad, lax.axis_index("gy") * up_bias.shape[0], up_bias.shape[0])

    def shard(value, dim):
        return lax.psum(lax.psum_scatter(value, "gy", scatter_dimension=dim, tiled=True), "gx")

    gq = shard(gqkv[:, :width], 1)
    gk = shard(gqkv[:, width : 2 * width], 1)
    gv = shard(gqkv[:, 2 * width :], 1)
    return (
        out,
        tg,
        gstem[: groups * 32],
        gstem[groups * 32 : groups * 32 + actions_n],
        gvec[1],
        gvec[2],
        gq,
        gk,
        gv,
        shard(gout, 0),
        gvec[3],
        gvec[4],
        shard(gup, 1),
        upb_grad,
        shard(gdown, 0),
        gvec[5],
    )


def solution(mesh):
    return jax.shard_map(
        per_device,
        mesh=mesh,
        in_specs=(
            P("gy", "gx", None),
            P("gy", "gx"),
            P(),
            P("gy", "gx", None),
            P(),
            P(),
            P(),
            P(),
            P(None, "gy"),
            P(None, "gy"),
            P(None, "gy"),
            P("gy", None),
            P(),
            P(),
            P(None, "gy"),
            P("gy"),
            P("gy", None),
            P(),
        ),
        out_specs=(
            P("gy", "gx", None),
            P("gy", "gx", None),
            P(),
            P(),
            P(),
            P(),
            P(None, "gy"),
            P(None, "gy"),
            P(None, "gy"),
            P("gy", None),
            P(),
            P(),
            P(None, "gy"),
            P("gy"),
            P("gy", None),
            P(),
        ),
        check_vma=False,
    )
```

```python
import functools

import jax
import jax.numpy as jnp
from jax import lax
from jax.experimental import pallas as pl
from jax.experimental.pallas import tpu as pltpu
from jax.sharding import PartitionSpec as P

HD = 64
PACK = 256
EPSILON = 1e-05
FLOAT = jnp.float32
BFLOAT = jnp.bfloat16
TILE = 512
MAX_ROWS = 2048
VMEM_LIMIT = 62 * 1024 * 1024
UNIT = 4
SUB = 512
FFB = 512
HOT_PAD = 128
GELU_C = 0.7978845608028654
GELU_A = 0.044715


def dot(left, right):
    return lax.dot_general(left, right, (((1,), (0,)), ((), ())), preferred_element_type=FLOAT)


def dot_t(left, right):
    return lax.dot_general(left, right, (((1,), (1,)), ((), ())), preferred_element_type=FLOAT)


def t_dot(left, right):
    return lax.dot_general(left, right, (((0,), (0,)), ((), ())), preferred_element_type=FLOAT)


def iota(shape, dim):
    return lax.broadcasted_iota(jnp.int32, shape, dim)


def norm_stats(values):
    average = jnp.mean(values, axis=-1, keepdims=True)
    centred = values - average
    spread = jnp.mean(centred * centred, axis=-1, keepdims=True)
    scale = lax.rsqrt(spread + EPSILON)
    return centred * scale, scale


def norm_back(grad, xhat, scale, gain):
    scaled = grad * gain
    mean_e = jnp.mean(scaled, axis=-1, keepdims=True)
    mean_x = jnp.mean(scaled * xhat, axis=-1, keepdims=True)
    return (scaled - mean_e - xhat * mean_x) * scale


def col_sum(values):
    return jnp.sum(values, axis=0, keepdims=True)


def head_reduce(values, op, fill):
    parts = []
    for half in range(PACK // 128):
        piece = values[:, half * 128 : (half + 1) * 128]
        low = iota(piece.shape, 1) < HD
        first = op(jnp.where(low, piece, fill), axis=-1, keepdims=True)
        second = op(jnp.where(low, fill, piece), axis=-1, keepdims=True)
        parts.append((low, first, second))
    return parts


def head_spread(parts):
    return jnp.concatenate([jnp.where(low, a, b) for low, a, b in parts], axis=1)


def block_diag(rows):
    mask = (iota((PACK, PACK), 0) // HD) == (iota((PACK, PACK), 1) // HD)
    return jnp.where(mask, jnp.concatenate([rows] * (PACK // HD), axis=0), jnp.zeros((), rows.dtype))


def diag_rows(full):
    lane_head = iota((HD, PACK), 1) // HD
    result = full[:HD]
    for head in range(1, PACK // HD):
        result = jnp.where(lane_head == head, full[head * HD : (head + 1) * HD], result)
    return result


def unrolled_loop(count, body):
    if count == 1:
        body(0)
    else:
        pl.loop(0, count)(body)


def row_maps(local_len, length, count, back):
    dest = iota((count, count), 1 if back else 0)
    src = iota((count, count), 0 if back else 1)
    want = ((dest % length) // local_len) * 16 + (dest // length) * local_len + dest % local_len
    return jnp.where(want == src, 1.0, 0.0).astype(BFLOAT)


def block_compute(local_len, refs, hooks):
    lat_ref, seg_ref, cot_ref, stem_ref, wqkv_ref, wout_ref, wup_ref, wdown_ref, upb_ref = refs["in"]
    out_ref, tg_ref = refs["stage"]
    gstem_ref, gqkv_ref, gout_ref, gup_ref, gdown_ref, gvec_ref = refs["grads"]
    tok_s, qkv_s, prob_s, mix_s, dbr_s, acc_s, dn_s, n2_s, cotp_s = refs["work"]
    rows, width = tok_s.shape
    places = cot_ref.shape[0]
    length = places * local_len
    packs = width // PACK
    group_rows = 16 // local_len * length
    tile = acc_s.shape[0]
    tiles = rows // tile
    groups = tile // group_rows
    ff = wup_ref.shape[1]
    hot_width = stem_ref.shape[0]
    classes = (hot_width - HOT_PAD) // 32

    def to_frames(ref, t, values):
        for g in range(groups):
            k0 = pl.multiple_of((t * groups + g) * 16, 16)
            back = dot(
                row_maps(local_len, length, group_rows, True),
                values[g * group_rows : (g + 1) * group_rows, :],
            )
            ref[:, pl.ds(k0, 16), :] = back.astype(BFLOAT).reshape(places, 16, width)

    def from_frames(ref, t):
        parts = []
        for g in range(groups):
            k0 = pl.multiple_of((t * groups + g) * 16, 16)
            raw = ref[:, pl.ds(k0, 16), :].reshape(group_rows, ref.shape[2])
            parts.append(dot(row_maps(local_len, length, group_rows, False), raw).astype(BFLOAT))
        return jnp.concatenate(parts, axis=0) if groups > 1 else parts[0]

    pairs = refs["pairs"]
    lat_rows = tile // places // pairs
    slot = lat_ref.shape[2] // pairs

    def make_hot(t):
        k0 = pl.multiple_of(t * lat_rows, lat_rows)
        raw = lat_ref[:, pl.ds(k0, lat_rows), :].reshape(places * lat_rows, lat_ref.shape[2])
        dest = iota((tile, places * lat_rows), 0)
        src = iota((tile, places * lat_rows), 1)
        frame = dest % local_len
        want = ((dest % length) // local_len) * lat_rows
        want += (dest // length) * (local_len // pairs) + frame // pairs
        lats = dot(jnp.where(want == src, 1.0, 0.0).astype(BFLOAT), raw)
        if pairs > 1:
            turn = iota(lats.shape, 0) % pairs
            lats = jnp.where(iota(lats.shape, 1) // slot == turn, lats, 0.0)
        lats = lats.astype(BFLOAT)
        parts = []
        for block in range(0, hot_width, 128):
            g = iota((lats.shape[1], 128), 0) % slot
            c = iota((lats.shape[1], 128), 1) + block
            spread = jnp.where(jnp.minimum(c // classes, 32) == g, 1.0, 0.0).astype(BFLOAT)
            val = dot(lats, spread)
            lane = iota((tile, 128), 1)
            target = (lane + block) % classes if block < hot_width - HOT_PAD else lane
            parts.append(jnp.where(val == target.astype(FLOAT), 1.0, 0.0).astype(BFLOAT))
        return jnp.concatenate(parts, axis=1)

    def gvec_add(row, values):
        gvec_ref[row : row + 1, :] += values

    gstem_ref[...] = jnp.zeros_like(gstem_ref)
    gqkv_ref[...] = jnp.zeros_like(gqkv_ref)
    gout_ref[...] = jnp.zeros_like(gout_ref)
    gup_ref[...] = jnp.zeros_like(gup_ref)
    gdown_ref[...] = jnp.zeros_like(gdown_ref)
    gvec_ref[...] = jnp.zeros_like(gvec_ref)

    g1, b1, g2, b2, bd = [ref[...] for ref in refs["vec"]]

    def seg_bias(seq):
        row = seg_ref[pl.ds(seq, 1), :]
        lane = iota((length, PACK), 1) % length
        key = iota((length, PACK), 0)
        first = jnp.broadcast_to(row[:, :128], (length, 128))
        pick = iota((length, 128), 0) == iota((length, 128), 1)
        column = jnp.sum(jnp.where(pick, first, 0.0), axis=1, keepdims=True)
        return jnp.where((column == row) & (key <= lane), 0.0, -1e30)

    hooks["start"]()

    @pl.loop(0, tiles)
    def phase_zero(t):
        hooks["lat_ready"](t)
        r0 = pl.multiple_of(t * tile, tile)
        tok_s[pl.ds(r0, tile), :] = dot(make_hot(t), stem_ref[...]).astype(BFLOAT)
        hooks["stem_done"](t)

    @pl.loop(0, packs)
    def phase_one(turn):
        pack = lax.rem(turn + refs["own"], packs)

        @pl.loop(0, tiles)
        def each(t):
            r0 = pl.multiple_of(t * tile, tile)
            here = pl.ds(r0, tile)
            xhat, _ = norm_stats(tok_s[here, :].astype(FLOAT))
            normed = (xhat * g1 + b1).astype(BFLOAT)
            col0 = pl.multiple_of(pack * PACK, PACK)
            cols = [pl.ds(pl.multiple_of(part * width + pack * PACK, PACK), PACK) for part in range(3)]
            for part in range(3):
                value = dot(normed, wqkv_ref[:, cols[part]])
                if part == 0:
                    value = value.astype(BFLOAT).astype(FLOAT) * 0.125
                qkv_s[here, cols[part]] = value.astype(BFLOAT)

            @pl.loop(0, tile // SUB)
            def attend(sub):
                units, bias = [], []
                for seq in range(SUB // length):
                    s0 = pl.multiple_of(r0 + sub * SUB + seq * length, length)
                    units.append(pl.ds(s0, length))
                    bias.append(seg_bias(t * (tile // length) + sub * (SUB // length) + seq))
                qs = [block_diag(qkv_s[rs, cols[0]]) for rs in units]
                ks = [qkv_s[rs, cols[1]] for rs in units]
                scores = [dot_t(k, q) + b for q, k, b in zip(qs, ks, bias)]
                es = [jnp.exp(x - jnp.max(x, axis=0, keepdims=True)) for x in scores]
                ps = [(e * (1.0 / jnp.sum(e, axis=0, keepdims=True))).astype(BFLOAT) for e in es]
                vs = [qkv_s[rs, cols[2]] for rs in units]
                ms = [diag_rows(t_dot(p, v)).astype(BFLOAT) for p, v in zip(ps, vs)]
                for p, m, rs in zip(ps, ms, units):
                    prob_s[rs, pl.ds(col0, PACK)] = p
                    mix_s[rs, pl.ds(col0, PACK)] = m

            hooks["attend_done"](turn, t)

    hooks["forward_done"]()

    def phase_two(t, leading):
        r0 = pl.multiple_of(t * tile, tile)
        here = pl.ds(r0, tile)
        resid = tok_s[here, :].astype(FLOAT) + dot(mix_s[here, :], wout_ref[...])
        xhat, scale = norm_stats(resid)
        n2_s[...] = (xhat * g2 + b2).astype(BFLOAT)
        hooks["cot_ready"](t)
        cotp_s[...] = from_frames(cot_ref, t)
        acc_s[...] = resid + bd
        dn_s[...] = jnp.zeros_like(dn_s)

        def feed(turn):
            if leading:
                hooks["feed_block"](turn)
            blocks = ff // FFB
            f = lax.rem(turn + refs["own"] * (blocks // 2), blocks)
            f0 = pl.multiple_of(f * FFB, FFB)
            fs = pl.ds(f0, FFB)
            n2 = n2_s[...]
            cot = cotp_s[...]
            up = wup_ref[:, fs]
            down = wdown_ref[fs, :]
            pre = dot(n2, up) + upb_ref[0:1, fs]
            square = pre * pre
            tanh = jnp.tanh(GELU_C * pre * (1.0 + GELU_A * square))
            half = 0.5 * (1.0 + tanh)
            hidden = (pre * half).astype(BFLOAT)
            slope = half + (0.5 * GELU_C) * pre * (1.0 - tanh * tanh) * (1.0 + 3.0 * GELU_A * square)
            acc_s[...] += dot(hidden, down)
            gdown_ref[fs, :] += t_dot(hidden, cot)
            d_pre = (dot_t(cot, down) * slope).astype(BFLOAT)
            sums = col_sum(d_pre.astype(FLOAT))
            for part in range(FFB // width):
                row = pl.multiple_of((f * (FFB // width) + part) * 16, 16)
                gvec_ref[pl.ds(row, 1), :] += sums[:, part * width : (part + 1) * width]
            gup_ref[:, fs] += t_dot(n2, d_pre)
            dn_s[...] += dot_t(d_pre, up)

        for turn in range(ff // FFB):
            feed(turn)

        cot_f = cotp_s[...].astype(FLOAT)
        gvec_add(5, col_sum(cot_f))
        to_frames(out_ref, t, acc_s[...].astype(BFLOAT))
        hooks["out_ready"](t)
        resid = tok_s[here, :].astype(FLOAT) + dot(mix_s[here, :], wout_ref[...])
        xhat, scale = norm_stats(resid)
        dn = dn_s[...]
        gvec_add(3, col_sum(dn * xhat))
        gvec_add(4, col_sum(dn))
        d_branch = (cot_f + norm_back(dn, xhat, scale, g2)).astype(BFLOAT)
        dbr_s[here, :] = d_branch
        gout_ref[...] += t_dot(mix_s[here, :], d_branch)
        mix_s[here, :] = dot_t(d_branch, wout_ref[...]).astype(BFLOAT)

    phase_two(0, True)
    pl.loop(1, tiles)(functools.partial(phase_two, leading=False))
    hooks["feed_done"]()

    @pl.loop(0, tiles)
    def phase_three(t):
        r0 = pl.multiple_of(t * tile, tile)
        here = pl.ds(r0, tile)

        @pl.loop(0, tile // 256)
        def attend(sub):
            for seq0 in range(0, 256 // length, UNIT):
                units = []
                for seq in range(seq0, seq0 + UNIT):
                    s0 = pl.multiple_of(r0 + sub * 256 + seq * length, length)
                    units += [(pl.ds(s0, length), pack * PACK) for pack in range(packs)]
                gs = [block_diag(mix_s[rs, c0 : c0 + PACK]) for rs, c0 in units]
                vs = [qkv_s[rs, 2 * width + c0 : 2 * width + c0 + PACK] for rs, c0 in units]
                dps = [dot_t(v, g).astype(BFLOAT).astype(FLOAT) for v, g in zip(vs, gs)]
                lows = [prob_s[rs, c0 : c0 + PACK] for rs, c0 in units]
                ws = [low.astype(FLOAT) * dp for low, dp in zip(lows, dps)]
                dss = [
                    (w - low.astype(FLOAT) * jnp.sum(w, axis=0, keepdims=True)).astype(BFLOAT)
                    for w, low in zip(ws, lows)
                ]
                dvs = [dot(low, g).astype(BFLOAT) for low, g in zip(lows, gs)]
                ks = [qkv_s[rs, width + c0 : width + c0 + PACK] for rs, c0 in units]
                qs = [block_diag(qkv_s[rs, c0 : c0 + PACK]) for rs, c0 in units]
                dks = [dot(ds, q).astype(BFLOAT) for ds, q in zip(dss, qs)]
                dqs = [(0.125 * diag_rows(t_dot(ds, k))).astype(BFLOAT) for ds, k in zip(dss, ks)]
                for dq, dk, dv, (rs, c0) in zip(dqs, dks, dvs, units):
                    qkv_s[rs, c0 : c0 + PACK] = dq
                    qkv_s[rs, width + c0 : width + c0 + PACK] = dk
                    qkv_s[rs, 2 * width + c0 : 2 * width + c0 + PACK] = dv

        hooks["attend_back_done"](t)
        xhat, scale = norm_stats(tok_s[here, :].astype(FLOAT))
        normed = (xhat * g1 + b1).astype(BFLOAT)
        for part in range(3):
            cols = slice(part * width, (part + 1) * width)
            gqkv_ref[:, cols] += t_dot(normed, qkv_s[here, cols])
        dn = dot_t(qkv_s[here, :], wqkv_ref[...])
        gvec_add(1, col_sum(dn * xhat))
        gvec_add(2, col_sum(dn))
        token_grad = (dbr_s[here, :].astype(FLOAT) + norm_back(dn, xhat, scale, g1)).astype(BFLOAT)
        hooks["tg_room"](t)
        to_frames(tg_ref, t, token_grad)
        hooks["tg_ready"](t)
        gstem_ref[...] += t_dot(make_hot(t), token_grad)
        hooks["tile_done"](t)


def no_tile_hook(t):
    return None


def no_pair_hook(a, b):
    return None


def no_hook():
    return None


NO_HOOKS = {
    "lat_ready": no_tile_hook,
    "stem_done": no_tile_hook,
    "attend_done": no_pair_hook,
    "feed_block": no_tile_hook,
    "attend_back_done": no_tile_hook,
    "cot_ready": no_tile_hook,
    "out_ready": no_tile_hook,
    "tg_room": no_tile_hook,
    "tg_ready": no_tile_hook,
    "tile_done": no_tile_hook,
    "start": no_hook,
    "forward_done": no_hook,
    "feed_done": no_hook,
}


def work_shapes(rows, width, tile):
    return [
        pltpu.VMEM((rows, width), BFLOAT),
        pltpu.VMEM((rows, 3 * width), BFLOAT),
        pltpu.VMEM((rows, width), BFLOAT),
        pltpu.VMEM((rows, width), BFLOAT),
        pltpu.VMEM((rows, width), BFLOAT),
        pltpu.VMEM((tile, width), FLOAT),
        pltpu.VMEM((tile, width), FLOAT),
        pltpu.VMEM((tile, width), BFLOAT),
        pltpu.VMEM((tile, width), BFLOAT),
    ]


def local_kernel(local_len, *refs):
    block_compute(
        local_len,
        {"in": refs[:9], "vec": refs[9:14], "stage": refs[14:16], "grads": refs[16:22], "work": refs[22:], "own": 0, "pairs": 1},
        NO_HOOKS,
    )


def run_local(local_len, lat, seg, cot, stem, wqkv, wout, wup, wdown, upb, *vec):
    places, per, width = cot.shape
    group_rows = 16 // local_len * (places * local_len)
    shape = jax.ShapeDtypeStruct
    vm = pl.BlockSpec(memory_space=pltpu.VMEM)
    return pl.pallas_call(
        functools.partial(local_kernel, local_len),
        out_shape=(
            shape(cot.shape, BFLOAT),
            shape(cot.shape, BFLOAT),
            shape(stem.shape, FLOAT),
            shape(wqkv.shape, FLOAT),
            shape(wout.shape, FLOAT),
            shape(wup.shape, FLOAT),
            shape(wdown.shape, FLOAT),
            shape((wup.shape[1] // width * 16, width), FLOAT),
        ),
        in_specs=[vm] * 14,
        out_specs=[vm] * 8,
        scratch_shapes=work_shapes(places * per, width, max(TILE, group_rows)),
        compiler_params=pltpu.CompilerParams(vmem_limit_bytes=60 * 1024 * 1024),
    )(lat, seg, cot, stem, wqkv, wout, wup, wdown, upb, *vec)


def wait_for(ref, sem):
    pltpu.make_async_copy(ref, ref, sem).wait()


DOWN, UP, STEM, QUERY = range(4)
EARLY = ((0, DOWN, 1), (1, UP, 1), (2, DOWN, 2))
ORDER = (
    (STEM, 1),
    (QUERY, 1),
    (UP, 2),
    (DOWN, 3),
    (STEM, 2),
    (UP, 3),
    (QUERY, 2),
    (STEM, 3),
    (DOWN, 4),
    (QUERY, 3),
    (UP, 4),
    (STEM, 4),
    (DOWN, 5),
    (QUERY, 4),
    (UP, 5),
    (STEM, 5),
    (QUERY, 5),
)
TURNS = tuple((dx, dy, dz) for dx in range(2) for dy in range(2) for dz in range(2))


class Reducer:
    def __init__(self, where, pieces, bufs, final, sems, everywhere):
        self.i, self.j = where
        self.pieces = pieces
        self.send, self.r1, self.r2, self.r3, self.r5, self.fin = bufs
        self.final = final
        self.ssem, self.rsem = sems
        self.core = self.bit(0)
        self.part = self.send.shape[1] // 4
        self.everywhere = everywhere
        self.mine = self.rows(0, 0)

    def bit(self, n):
        return lax.rem(self.i // (1 << n), 2)

    def near(self, bit):
        step = 1 << bit
        return (self.i + step - 2 * step * self.bit(bit), self.j)

    def rows(self, dy, dz):
        y = self.bit(1) + dy - 2 * dy * self.bit(1)
        z = self.bit(2) + dz - 2 * dz * self.bit(2)
        return pl.ds(pl.multiple_of((y * 2 + z) * self.part, 16), self.part)

    def plane(self, dx):
        return 1 - self.j if dx else self.j

    def member(self, dx, dy, dz):
        place = self.i + dy * (2 - 4 * self.bit(1)) + dz * (4 - 8 * self.bit(2))
        return (place, self.plane(dx))

    def copy(self, n, src, dst, device):
        return pltpu.make_async_remote_copy(
            src_ref=src,
            dst_ref=dst,
            send_sem=self.ssem.at[n],
            recv_sem=self.rsem.at[n],
            device_id=device,
            device_id_type=pl.DeviceIdType.MESH,
        )

    def core_copy(self):
        return self.copy(0, self.send, self.r1, self.near(0))

    def start_core(self):
        for h in range(2):
            for at, take in self.pieces(h, 1 - self.core):
                self.send[h, at[0], at[1]] = take().astype(BFLOAT)
        self.core_copy().start()

    def x_copy(self):
        return self.copy(1, self.send.at[0], self.r2, (self.i, 1 - self.j))

    def core_to_x(self):
        self.core_copy().wait()
        for n, h in enumerate((1 - self.j, self.j)):
            for at, take in self.pieces(h, self.core):
                arrived = self.r1[h, at[0], at[1]].astype(FLOAT)
                self.send[n, at[0], at[1]] = (take() + arrived).astype(BFLOAT)
            if n == 0:
                self.x_copy().start()

    def x_to_direct(self):
        self.x_copy().wait()
        self.send[1] = (self.send[1].astype(FLOAT) + self.r2[...].astype(FLOAT)).astype(BFLOAT)
        for n, (dx, dy, dz) in enumerate(TURNS[3:0:-1]):
            self.copy(6, self.send.at[1, self.rows(dy, dz), :], self.r3.at[n], self.member(dx, dy, dz)).start()

    def z_copy(self):
        return self.copy(2, self.send.at[1, self.mine, :], self.r5, self.near(3))

    def direct_to_z(self):
        wait_for(self.r3, self.ssem.at[6])
        wait_for(self.r3, self.rsem.at[6])
        total = self.send[1, self.mine, :].astype(FLOAT)
        for n in range(3):
            total += self.r3[n].astype(FLOAT)
        self.send[1, self.mine, :] = total.astype(BFLOAT)
        self.z_copy().start()

    def keep_copy(self):
        return pltpu.make_async_copy(self.fin, self.final.at[self.core, self.mine, :], self.ssem.at[7])

    def z_to_gather(self):
        self.z_copy().wait()
        total = self.send[1, self.mine, :].astype(FLOAT) + self.r5[...].astype(FLOAT)
        self.fin[...] = total.astype(BFLOAT)
        self.keep_copy().start()
        dst = self.final.at[self.core, self.mine, :]
        for dx, dy, dz in TURNS[:0:-1]:
            if dx == 0 or self.everywhere is not None:
                self.copy(3 + dx, self.fin, dst, self.member(dx, dy, dz)).start()

    def core_gather(self):
        if self.everywhere is not None:
            place = self.everywhere.at[:, self.core]
        else:
            place = self.final.at[self.core]
        return self.copy(5, place, place, self.near(0))

    def gather_to_core(self):
        self.keep_copy().wait()
        three = self.final.at[self.core, 0 : 3 * self.part, :]
        wait_for(three, self.ssem.at[3])
        wait_for(three, self.rsem.at[3])
        if self.everywhere is not None:
            four = self.everywhere.at[1 - self.j, self.core]
            wait_for(four, self.ssem.at[4])
            wait_for(four, self.rsem.at[4])
        self.core_gather().start()

    def step(self, n):
        (
            self.start_core,
            self.core_to_x,
            self.x_to_direct,
            self.direct_to_z,
            self.z_to_gather,
            self.gather_to_core,
        )[n]()


def wide_kernel(local_len, *refs):
    (
        lat_hbm, seg_ref, cot_hbm, stem_hbm, extra_hbm,
        wq_hbm, wk_hbm, wv_hbm, wo_hbm, wup_hbm, wdown_hbm, upb_hbm,
    ) = refs[:12]
    vec = refs[12:17]
    out_hbm, tg_hbm, down_hbm, up_hbm, query_hbm, shared_hbm = refs[17:23]
    (
        lat_s, frame_s, stem_s, wqkv_s, wout_s, wup_s, wdown_s, upb_s,
        gstem_s, gqkv_s, gout_s, gup_s, gdown_s, gvec_s,
    ) = refs[23:37]
    work = refs[37:44]
    own_s = refs[44]
    group_bufs = [refs[45 + 6 * n : 51 + 6 * n] for n in range(4)]
    sizes = [bufs[0].shape[1] for bufs in group_bufs]
    tile = work[5].shape[0]
    work = work[:5] + (own_s.at[0:tile, :], own_s.at[tile : 2 * tile, :]) + work[5:]
    (
        lat_send, lat_recv, cot_send, cot_recv, own_sem, out_send, out_recv, tg_send, tg_recv,
        w_local, wx_send, wx_recv, wy_send, wy_recv, wc_send, wc_recv,
    ) = refs[69:85]
    group_sems = [refs[85 + 2 * n : 87 + 2 * n] for n in range(4)]
    i, j = lax.axis_index("gx"), lax.axis_index("gy")
    places = lax.axis_size("gx")
    core = lax.rem(i, 2)
    sibling = (i + 1 - 2 * core, j)
    ybit = lax.rem(i // 2, 2)
    beside = (i + 2 - 4 * ybit, j)
    across = (i, 1 - j)
    tiles = work[0].shape[0] // tile
    width = work[0].shape[1]
    mesh_id = pl.DeviceIdType.MESH

    def remote(src, dst, send, recv, device):
        return pltpu.make_async_remote_copy(
            src_ref=src, dst_ref=dst, send_sem=send, recv_sem=recv, device_id=device, device_id_type=mesh_id
        )

    barrier = pltpu.get_barrier_semaphore()

    @pl.loop(1, places)
    def greet(k):
        pl.semaphore_signal(barrier, inc=1, device_id=(lax.rem(i + k, places), j), device_id_type=mesh_id)

    for dy in range(2):
        for dz in range(2):
            place = i + dy * (2 - 4 * ybit) + dz * (4 - 8 * lax.rem(i // 4, 2))
            pl.semaphore_signal(barrier, inc=1, device_id=(place, 1 - j), device_id_type=mesh_id)
    pl.semaphore_wait(barrier, places + 3)

    def part(ref, t):
        count = ref.shape[1] // tiles
        return pl.ds(pl.multiple_of(t * count, count), count)

    def scatter(src, dst, t, send, recv):
        @pl.loop(1, places)
        def each(k):
            d = lax.rem(i + k, places)
            remote(src.at[d, part(src, t), :], dst.at[i, part(src, t), :], send, recv, (d, j)).start()

    def keep(src, dst, t, sem):
        return pltpu.make_async_copy(src.at[i, part(src, t), :], dst.at[i, part(src, t), :], sem)

    def most(ref, t):
        return ref.at[0 : places - 1, part(ref, t), :]

    half = wq_hbm.shape[1]

    ff_half = upb_hbm.shape[1]
    blocks = ff_half // FFB

    def weight_views(owner, share):
        def rows_of(count):
            if share == "all":
                return 0, count
            if share == "half":
                return pl.multiple_of(core * (count // 2), 16), count // 2
            return pl.multiple_of((core * 2 + ybit) * (count // 4), 16), count // 4

        start, size = rows_of(width)
        r = pl.ds(start, size)
        views = []
        for n, src in enumerate((wq_hbm, wk_hbm, wv_hbm)):
            at = pl.ds(pl.multiple_of(n * width + owner * half, half), half)
            views.append((src.at[r, :], wqkv_s.at[r, at]))
        count = wo_hbm.shape[0]
        start, size = rows_of(count)
        there = pl.ds(pl.multiple_of(owner * count + start, 16), size)
        views.append((wo_hbm.at[pl.ds(start, size), :], wout_s.at[there, :]))
        start, size = rows_of(FFB)
        for block in range(blocks):
            at = pl.ds(pl.multiple_of(owner * ff_half + block * FFB, 128), FFB)
            views.append((wup_hbm.at[r, block * FFB : (block + 1) * FFB], wup_s.at[r, at]))
            here = pl.ds(pl.multiple_of(block * FFB + start, 16), size)
            there = pl.ds(pl.multiple_of(owner * ff_half + block * FFB + start, 16), size)
            views.append((wdown_hbm.at[here, :], wdown_s.at[there, :]))
        return views

    here_views = weight_views(j, "all")
    x_copies = [
        remote(src, dst, wx_send.at[n], wx_recv.at[n], across)
        for n, (src, dst) in enumerate(weight_views(j, "quarter")[:4] + weight_views(j, "half")[4:])
    ]
    y_copies = [
        remote(dst, dst, wy_send.at[n], wy_recv.at[n], beside)
        for n, (_, dst) in enumerate(weight_views(1 - j, "quarter")[:4])
    ]
    c_copies = [
        remote(dst, dst, wc_send.at[n], wc_recv.at[n], sibling)
        for n, (_, dst) in enumerate(weight_views(1 - j, "half"))
    ]
    own_copies = [pltpu.make_async_copy(src, dst, w_local.at[n]) for n, (src, dst) in enumerate(here_views)]
    n_weights = len(x_copies)
    upb_at = pl.ds(pl.multiple_of(j * ff_half, 128), ff_half)
    upb_x = remote(upb_hbm, upb_s.at[:, upb_at], wx_send.at[n_weights], wx_recv.at[n_weights], across)
    upb_own = pltpu.make_async_copy(upb_hbm, upb_s.at[:, upb_at], w_local.at[n_weights])

    for n in range(4):
        x_copies[n].start()

    @pl.loop(0, tiles)
    def send_lat(t):
        keep(lat_hbm, lat_s, t, own_sem.at[t]).start()
        scatter(lat_hbm, lat_s, t, lat_send, lat_recv.at[t])

    stem_rows_in = stem_hbm.shape[0]
    stem_copies = [
        pltpu.make_async_copy(stem_hbm, stem_s.at[0:stem_rows_in, :], w_local.at[n_weights + 1]),
        pltpu.make_async_copy(extra_hbm, stem_s.at[stem_rows_in:, :], w_local.at[n_weights + 2]),
    ]
    for copy in stem_copies:
        copy.start()
    for n in range(4, n_weights):
        x_copies[n].start()
    for copy in own_copies:
        copy.start()
    upb_x.start()
    upb_own.start()

    def send_cot(t):
        keep(cot_hbm, frame_s, t, own_sem.at[tiles + t]).start()
        scatter(cot_hbm, frame_s, t, cot_send, cot_recv.at[t])

    def move(first, last, before, after):
        for n in range(first, last):
            before[n].wait()
            if after is not None:
                after[n].start()

    for t in range(tiles):
        send_cot(t)

    last_tile = tiles - 1
    middle = min(1, last_tile)

    hooks = dict(NO_HOOKS)

    def lat_ready(t):
        keep(lat_hbm, lat_s, t, own_sem.at[t]).wait()
        wait_for(most(lat_s, t), lat_recv.at[t])

        @pl.when(t == 0)
        def _():
            for copy in stem_copies:
                copy.wait()

    def stem_done(t):
        @pl.when(t == last_tile)
        def _():
            move(0, 4, x_copies, y_copies)
            move(0, 4, own_copies, None)

    def attend_done(turn, t):
        @pl.when((turn == 0) & (t == last_tile))
        def _():
            move(0, 4, y_copies, c_copies)
            move(0, 4, c_copies, None)

        @pl.when((turn == 1) & (t == middle))
        def _():
            move(4, 6, x_copies, c_copies)

    def forward_done():
        upb_x.wait()
        upb_own.wait()
        move(4, n_weights, own_copies, None)

    def feed_block(turn):
        first = 4 + 2 * (turn - blocks)
        if turn > blocks:
            move(first, first + 2, x_copies, c_copies)
        if turn >= blocks:
            move(first, first + 2, c_copies, None)

    def cot_ready(t):
        keep(cot_hbm, frame_s, t, own_sem.at[tiles + t]).wait()
        wait_for(most(frame_s, t), cot_recv.at[t])

    def out_ready(t):
        keep(frame_s, out_hbm, t, own_sem.at[2 * tiles + t]).start()
        scatter(frame_s, out_hbm, t, out_send.at[t], out_recv)

    def tg_room(t):
        keep(frame_s, out_hbm, t, own_sem.at[2 * tiles + t]).wait()
        wait_for(most(frame_s, t), out_send.at[t])

    def send_tg(t):
        keep(frame_s, tg_hbm, t, own_sem.at[3 * tiles + t]).start()
        scatter(frame_s, tg_hbm, t, tg_send.at[t], tg_recv)

    def tg_ready(t):
        send_tg(t)

    def grab(ref, r0, nrows, c0, ncols):
        return lambda: ref[pl.ds(r0, nrows), pl.ds(c0, ncols)]

    def mult(value, by):
        return pl.multiple_of(value, by)

    up_half = gup_s.shape[1] // 2
    up_rows = width // 2
    down_rows = gdown_s.shape[0] // 4
    out_rows = gout_s.shape[0] // 4
    stem_rows = gstem_s.shape[0] // 4

    qrows = width // 2

    def down_pieces(h, c):
        return [((slice(None), slice(None)), grab(gdown_s, mult((h * 2 + c) * down_rows, 16), down_rows, 0, width))]

    def up_pieces(h, c):
        found, base = [], 0
        for block in range(up_half // width):
            found.append(
                (
                    (slice(base, base + up_rows), slice(None)),
                    grab(gup_s, mult(c * up_rows, 16), up_rows, mult(h * up_half + block * width, 128), width),
                )
            )
            base += up_rows
        found.append(
            (
                (slice(base, base + out_rows), slice(None)),
                grab(gout_s, mult((h * 2 + c) * out_rows, 16), out_rows, 0, width),
            )
        )
        return found

    def stem_pieces(h, c):
        found = [
            (
                (slice(0, stem_rows), slice(None)),
                grab(gstem_s, mult((h * 2 + c) * stem_rows, 16), stem_rows, 0, width),
            ),
            (
                (slice(stem_rows, stem_rows + 16), slice(None)),
                grab(gvec_s, mult((h * 2 + c) * 16, 16), 16, 0, width),
            ),
        ]
        base, end = stem_rows + 16, sizes[2]
        if end > base:
            found.append(((slice(base, end), slice(None)), lambda: jnp.zeros((end - base, width), FLOAT)))
        return found

    def query_pieces(h, c):
        found = [
            (
                (slice(0, qrows), slice(n * half, (n + 1) * half)),
                grab(gqkv_s, mult(c * qrows, 16), qrows, mult(n * width + h * half, 128), half),
            )
            for n in range(2)
        ]
        for n in range(2):
            found.append(
                (
                    (slice(qrows, qrows + qrows // 2), slice(n * half, (n + 1) * half)),
                    grab(gqkv_s, mult(c * qrows + n * (qrows // 2), 16), qrows // 2, mult(2 * width + h * half, 128), half),
                )
            )
        return found

    where = (i, j)
    down, up, stem, query = [
        Reducer(where, pieces, bufs, final, sems, everywhere)
        for pieces, bufs, final, sems, everywhere in zip(
            (down_pieces, up_pieces, stem_pieces, query_pieces),
            group_bufs,
            (down_hbm, up_hbm, shared_hbm.at[j], query_hbm),
            group_sems,
            (None, None, shared_hbm, None),
        )
    ]

    def feed_done():
        down.start_core()
        up.start_core()

    def attend_back_done(t):
        for at, group, n in EARLY:

            @pl.when(t == min(at, last_tile))
            def _():
                (down, up)[group].step(n)

    hooks.update(
        lat_ready=lat_ready,
        stem_done=stem_done,
        attend_done=attend_done,
        feed_block=feed_block,
        attend_back_done=attend_back_done,
        forward_done=forward_done,
        cot_ready=cot_ready,
        out_ready=out_ready,
        tg_room=tg_room,
        tg_ready=tg_ready,
        feed_done=feed_done,
    )
    block_compute(
        local_len,
        {
            "in": (lat_s, seg_ref, frame_s, stem_s, wqkv_s, wout_s, wup_s, wdown_s, upb_s),
            "vec": vec,
            "own": j,
            "pairs": frame_s.shape[1] // lat_s.shape[1],
            "stage": (frame_s, frame_s),
            "grads": (gstem_s, gqkv_s, gout_s, gup_s, gdown_s, gvec_s),
            "work": work,
        },
        hooks,
    )
    stem.start_core()
    query.start_core()
    groups = (down, up, stem, query)
    for g, n in ORDER:
        groups[g].step(n)
    for group in groups:
        group.core_gather().wait()
    wait_for(lat_hbm.at[0 : places - 1], lat_send)
    wait_for(cot_hbm.at[0 : places - 1], cot_send)
    wait_for(out_hbm.at[0 : places - 1], out_recv)
    wait_for(tg_hbm.at[0 : places - 1], tg_recv)

    @pl.loop(0, tiles)
    def drain(t):
        keep(frame_s, tg_hbm, t, own_sem.at[3 * tiles + t]).wait()
        wait_for(most(frame_s, t), tg_send.at[t])


def reduce_shapes(half, width):
    return [
        pltpu.VMEM((2, half, width), BFLOAT),
        pltpu.VMEM((2, half, width), BFLOAT),
        pltpu.VMEM((half, width), BFLOAT),
        pltpu.VMEM((3, half // 4, width), BFLOAT),
        pltpu.VMEM((half // 4, width), BFLOAT),
        pltpu.VMEM((half // 4, width), BFLOAT),
    ]


def run_wide(local_len, lat, seg, cot, stem, extra, wq, wk, wv, wo, wup, wdown, upb, *vec):
    places, per, width = cot.shape
    rows = places * per
    ff = 2 * wup.shape[1]
    hot_width = stem.shape[0] + extra.shape[0]
    shape = jax.ShapeDtypeStruct
    vm = pl.BlockSpec(memory_space=pltpu.VMEM)
    hbm = pl.BlockSpec(memory_space=pl.ANY)
    stem_used = hot_width // 4 + 16
    sizes = (
        ff // 4,
        (width // 2) * (wup.shape[1] // width) + width // 4,
        -(-stem_used // 64) * 64,
        width // 2 + width // 4,
    )
    tiles = rows // TILE
    n_weights = 4 + 2 * (wup.shape[1] // FFB)
    dma = pltpu.SemaphoreType.DMA
    scratch = [
        pltpu.VMEM(lat.shape, BFLOAT),
        pltpu.VMEM(cot.shape, BFLOAT),
        pltpu.VMEM((hot_width, width), BFLOAT),
        pltpu.VMEM((width, 3 * width), BFLOAT),
        pltpu.VMEM((width, width), BFLOAT),
        pltpu.VMEM((width, ff), BFLOAT),
        pltpu.VMEM((ff, width), BFLOAT),
        pltpu.VMEM((1, ff), FLOAT),
        pltpu.VMEM((hot_width, width), FLOAT),
        pltpu.VMEM((width, 3 * width), FLOAT),
        pltpu.VMEM((width, width), FLOAT),
        pltpu.VMEM((width, ff), FLOAT),
        pltpu.VMEM((ff, width), FLOAT),
        pltpu.VMEM((ff // width * 16, width), FLOAT),
    ]
    scratch += [item for n, item in enumerate(work_shapes(rows, width, TILE)) if n not in (5, 6)]
    scratch += [pltpu.VMEM((2 * TILE, width), FLOAT)]
    for size in sizes:
        scratch += reduce_shapes(size, width)
    scratch += [
        dma,
        dma((tiles,)),
        dma,
        dma((tiles,)),
        dma((4 * tiles,)),
        dma((tiles,)),
        dma,
        dma((tiles,)),
        dma,
        dma((n_weights + 3,)),
        dma((n_weights + 1,)),
        dma((n_weights + 1,)),
        dma((n_weights,)),
        dma((n_weights,)),
        dma((n_weights,)),
        dma((n_weights,)),
    ]
    scratch += [dma((8,))] * 8
    return pl.pallas_call(
        functools.partial(wide_kernel, local_len),
        out_shape=(shape(cot.shape, BFLOAT), shape(cot.shape, BFLOAT))
        + tuple(shape((2, sizes[n], width), BFLOAT) for n in (0, 1, 3))
        + (shape((2, 2, sizes[2], width), BFLOAT),),
        in_specs=[hbm, vm] + [hbm] * 10 + [vm] * 5,
        out_specs=[hbm] * 6,
        scratch_shapes=scratch,
        compiler_params=pltpu.CompilerParams(
            vmem_limit_bytes=VMEM_LIMIT, collective_id=0, has_side_effects=True
        ),
    )(lat, seg, cot, stem, extra, wq, wk, wv, wo, wup, wdown, upb, *vec)


def per_device(
    latents,
    actions,
    segment_ids,
    cotangent,
    stem_weight,
    action_table,
    first_gain,
    first_bias,
    query_weight,
    key_weight,
    value_weight,
    out_weight,
    second_gain,
    second_bias,
    up_weight,
    up_bias,
    down_weight,
    down_bias,
):
    half_seqs, local_len, groups = latents.shape
    width = stem_weight.shape[1]
    places = lax.axis_size("gx")
    length = places * local_len
    seqs = half_seqs // places
    rows = seqs * length
    actions_n = action_table.shape[0]

    lat = jnp.concatenate([latents, actions[..., None]], axis=-1).astype(BFLOAT)
    lat = lat.reshape(places, seqs, local_len, groups + 1)
    cot = cotangent.reshape(places, seqs * local_len, width)
    first_seq = (lax.axis_index("gy") * places + lax.axis_index("gx")) * seqs
    seg = lax.dynamic_slice_in_dim(segment_ids, first_seq, seqs, 0)
    seg = jnp.tile(seg.astype(FLOAT), (1, PACK // length))
    extra = jnp.pad(action_table, ((0, HOT_PAD - actions_n), (0, 0)))
    vec = [item[None] for item in (first_gain, first_bias, second_gain, second_bias, down_bias)]
    if rows % TILE == 0 and rows <= MAX_ROWS and places == 16:
        lat = jnp.pad(latents, ((0, 0), (0, 0), (0, 64 - groups)))
        lat += jnp.pad(actions[..., None], ((0, 0), (0, 0), (groups, 63 - groups)))
        lat = lat.astype(BFLOAT).reshape(places, seqs * local_len // 2, 128)
        out, tg, gdown, up, query, shared = run_wide(
            local_len, lat, seg, cot, stem_weight, extra, query_weight, key_weight, value_weight,
            out_weight, up_weight, down_weight, up_bias[None], *vec,
        )
        out = out.reshape(half_seqs, local_len, width)
        tg = tg.reshape(half_seqs, local_len, width)
        half = width // 2
        cols = query_weight.shape[1]
        blocks = up_weight.shape[1] // width
        gdown = gdown.astype(FLOAT).reshape(down_weight.shape)
        gup = jnp.concatenate([up[:, b * half : (b + 1) * half] for b in range(blocks)], axis=2)
        gup = gup.astype(FLOAT).reshape(up_weight.shape)
        gout = up[:, blocks * half :].astype(FLOAT).reshape(out_weight.shape)
        query = query.astype(FLOAT)
        gq = query[:, :half, :cols].reshape(width, cols)
        gk = query[:, :half, cols:].reshape(width, cols)
        part = query[:, half:]
        gv = jnp.concatenate([part[:, :, :cols], part[:, :, cols:]], axis=1).reshape(width, cols)
        stem_rows = (stem_weight.shape[0] + HOT_PAD) // 4
        gstem = shared[:, :, :stem_rows].astype(FLOAT).reshape(4 * stem_rows, width)
        first = shared[0, 0, stem_rows : stem_rows + 16].astype(FLOAT)
        upb_grad = lax.dynamic_index_in_dim(shared[:, :, stem_rows], lax.axis_index("gy"), 0, False)
        upb_grad = upb_grad.astype(FLOAT).reshape(up_bias.shape)
        return (
            out,
            tg,
            gstem[: groups * 32],
            gstem[groups * 32 : groups * 32 + actions_n],
            first[1],
            first[2],
            gq,
            gk,
            gv,
            gout,
            first[3],
            first[4],
            gup,
            upb_grad,
            gdown,
            first[5],
        )
    lat = lat.reshape(places, seqs * local_len, groups + 1)
    lat = jnp.pad(lat, ((0, 0), (0, 0), (0, 128 - groups - 1)))
    lat = lax.all_to_all(lat, "gx", split_axis=0, concat_axis=0, tiled=True)
    cot = lax.all_to_all(cot, "gx", split_axis=0, concat_axis=0, tiled=True)
    gather = functools.partial(lax.all_gather, axis_name="gy", tiled=True)
    wqkv = jnp.concatenate(
        [gather(item, axis=1) for item in (query_weight, key_weight, value_weight)], axis=1
    )
    wout = gather(out_weight, axis=0)
    wup = gather(up_weight, axis=1)
    wdown = gather(down_weight, axis=0)
    upb = gather(up_bias, axis=0)[None]
    stem = jnp.concatenate([stem_weight, extra], axis=0)
    out, tg, gstem, gqkv, gout, gup, gdown, gvec = run_local(
        local_len, lat, seg, cot, stem, wqkv, wout, wup, wdown, upb, *vec
    )
    out = lax.all_to_all(out, "gx", split_axis=0, concat_axis=0, tiled=True)
    tg = lax.all_to_all(tg, "gx", split_axis=0, concat_axis=0, tiled=True)
    out = out.reshape(half_seqs, local_len, width)
    tg = tg.reshape(half_seqs, local_len, width)
    both = ("gx", "gy")
    gstem, gvec = lax.psum((gstem, gvec), both)
    upb_grad = gvec[::16].reshape(-1)
    upb_grad = lax.dynamic_slice_in_dim(upb_grad, lax.axis_index("gy") * up_bias.shape[0], up_bias.shape[0])

    def shard(value, dim):
        return lax.psum(lax.psum_scatter(value, "gy", scatter_dimension=dim, tiled=True), "gx")

    gq = shard(gqkv[:, :width], 1)
    gk = shard(gqkv[:, width : 2 * width], 1)
    gv = shard(gqkv[:, 2 * width :], 1)
    return (
        out,
        tg,
        gstem[: groups * 32],
        gstem[groups * 32 : groups * 32 + actions_n],
        gvec[1],
        gvec[2],
        gq,
        gk,
        gv,
        shard(gout, 0),
        gvec[3],
        gvec[4],
        shard(gup, 1),
        upb_grad,
        shard(gdown, 0),
        gvec[5],
    )


def solution(mesh):
    return jax.shard_map(
        per_device,
        mesh=mesh,
        in_specs=(
            P("gy", "gx", None),
            P("gy", "gx"),
            P(),
            P("gy", "gx", None),
            P(),
            P(),
            P(),
            P(),
            P(None, "gy"),
            P(None, "gy"),
            P(None, "gy"),
            P("gy", None),
            P(),
            P(),
            P(None, "gy"),
            P("gy"),
            P("gy", None),
            P(),
        ),
        out_specs=(
            P("gy", "gx", None),
            P("gy", "gx", None),
            P(),
            P(),
            P(),
            P(),
            P(None, "gy"),
            P(None, "gy"),
            P(None, "gy"),
            P("gy", None),
            P(),
            P(),
            P(None, "gy"),
            P("gy"),
            P("gy", None),
            P(),
        ),
        check_vma=False,
    )
```
